32 devices in a mesh: grp: 2 (over y), tile: 16 (over z, x, core).
Axes of the slice: x: 2, y: 2, z: 4, core: 2. Of those that a mesh axis runs over, the one named last changes fastest.
Arguments:
- fields: bfloat16 [6, 128, 128, 256], P('grp', 'tile'), parts along dimension 0, may hold values from -6 to 6
- seam_tile: int32 [3, 16, 2], P(None, 'tile'), may hold values from 0 to 47, as said below
- seam_code: int32 [3, 16, 2], P(None, 'tile'), may hold values from 0 to 3
- encoder_weight: bfloat16 [3, 3, 256, 256], replicated, may hold values from -0.125 to 0.125
- encoder_bias: float32 [256], replicated, may hold values from -3 to 3
- middle_weight: bfloat16 [3, 3, 256, 256], replicated, may hold values from -0.125 to 0.125
- middle_bias: float32 [256], replicated, may hold values from -3 to 3
- upconv_weight: bfloat16 [2, 2, 256, 256], replicated, may hold values from -0.375 to 0.375
- upconv_bias: float32 [256], replicated, may hold values from -3 to 3
- decoder_weight: bfloat16 [3, 3, 512, 256], replicated, may hold values from -0.09375 to 0.09375
- decoder_offset_bias: float32 [256], replicated, may hold values from -3 to 3
Outputs:
- decoded: bfloat16 [6, 128, 128, 256], P('grp', 'tile'), parts along dimension 0
The draws below stay inside these ranges and needn't reach their ends.
There are 2 independent parts, one for each index of `grp`. The reference program is written for one: setup_inputs(seed, part) draws one part's arguments, and reference() takes and returns one part's arrays. A program takes and returns all parts, laid end to end along the dimension named above; an argument that names none is the same for every part. Nothing has to cross between parts.
Inputs may be any that keep to these rules, and one draw needn't show every extreme that they name: `seam_tile`: for each side, the 12 faces (cycle, face) name 12 different partner faces; all 4 tiles of one face side share the partner face and the code, and strip s names the tile of strip s of the partner face, or of strip 4 - 1 - s where the code is 2 or more.
All inputs are finite; a program needn't handle non-finite values.
Results may differ from the reference program's by a relative error of at most 0.0048.
Values may be sent and summed in bfloat16 or wider, within the bound.
No kernel may reach another device: no remote copies, remote signals or barrier semaphores. Data moves between devices by JAX's collectives and lax.ppermute only.
A program may use at most 128 MiB of HBM per device.

```python
import jax
import jax.numpy as jnp

C = 256
COLS = 128
TILES = 16
STRIPS = 4
ROWS = 128


def seam_layout(key):
    base = jax.random.fold_in(key, 7)
    key_left, key_right, key_code = jax.random.split(base, 3)
    order_left = jax.random.permutation(key_left, 12)
    order_right = jax.random.permutation(key_right, 12)
    partner_face = jnp.stack([order_left, order_right], axis=-1).reshape(3, 4, 1, 2).astype(jnp.int32)
    code_order = jax.random.permutation(key_code, 24)
    face_code = (code_order % 4).reshape(3, 4, 1, 2).astype(jnp.int32)
    strip_index = jnp.arange(STRIPS, dtype=jnp.int32).reshape(1, 1, STRIPS, 1)
    partner_strip = jnp.where(face_code >= 2, STRIPS - 1 - strip_index, strip_index)
    partner_cycle = partner_face // 4
    partner_in_cycle = partner_face % 4
    partner_place = (partner_in_cycle * STRIPS + partner_strip - STRIPS // 2) % TILES
    adjacent_tile = partner_cycle * TILES + partner_place
    seam_codes = jnp.broadcast_to(face_code, (3, 4, STRIPS, 2))
    adjacent_tile = jnp.roll(adjacent_tile.reshape(3, TILES, 2), -(STRIPS // 2), axis=1)
    seam_codes = jnp.roll(seam_codes.reshape(3, TILES, 2), -(STRIPS // 2), axis=1)
    return (adjacent_tile.astype(jnp.int32), seam_codes.astype(jnp.int32))


def draw_seam_tile(key, part):
    return seam_layout(key)[0]


def draw_seam_code(key, part):
    return seam_layout(key)[1]


def level_of(rng, dims, shards, smallest, high):
    factor_of = 1.0
    for axis_at, blocks in shards:
        steps = jax.random.uniform(jax.random.fold_in(jax.random.fold_in(rng, 6), axis_at), (blocks,), jnp.float32, smallest / len(shards), high / len(shards))
        factor_of = factor_of * jnp.repeat(jnp.exp(steps), dims[axis_at] // blocks).reshape((-1,) + (1,) * (len(dims) - 1 - axis_at))
    return factor_of


def bell_draw(rng, shape, spread, limit, shards=(), kind=jnp.bfloat16):
    entries = jax.random.normal(rng, shape, jnp.float32) * spread
    if len(shards) > 0:
        entries = level_of(rng, shape, shards, -0.22, 0.18) * entries
    return jnp.clip(entries, min=-limit, max=limit).astype(kind)


def setup_inputs(seed: int = 0, part: int = 0) -> dict:
    seeds = jax.random.split(jax.random.key(seed), 12)
    part_splits = jax.random.split(jax.random.fold_in(seeds[11], part), 12)
    fields = bell_draw(part_splits[0], (3, ROWS, COLS, C), 1.0, 6.0, ((1, 16),))
    seam_tile = draw_seam_tile(jax.random.fold_in(seeds[11], 71), part)
    seam_code = draw_seam_code(jax.random.fold_in(seeds[11], 71), part)
    encoder_weight = bell_draw(seeds[3], (3, 3, C, C), (9 * C) ** -0.5, 0.125)
    encoder_bias = bell_draw(seeds[4], (C,), 0.5, 3.0, (), jnp.float32)
    middle_weight = bell_draw(seeds[5], (3, 3, C, C), (9 * C) ** -0.5, 0.125)
    middle_bias = bell_draw(seeds[6], (C,), 0.5, 3.0, (), jnp.float32)
    upconv_weight = bell_draw(seeds[7], (2, 2, C, C), C ** -0.5, 0.375)
    upconv_bias = bell_draw(seeds[8], (C,), 0.5, 3.0, (), jnp.float32)
    decoder_weight = bell_draw(seeds[9], (3, 3, 2 * C, C), (18 * C) ** -0.5, 0.09375)
    decoder_offset_bias = bell_draw(seeds[10], (C,), 0.5, 3.0, (), jnp.float32)
    return dict(fields=fields, seam_tile=seam_tile, seam_code=seam_code, encoder_weight=encoder_weight, encoder_bias=encoder_bias, middle_weight=middle_weight, middle_bias=middle_bias, upconv_weight=upconv_weight, upconv_bias=upconv_bias, decoder_weight=decoder_weight, decoder_offset_bias=decoder_offset_bias)


def gelu_tanh(values):
    return jax.nn.gelu(values, approximate=True)


def blank_edge_rows(extended, top_face, bottom_face):
    upper_row = extended[..., :1, :, :]
    lower_row = extended[..., -1:, :, :]
    upper_row = jnp.where(top_face, jnp.zeros_like(upper_row), upper_row)
    lower_row = jnp.where(bottom_face, jnp.zeros_like(lower_row), lower_row)
    return jnp.concatenate([upper_row, extended[..., 1:-1, :, :], lower_row], axis=-3)


def boundary_columns(extended):
    return jnp.stack([extended[..., :, 0, :], extended[..., :, -1, :]], axis=-3)


def pick_partner(flattened, partners, seam_codes):
    chosen = flattened[partners]
    column_bit = (seam_codes % 2)[..., None, None]
    single = jnp.where(column_bit == 0, chosen[..., 0, :, :], chosen[..., 1, :, :])
    mirror_flag = (seam_codes // 2)[..., None, None]
    return jnp.where(mirror_flag == 1, single[..., ::-1, :], single)


def attach_columns(extended, picked):
    left_col = picked[..., 0, :, :][..., :, None, :]
    right_col = picked[..., 1, :, :][..., :, None, :]
    return jnp.concatenate([left_col, extended, right_col], axis=-2)


def convolve(padded, weight, bias):
    leading = padded.shape[:-3]
    rows_out = padded.shape[-3] - 2
    cols_out = padded.shape[-2] - 2
    chans_in = padded.shape[-1]
    chans_out = weight.shape[-1]
    accumulated = jnp.zeros(leading + (rows_out, cols_out, chans_out), jnp.float32)
    for row_tap in range(3):
        for col_tap in range(3):
            window = padded[..., row_tap:row_tap + rows_out, col_tap:col_tap + cols_out, :]
            product = jnp.dot(window.reshape(-1, chans_in), weight[row_tap, col_tap], preferred_element_type=jnp.float32)
            accumulated = accumulated + product.reshape(accumulated.shape)
    return accumulated + bias


def coarsen_grid(sphere_map):
    leading = sphere_map.shape[:-3]
    rows_in, cols_in, chans_in = sphere_map.shape[-3:]
    values = sphere_map.astype(jnp.float32).reshape(leading + (rows_in // 2, 2, cols_in // 2, 2, chans_in))
    return jnp.mean(values, axis=(-4, -2)).astype(jnp.bfloat16)


def upsample(coarse, weight, bias):
    leading = coarse.shape[:-3]
    rows_in, cols_in, chans_in = coarse.shape[-3:]
    chans_out = weight.shape[-1]
    flattened = coarse.reshape(-1, chans_in)
    phases = []
    for row_phase in range(2):
        phase_row = []
        for col_phase in range(2):
            product = jnp.dot(flattened, weight[row_phase, col_phase], preferred_element_type=jnp.float32)
            phase_row.append(product.reshape(leading + (rows_in, cols_in, chans_out)))
        phases.append(jnp.stack(phase_row, axis=-2).reshape(leading + (rows_in, 2 * cols_in, chans_out)))
    full = jnp.stack(phases, axis=-3).reshape(leading + (2 * rows_in, 2 * cols_in, chans_out))
    return (full + bias).astype(jnp.bfloat16)


def pad_field(sphere_map, partners, seam_codes):
    rows_in = sphere_map.shape[1] // TILES
    tiles = sphere_map.reshape(3, TILES, rows_in, sphere_map.shape[2], sphere_map.shape[3])
    upper_row = jnp.roll(tiles[:, :, -1:], 1, axis=1)
    lower_row = jnp.roll(tiles[:, :, :1], -1, axis=1)
    extended = jnp.concatenate([upper_row, tiles, lower_row], axis=2)
    strip_index = ((jnp.arange(TILES, dtype=jnp.int32) + STRIPS // 2) % STRIPS).reshape(1, TILES, 1, 1, 1)
    extended = blank_edge_rows(extended, strip_index == 0, strip_index == STRIPS - 1)
    edges = boundary_columns(extended)
    flattened = edges.reshape((3 * TILES,) + edges.shape[2:])
    return attach_columns(extended, pick_partner(flattened, partners, seam_codes))


def reference(fields, seam_tile, seam_code, encoder_weight, encoder_bias, middle_weight, middle_bias, upconv_weight, upconv_bias, decoder_weight, decoder_offset_bias):
    padded = pad_field(fields, seam_tile, seam_code)
    shortcut_map = gelu_tanh(convolve(padded, encoder_weight, encoder_bias)).astype(jnp.bfloat16)
    shortcut_map = shortcut_map.reshape(3, ROWS, COLS, C)
    averaged_map = coarsen_grid(shortcut_map)
    padded = pad_field(averaged_map, seam_tile, seam_code)
    coarse = gelu_tanh(convolve(padded, middle_weight, middle_bias)).astype(jnp.bfloat16)
    coarse = coarse.reshape(3, ROWS // 2, COLS // 2, C)
    upsampled = upsample(coarse, upconv_weight, upconv_bias)
    joined = jnp.concatenate([upsampled, shortcut_map], axis=-1)
    padded = pad_field(joined, seam_tile, seam_code)
    decoded = convolve(padded, decoder_weight, decoder_offset_bias).astype(jnp.bfloat16)
    return decoded.reshape(3, ROWS, COLS, C)
```

```python
import functools

import jax
import jax.numpy as jnp
from jax import lax
from jax.experimental import pallas as pl
from jax.experimental.pallas import tpu as pltpu
from jax.sharding import PartitionSpec as P

F32 = jnp.float32
BF16 = jnp.bfloat16
FACES = 4
MIB = 1 << 20


def dot(a, b):
    return jnp.dot(a, b, preferred_element_type=F32)


def gelu(x):
    return 0.5 * x * (1.0 + jnp.tanh(0.7978845608 * (x + 0.044715 * x * x * x)))


def rows_iota(n):
    return lax.broadcasted_iota(jnp.int32, (n, 1), 0)


class Layout:
    def __init__(self, tiles, height, depth, base, payload):
        self.tiles = tiles
        self.strips = tiles // FACES
        self.height = height
        self.depth = depth
        self.base = base
        self.payload = payload
        self.joint = self.strips == 4
        self.stride = height + (depth if self.joint else 2 * depth)

    def source(self, strip, flip, face, column, row):
        height, last = self.height, self.strips - 1
        strip = jnp.where(flip == 1, last - strip, strip)
        row = jnp.where(flip == 1, height - 1 - row, row)
        upper = jnp.where(strip >= self.strips // 2, 1, 0)
        odd = lax.rem(strip, 2)
        above = row < 0
        below = row >= height
        away = jnp.where(above, -row, row - (height - 1))
        near = (above & (odd == 1)) | (below & (odd == 0))
        missing = (above & (strip == 0)) | (below & (strip == last))
        own = (face * 2 + upper) * self.payload
        start = self.base + column * self.stride
        inside = own + start + row
        beside = own + start + height + away - 1
        if self.joint:
            across = (face * 2 + 1 - upper) * self.payload + start
            far = across + jnp.where(above, height - away, away - 1)
        else:
            far = beside + self.depth
        place = jnp.where(above | below, jnp.where(near, beside, far), inside)
        return jnp.where(missing, -1, place)


def strip_of(tiles):
    strips = tiles // FACES
    return lax.rem(lax.axis_index("tile") + strips // 2, strips)


def seam_of(tile_ref, code_ref, tiles, cycle, side):
    strips = tiles // FACES
    partner = tile_ref[cycle, 0, side]
    code = code_ref[cycle, 0, side]
    other = lax.div(partner, tiles)
    place = partner - other * tiles + strips // 2
    face = lax.rem(lax.div(place, strips), FACES)
    return other, face, lax.rem(code, 2), lax.div(code, 2)


def pick(targets, table):
    wanted = jnp.concatenate(targets, axis=0)
    shape = (wanted.shape[0], table.shape[0])
    lanes = lax.broadcasted_iota(jnp.int32, shape, 1)
    chooser = jnp.where(lanes == wanted, 1.0, 0.0).astype(BF16)
    return dot(chooser, table).astype(BF16)


def shifted_sum(taps, cols):
    left, middle, right = taps
    n = middle.shape[0]
    place = lax.broadcasted_iota(jnp.int32, middle.shape, 0) & (cols - 1)
    left = jnp.where(place == 0, 0.0, pltpu.roll(left, 1, 0))
    right = jnp.where(place == cols - 1, 0.0, pltpu.roll(right, n - 1, 0))
    return middle + left + right


def stack_taps(stacked, row_of, rows):
    depth = stacked.shape[-1] // 3
    for row in range(-1, rows + 1):
        value = row_of(row)
        for tap in range(3):
            at = row + 1 - tap
            if 0 <= at < rows:
                stacked[at, :, tap * depth : (tap + 1) * depth] = value


def column_taps(lhs, weight_ref):
    depth = weight_ref.shape[2]
    return [
        dot(lhs, weight_ref[:, tap].reshape(3 * depth, weight_ref.shape[3]))
        for tap in range(3)
    ]


def halo_rows(rows_ref, near, odd, height):
    zero = jnp.zeros_like(near)
    upper = jnp.where(odd == 1, near, zero)
    lower = jnp.where(odd == 1, zero, near)

    def row_of(row):
        if row < 0:
            return upper
        if row >= height:
            return lower
        return rows_ref[0, row]

    return row_of


def column_sum(parts, cycle, height):
    at = cycle * 16
    return sum(parts[tap][at + tap : at + tap + height] for tap in range(3))


def pack_fields(layout, left_ref, right_ref, near_ref, far_ref, tile_ref, code_ref, out_ref, scratch):
    height = layout.height
    cols = near_ref.shape[1]
    cycles = near_ref.shape[0]
    block = left_ref.shape[2]
    scratch[...] = jnp.zeros_like(scratch)
    lanes = lax.broadcasted_iota(jnp.int32, (1, scratch.shape[1]), 1)
    noted = jnp.zeros((1, scratch.shape[1]), F32)
    for cycle in range(cycles):
        for side in range(2):
            column = cycle * 2 + side
            start = column * layout.stride
            ref, at = ((left_ref, 0), (right_ref, block - 1))[side]
            for row in range(height):
                scratch[start + row : start + row + 1] = ref[cycle, row].astype(F32)[at : at + 1]
            halos = [near_ref] if layout.joint else [near_ref, far_ref]
            for k, halo in enumerate(halos):
                first = 0 if side == 0 else cols - 16
                value = halo[cycle, first : first + 16].astype(F32)
                pos = 0 if side == 0 else 15
                scratch[start + height + k : start + height + k + 1] = value[pos : pos + 1]
            other, face, side_bit, flip = seam_of(tile_ref, code_ref, layout.tiles, cycle, side)
            number = (other * FACES + face) * 4 + flip * 2 + side_bit
            noted = jnp.where(lanes == column, number.astype(F32), noted)
    table = 2 * cycles * layout.stride
    scratch[table : table + 1] = noted
    packed = scratch[...].astype(BF16)
    for member in range(out_ref.shape[0]):
        out_ref[member] = packed


def encode(tiles, x_ref, near_ref, w_ref, b_ref, skip_ref, pre_row_ref, pre_col_ref, stacked):
    height, cols = x_ref.shape[1:3]
    odd = lax.rem(strip_of(tiles), 2)
    stack_taps(stacked, halo_rows(x_ref, near_ref[0], odd, height), height)
    chunk = 4
    for first in range(0, height, chunk):
        lhs = stacked[first : first + chunk].reshape(chunk * cols, stacked.shape[2])
        total = shifted_sum(column_taps(lhs, w_ref), cols) + b_ref[...]
        skip_ref[0, first : first + chunk] = gelu(total).astype(BF16).reshape(chunk, cols, -1)
        for row in range(chunk):
            at = row * cols
            pre_col_ref[0, 0, first + row : first + row + 1] = total[at : at + 1]
            pre_col_ref[0, 1, first + row : first + row + 1] = total[at + cols - 1 : at + cols]
        if first == 0:
            @pl.when(odd == 0)
            def _():
                pre_row_ref[0] = total[:cols]
        if first + chunk == height:
            @pl.when(odd == 1)
            def _():
                pre_row_ref[0] = total[(chunk - 1) * cols :]


def mend(layout, recv_ref, far_ref, w_ref, b_ref, skip_ref, pre_row_ref, pre_col_ref, tile_ref, code_ref,
         out_ref, pooled_ref, near_out, far_out):
    tiles, height = layout.tiles, layout.height
    cycles, _, cols, chans = skip_ref.shape
    strip = strip_of(tiles)
    odd = lax.rem(strip, 2)
    ends = (strip == 0) | (strip == layout.strips - 1)
    row_iota = rows_iota(16) - 1
    targets = []
    for side in range(2):
        for cycle in range(cycles):
            other, face, side_bit, flip = seam_of(tile_ref, code_ref, tiles, cycle, side)
            place = layout.source(strip, flip, face, other * 2 + side_bit, row_iota)
            targets.append(jnp.where(row_iota <= height, place, -1))
    pads = pick(targets, recv_ref[...])
    half = pads.shape[0] // 2
    seams = [
        [dot(pads[side * half : (side + 1) * half], w_ref[tap, 2 * side]) for tap in range(3)]
        for side in range(2)
    ]
    far_at = jnp.where(odd == 1, height - 1, 0)
    far_tap = jnp.where(odd == 1, 2, 0)
    far = far_ref[...].reshape(cycles * cols, chans)
    far = jnp.where(ends, jnp.zeros_like(far), far)
    far_sum = shifted_sum([dot(far, w_ref[far_tap, tap]) for tap in range(3)], cols)
    iota8 = lax.broadcasted_iota(jnp.int32, (height, chans), 0)
    iota16 = lax.broadcasted_iota(jnp.int32, (16, chans), 0)
    for cycle in range(cycles):
        extra = far_sum[cycle * cols : (cycle + 1) * cols]
        out_ref[cycle] = skip_ref[cycle]
        out_ref[cycle, far_at] = gelu(pre_row_ref[cycle] + extra).astype(BF16)
        for side in range(2):
            total = pre_col_ref[cycle, side] + column_sum(seams[side], cycle, height)
            corner = extra[:1] if side == 0 else extra[cols - 1 :]
            total = gelu(total + jnp.where(iota8 == far_at, corner, 0.0))
            first, at = (0, 0) if side == 0 else (cols - 16, 15)
            for row in range(height):
                block = out_ref[cycle, row, first : first + 16].astype(F32)
                block = jnp.where(iota16 == at, total[row : row + 1], block)
                out_ref[cycle, row, first : first + 16] = block.astype(BF16)
    fine = lax.broadcasted_iota(jnp.int32, (cols // 2, 2 * cols), 1) & (cols - 1)
    coarse = lax.broadcasted_iota(jnp.int32, (cols // 2, 2 * cols), 0)
    mean = jnp.where(lax.shift_right_logical(fine, 1) == coarse, 0.25, 0.0).astype(BF16)
    for cycle in range(cycles):
        for row in range(height // 2):
            pair = out_ref[cycle, 2 * row : 2 * row + 2].reshape(2 * cols, chans)
            pooled_ref[cycle, row] = dot(mean, pair).astype(BF16)
    low = height // 2 - 1
    for cycle in range(cycles):
        for ref, at_top in ((near_out, odd == 1), (far_out, odd == 0)):
            ref[cycle, :cols] = out_ref[cycle, jnp.where(at_top, 0, height - 1)]
            ref[cycle, cols : cols + cols // 2] = pooled_ref[cycle, jnp.where(at_top, 0, low)]
            ref[cycle, cols + cols // 2 :] = pooled_ref[cycle, jnp.where(at_top, 1, low - 1)]


def pack_skip(coarse, fine, left_ref, right_ref, pooled_ref, near_ref, far_ref, out_ref, scratch):
    cycles = near_ref.shape[0]
    cols = near_ref.shape[1] // 2
    half = cols // 2
    scratch[...] = jnp.zeros_like(scratch)
    halos = [near_ref] if coarse.joint else [near_ref, far_ref]

    def block(ref, at):
        first = at // 16 * 16
        return ref[first : first + 16].astype(F32)[at - first : at - first + 1]

    for cycle in range(cycles):
        for side in range(2):
            for depth in range(2):
                at = depth if side == 0 else half - 1 - depth
                start = coarse.base + ((cycle * 2 + side) * 2 + depth) * coarse.stride
                for row in range(coarse.height):
                    scratch[start + row : start + row + 1] = block(pooled_ref.at[cycle, row], at)
                for k, halo in enumerate(halos):
                    for away in range(2):
                        put = start + coarse.height + 2 * k + away
                        scratch[put : put + 1] = block(halo.at[cycle], cols + away * half + at)
            start = fine.base + (cycle * 2 + side) * fine.stride
            ref, at = (left_ref, 0) if side == 0 else (right_ref, 15)
            for row in range(fine.height):
                scratch[start + row : start + row + 1] = block(ref.at[cycle, row], at)
            for k, halo in enumerate(halos):
                put = start + fine.height + k
                scratch[put : put + 1] = block(halo.at[cycle], 0 if side == 0 else cols - 1)
    packed = scratch[...].astype(BF16)
    for member in range(out_ref.shape[0]):
        out_ref[member] = packed


def decode_skip(tiles, x_ref, near_ref, w_ref, out_ref, stacked):
    height, cols = x_ref.shape[1:3]
    odd = lax.rem(strip_of(tiles), 2)
    near = near_ref[0, :cols]
    stack_taps(stacked, halo_rows(x_ref, near, odd, height), height)
    chunk = 4
    for first in range(0, height, chunk):
        lhs = stacked[first : first + chunk].reshape(chunk * cols, stacked.shape[2])
        total = shifted_sum(column_taps(lhs, w_ref), cols)
        out_ref[0, first : first + chunk] = total.reshape(chunk, cols, -1)


def decode(coarse_at, fine_at, tab_ref, tile_ref, code_ref, recv_ref, pre_ref, pooled_ref, near_ref, far_ref,
           wm_ref, bm_ref, u_ref, bu_ref, wd_ref, bd_ref, out_ref,
           pooled_pads, fine_sums, stacked, upper, joined):
    tiles, strips = coarse_at.tiles, coarse_at.strips
    height, cols, chans = out_ref.shape[1:]
    low, half = height // 2, cols // 2
    cycle_now = pl.program_id(0)
    cycles = 3
    strip = strip_of(tiles)
    odd = lax.rem(strip, 2)
    first_strip, last_strip = strip == 0, strip == strips - 1
    ends = first_strip | last_strip

    @pl.when(cycle_now == 0)
    def _():
        rows8 = rows_iota(8) - 2
        rows16 = rows_iota(16) - 1
        aligned, taps, skips, sides, flips, strips_at = [], [[], [], []], [], [], [], []
        for side in range(2):
            for cycle in range(cycles):
                other, face, side_bit, flip = seam_of(tile_ref, code_ref, tiles, cycle, side)
                column = other * 2 + side_bit
                aligned.append(coarse_at.source(strip, flip, face, column * 2, rows8))
                place = fine_at.source(strip, flip, face, column, rows16)
                skips.append(jnp.where(rows16 <= height, place, -1))
                there = jnp.where(flip == 1, strips - 1 - strip, strip)
                number = tab_ref[face * 2, column]
                beyond = lax.div(number, 4)
                code = lax.rem(number, 4)
                other2, face2 = lax.div(beyond, FACES), lax.rem(beyond, FACES)
                column2 = other2 * 2 + lax.rem(code, 2)
                pad = coarse_at.source(there, lax.div(code, 2), face2, column2 * 2, rows8)
                edge = coarse_at.source(there, 0, face, column * 2, rows8)
                inner = coarse_at.source(there, 0, face, column * 2 + 1, rows8)
                taps[0].append(jnp.where(side_bit == 0, pad, inner))
                taps[1].append(edge)
                taps[2].append(jnp.where(side_bit == 0, inner, pad))
                sides.append(side_bit)
                flips.append(flip)
                strips_at.append(there)
        got = pick(aligned + taps[0] + taps[1] + taps[2] + skips, recv_ref[...])
        n = 8 * 2 * cycles
        own = got[:n]
        for side in range(2):
            part = own[side * n // 2 : (side + 1) * n // 2]
            sums = [dot(part, wm_ref[tap, 2 * side]) for tap in range(3)]
            for cycle in range(cycles):
                at = cycle * 8
                total = sum(sums[tap][at + tap : at + tap + 6] for tap in range(3))
                pooled_pads[cycle, side, 0:6] = total
        there = got[n : 4 * n]
        rows = [
            sum(dot(there[tap * n : (tap + 1) * n], wm_ref[row, tap]) for tap in range(3))
            for row in range(3)
        ]
        total = pltpu.roll(rows[0], 1, 0) + rows[1] + pltpu.roll(rows[2], n - 1, 0)
        at8 = lax.broadcasted_iota(jnp.int32, (8, chans), 0) - 2
        keep = jnp.concatenate(
            [
                jnp.where(((at8 < 0) & (s == 0)) | ((at8 >= low) & (s == strips - 1)), 0.0, 1.0)
                for s in strips_at
            ],
            axis=0,
        )
        right = jnp.concatenate([jnp.where(at8 > -99, b, 0) for b in sides], axis=0) == 1
        column = (gelu(total + bm_ref[...]) * keep).astype(BF16)
        phases = []
        for a in range(2):
            both = [dot(column, u_ref[a, b]) for b in range(2)]
            value = (jnp.where(right, both[1], both[0]) + bu_ref[...]) * keep
            phases.append(value.astype(BF16))
        places = []
        for k in range(2 * cycles):
            fine = jnp.where(flips[k] == 1, height - 1 - rows16, rows16)
            a = fine & 1
            place = a * n + k * 8 + lax.shift_right_arithmetic(fine - a, 1) + 2
            places.append(jnp.where(rows16 <= height, place, -1))
        column = pick(places, jnp.concatenate(phases, axis=0))
        skip_column = got[4 * n :]
        half_rows = 16 * cycles
        for side in range(2):
            part = slice(side * half_rows, (side + 1) * half_rows)
            sums = [
                dot(column[part], wd_ref[tap, 2 * side, :chans])
                + dot(skip_column[part], wd_ref[tap, 2 * side, chans:])
                for tap in range(3)
            ]
            for cycle in range(cycles):
                fine_sums[cycle, side] = column_sum(sums, cycle, height)

    near, far = near_ref[0], far_ref[0]
    far = jnp.where(ends, jnp.zeros_like(far), far)
    top = jnp.where(odd == 1, near, far)
    bottom = jnp.where(odd == 1, far, near)

    def pooled_row(row):
        if row < -1:
            return top[cols + half :]
        if row < 0:
            return top[cols : cols + half]
        if row < low:
            return pooled_ref[0, row]
        if row == low:
            return bottom[cols : cols + half]
        return bottom[cols + half :]

    stack_taps(upper, lambda row: pooled_row(row - 1), low + 2)
    lhs = upper[...].reshape((low + 2) * half, 3 * chans)
    total = shifted_sum(column_taps(lhs, wm_ref), half)
    total = total.reshape(low + 2, half, chans)
    place = lax.broadcasted_iota(jnp.int32, (half, chans), 0)
    rows = []
    for row in range(low + 2):
        value = total[row] + bm_ref[...]
        value = value + jnp.where(place == 0, pooled_pads[cycle_now, 0, row : row + 1], 0.0)
        value = value + jnp.where(place == half - 1, pooled_pads[cycle_now, 1, row : row + 1], 0.0)
        value = gelu(value)
        if row == 0:
            value = jnp.where(first_strip, 0.0, value)
        if row == low + 1:
            value = jnp.where(last_strip, 0.0, value)
        rows.append(value.astype(BF16))
    for a in range(2):
        part = jnp.concatenate(rows[1:] if a == 0 else rows[:-1], axis=0)
        for b in range(2):
            value = dot(part, u_ref[a, b]) + bu_ref[...]
            for k in range(low + 1):
                at = 2 * k + 1 - a
                for lane in range(0, chans, 128):
                    part_of = value[k * half : (k + 1) * half, lane : lane + 128]
                    joined[at, lane // 128, pl.ds(b, half, 2), :] = part_of

    def fine_row(row):
        value = jnp.concatenate([joined[row + 1, k] for k in range(chans // 128)], axis=1)
        if row < 0:
            value = jnp.where(first_strip, 0.0, value)
        if row >= height:
            value = jnp.where(last_strip, 0.0, value)
        return value.astype(BF16)

    stack_taps(stacked, fine_row, height)
    far_at = jnp.where(odd == 1, height - 1, 0)
    far_tap = jnp.where(odd == 1, 2, 0)
    extra = shifted_sum([dot(far[:cols], wd_ref[far_tap, tap, chans:]) for tap in range(3)], cols)
    pre_ref[0, far_at] = pre_ref[0, far_at] + extra
    edge = lax.broadcasted_iota(jnp.int32, (cols, chans), 0)
    chunk = 4
    for first in range(0, height, chunk):
        lhs = stacked[first : first + chunk].reshape(chunk * cols, 3 * chans)
        weights = [wd_ref[:, tap, :chans].reshape(3 * chans, chans) for tap in range(3)]
        total = shifted_sum([dot(lhs, w) for w in weights], cols)
        total = total.reshape(chunk, cols, chans)
        for row in range(chunk):
            at = first + row
            value = total[row] + pre_ref[0, at] + bd_ref[...]
            value = value + jnp.where(edge == 0, fine_sums[cycle_now, 0, at : at + 1], 0.0)
            value = value + jnp.where(edge == cols - 1, fine_sums[cycle_now, 1, at : at + 1], 0.0)
            out_ref[0, at] = value.astype(BF16)


def whole(shape):
    return pl.BlockSpec(shape, lambda *_: (0,) * len(shape))


def per_cycle(shape):
    return pl.BlockSpec((1,) + shape[1:], lambda c: (c,) + (0,) * (len(shape) - 1))


def smem():
    return pl.BlockSpec(memory_space=pltpu.SMEM)


def params(mib):
    return pltpu.CompilerParams(vmem_limit_bytes=mib * MIB)


def on_device(tiles, fields, seam_tile, seam_code, encoder_weight, encoder_bias, middle_weight,
              middle_bias, upconv_weight, upconv_bias, decoder_weight, decoder_offset_bias):
    cycles, height, cols, chans = fields.shape
    low, half = height // 2, cols // 2
    strips = tiles // FACES
    joint = strips == 4

    def strip(t):
        return (t + strips // 2) % strips

    near_pairs, far_pairs = [], []
    for t in range(tiles):
        pairs = near_pairs if strip(t) % 2 == 0 else far_pairs
        after = (t + 1) % tiles
        pairs += [(t, after), (after, t)]

    def tile_at(face, s):
        return (face * strips + s - strips // 2) % tiles

    groups = [
        [tile_at(face, s) for face in range(FACES) for s in (k, strips - 1 - k)]
        for k in range(strips // 2)
    ]
    members = 2 * FACES

    def share(x):
        return lax.all_to_all(x, "tile", 0, 0, tiled=True, axis_index_groups=groups)

    spec = Layout(tiles, height, 1, 0, 0)
    spec.payload = (2 * cycles * spec.stride + 1 + 15) // 16 * 16
    coarse_at = Layout(tiles, low, 2, 0, 0)
    fine_at = Layout(tiles, height, 1, 4 * cycles * coarse_at.stride, 0)
    payload = (fine_at.base + 2 * cycles * fine_at.stride + 15) // 16 * 16
    coarse_at.payload = fine_at.payload = payload

    odd = strip_of(tiles) % 2 == 1
    top, bottom = fields[:, 0], fields[:, -1]
    near = lax.ppermute(jnp.where(odd, top, bottom), "tile", near_pairs)
    far = lax.ppermute(jnp.where(odd, bottom, top), "tile", far_pairs)
    eb, mb, ub, db = (b.reshape(1, chans) for b in (encoder_bias, middle_bias, upconv_bias, decoder_offset_bias))

    edge = (cycles, height, 16, chans)
    row_shape = (cycles, cols, chans)
    left_edge = pl.BlockSpec(edge, lambda *_: (0, 0, 0, 0))
    right_edge = pl.BlockSpec(edge, lambda *_: (0, 0, cols // 16 - 1, 0))
    packed = pl.pallas_call(
        functools.partial(pack_fields, spec),
        out_shape=jax.ShapeDtypeStruct((members, spec.payload, chans), BF16),
        grid=(1,),
        in_specs=[left_edge, right_edge, whole(row_shape), whole(row_shape), smem(), smem()],
        out_specs=whole((members, spec.payload, chans)),
        scratch_shapes=[pltpu.VMEM((spec.payload, chans), F32)],
        compiler_params=params(16),
        name="pack_fields",
    )(fields, fields, near, near if joint else far, seam_tile, seam_code)
    recv = share(packed)
    table = recv[:, 2 * cycles * spec.stride, : 2 * cycles].astype(jnp.int32)

    tall = (cycles, height, cols, chans)
    wshape = (3, 3, chans, chans)
    conv_cost = pl.CostEstimate(
        flops=2 * cycles * height * cols * 9 * chans * chans, bytes_accessed=8 * MIB, transcendentals=0
    )
    skip, pre_row, pre_col = pl.pallas_call(
        functools.partial(encode, tiles),
        out_shape=[
            jax.ShapeDtypeStruct(tall, BF16),
            jax.ShapeDtypeStruct(row_shape, F32),
            jax.ShapeDtypeStruct((cycles, 2, height, chans), F32),
        ],
        grid=(cycles,),
        in_specs=[per_cycle(tall), per_cycle(row_shape), whole(wshape), whole((1, chans))],
        out_specs=[per_cycle(tall), per_cycle(row_shape), per_cycle((cycles, 2, height, chans))],
        scratch_shapes=[pltpu.VMEM((height, cols, 3 * chans), BF16)],
        compiler_params=params(24),
        cost_estimate=conv_cost,
        name="encode",
    )(fields, near, encoder_weight, eb)

    wide = (cycles, 2 * cols, chans)
    skip, pooled, near_out, far_out = pl.pallas_call(
        functools.partial(mend, spec),
        out_shape=[
            jax.ShapeDtypeStruct(tall, BF16),
            jax.ShapeDtypeStruct((cycles, low, half, chans), BF16),
            jax.ShapeDtypeStruct(wide, BF16),
            jax.ShapeDtypeStruct(wide, BF16),
        ],
        in_specs=[pl.BlockSpec(memory_space=pltpu.VMEM)] * 7 + [smem(), smem()],
        compiler_params=params(24),
        name="mend",
    )(recv.reshape(-1, chans), far, encoder_weight, eb, skip, pre_row, pre_col, seam_tile, seam_code)

    near2 = lax.ppermute(near_out, "tile", near_pairs)
    far2 = lax.ppermute(far_out, "tile", far_pairs)
    packed = pl.pallas_call(
        functools.partial(pack_skip, coarse_at, fine_at),
        out_shape=jax.ShapeDtypeStruct((members, payload, chans), BF16),
        grid=(1,),
        in_specs=[left_edge, right_edge, whole((cycles, low, half, chans)), whole(wide), whole(wide)],
        out_specs=whole((members, payload, chans)),
        scratch_shapes=[pltpu.VMEM((payload, chans), F32)],
        compiler_params=params(16),
        name="pack_skip",
    )(skip, skip, pooled, near2, near2 if joint else far2)
    recv2 = share(packed)

    pre = pl.pallas_call(
        functools.partial(decode_skip, tiles),
        out_shape=jax.ShapeDtypeStruct(tall, F32),
        grid=(cycles,),
        in_specs=[
            per_cycle(tall),
            per_cycle(wide),
            pl.BlockSpec(wshape, lambda c: (0, 0, 1, 0)),
        ],
        out_specs=per_cycle(tall),
        scratch_shapes=[pltpu.VMEM((height, cols, 3 * chans), BF16)],
        compiler_params=params(24),
        cost_estimate=conv_cost,
        name="decode_skip",
    )(skip, near2, decoder_weight)

    return pl.pallas_call(
        functools.partial(decode, coarse_at, fine_at),
        out_shape=jax.ShapeDtypeStruct(tall, BF16),
        grid=(cycles,),
        in_specs=[
            smem(),
            smem(),
            smem(),
            whole((members * payload, chans)),
            per_cycle(tall),
            per_cycle((cycles, low, half, chans)),
            per_cycle(wide),
            per_cycle(wide),
            whole(wshape),
            whole((1, chans)),
            whole((2, 2, chans, chans)),
            whole((1, chans)),
            whole((3, 3, 2 * chans, chans)),
            whole((1, chans)),
        ],
        out_specs=per_cycle(tall),
        scratch_shapes=[
            pltpu.VMEM((cycles, 2, 8, chans), F32),
            pltpu.VMEM((cycles, 2, height, chans), F32),
            pltpu.VMEM((height, cols, 3 * chans), BF16),
            pltpu.VMEM((low + 2, half, 3 * chans), BF16),
            pltpu.VMEM((height + 2, chans // 128, cols, 128), F32),
        ],
        compiler_params=params(40),
        name="decode",
    )(table, seam_tile, seam_code, recv2.reshape(-1, chans), pre, pooled, near2, far2,
      middle_weight, mb, upconv_weight, ub, decoder_weight, db)


def solution(mesh):
    return jax.shard_map(
        functools.partial(on_device, mesh.shape["tile"]),
        mesh=mesh,
        in_specs=(P("grp", "tile", None, None), P(None, "tile", None), P(None, "tile", None)) + (P(),) * 8,
        out_specs=P("grp", "tile", None, None),
        check_vma=False,
    )
```

```python
import functools

import jax
import jax.numpy as jnp
from jax import lax
from jax.experimental import pallas as pl
from jax.experimental.pallas import tpu as pltpu
from jax.sharding import PartitionSpec as P

F32 = jnp.float32
BF16 = jnp.bfloat16
FACES = 4
MIB = 1 << 20


def dot(a, b):
    return jnp.dot(a, b, preferred_element_type=F32)


def gelu(x):
    return 0.5 * x * (1.0 + jnp.tanh(0.7978845608 * (x + 0.044715 * x * x * x)))


def rows_iota(n):
    return lax.broadcasted_iota(jnp.int32, (n, 1), 0)


class Layout:
    def __init__(self, tiles, height, depth, columns, own, near, tail):
        self.tiles = tiles
        self.strips = tiles // FACES
        self.joint = self.strips == 4
        self.height = height
        self.depth = depth
        self.columns = columns
        self.own = own
        self.near = near
        self.far = near + tail
        self.payload = 0

    def source(self, strip, flip, face, column, row):
        height, last = self.height, self.strips - 1
        strip = jnp.where(flip == 1, last - strip, strip)
        row = jnp.where(flip == 1, height - 1 - row, row)
        upper = jnp.where(strip >= self.strips // 2, 1, 0)
        odd = lax.rem(strip, 2)
        above = row < 0
        below = row >= height
        away = jnp.where(above, -row, row - (height - 1)) - 1
        near = (above & (odd == 1)) | (below & (odd == 0))
        missing = (above & (strip == 0)) | (below & (strip == last))
        member = (face * 2 + upper) * self.payload
        inside = member + self.own + column * height + row
        beside = member + self.near + column * self.depth + away
        if self.joint:
            across = (face * 2 + 1 - upper) * self.payload + self.own + column * height
            far = across + jnp.where(above, height - 1 - away, away)
        else:
            far = member + self.far + column * self.depth + away
        place = jnp.where(above | below, jnp.where(near, beside, far), inside)
        return jnp.where(missing, -1, place)


def strip_of(tiles):
    strips = tiles // FACES
    return lax.rem(lax.axis_index("tile") + strips // 2, strips)


def seam_of(tile_ref, code_ref, tiles, cycle, side):
    strips = tiles // FACES
    partner = tile_ref[0, side, cycle]
    code = code_ref[0, side, cycle]
    other = lax.div(partner, tiles)
    place = partner - other * tiles + strips // 2
    face = lax.rem(lax.div(place, strips), FACES)
    return other, face, lax.rem(code, 2), lax.div(code, 2)


def pick(targets, table):
    wanted = jnp.concatenate(targets, axis=0)
    shape = (wanted.shape[0], table.shape[0])
    lanes = lax.broadcasted_iota(jnp.int32, shape, 1)
    chooser = jnp.where(lanes == wanted, 1.0, 0.0).astype(BF16)
    return dot(chooser, table).astype(BF16)


def shifted_sum(taps, cols):
    left, middle, right = taps
    n = middle.shape[0]
    place = lax.broadcasted_iota(jnp.int32, middle.shape, 0) & (cols - 1)
    left = jnp.where(place == 0, 0.0, pltpu.roll(left, 1, 0))
    right = jnp.where(place == cols - 1, 0.0, pltpu.roll(right, n - 1, 0))
    return middle + left + right


def stack_taps(stacked, row_of, rows):
    depth = stacked.shape[-1] // 3
    for row in range(-1, rows + 1):
        value = row_of(row)
        for tap in range(3):
            at = row + 1 - tap
            if 0 <= at < rows:
                stacked[at, :, tap * depth : (tap + 1) * depth] = value


def column_taps(lhs, weight_ref):
    depth = weight_ref.shape[2]
    return [
        dot(lhs, weight_ref[:, tap].reshape(3 * depth, weight_ref.shape[3]))
        for tap in range(3)
    ]


def halo_rows(rows_ref, top, bottom):
    def row_of(row):
        if row < 0:
            return top
        if row >= rows_ref.shape[0]:
            return bottom
        return rows_ref[row]

    return row_of


def top_and_bottom(near, far, odd, ends):
    far = jnp.where(ends, jnp.zeros_like(far), far)
    return jnp.where(odd == 1, near, far), jnp.where(odd == 1, far, near)


def column_sum(parts, cycle, height):
    at = cycle * 16
    return sum(parts[tap][at + tap : at + tap + height] for tap in range(3))


def lift(layout, x_hbm, tile_ref, code_ref, own_hbm, near_tail_hbm, far_tail_hbm, near_hbm, far_hbm,
         edges, rows, own, tails, own16, tails16, in_sems, out_sems):
    height = layout.height
    cycles, cols = x_hbm.shape[0], x_hbm.shape[2]
    upper = lax.rem(strip_of(layout.tiles), 2) * (height - 1)
    nearest = (height - 1 - upper, upper)
    pairs = [(x_hbm.at[:, :, pl.ds(first, 16)], edges.at[side]) for side, first in enumerate((0, cols - 16))]
    arriving = fetch(pairs + [(x_hbm.at[:, nearest[k]], rows.at[k]) for k in range(2)], in_sems)
    lanes = lax.broadcasted_iota(jnp.int32, (1, own.shape[1]), 1)
    noted = jnp.zeros((1, own.shape[1]), F32)
    for cycle in range(cycles):
        for side in range(2):
            other, face, side_bit, flip = seam_of(tile_ref, code_ref, layout.tiles, cycle, side)
            number = (other * FACES + face) * 4 + flip * 2 + side_bit
            noted = jnp.where(lanes == cycle * 2 + side, number.astype(F32), noted)
    tails[...] = jnp.zeros_like(tails)
    for k in range(2):
        tails[k, layout.columns : layout.columns + 1] = noted
    for side in range(2):
        arriving[side].wait()
        at = 15 * side
        for cycle in range(cycles):
            column = cycle * 2 + side
            for row in range(height):
                value = edges[side, cycle, row].astype(F32)[at : at + 1]
                own[column * height + row : column * height + row + 1] = value
            for k in range(2):
                value = edges[side, cycle, nearest[k]].astype(F32)[at : at + 1]
                tails[k, column : column + 1] = value
    own16[...] = own[...].astype(BF16)
    tails16[...] = tails[...].astype(BF16)
    pairs = [(tails16.at[0], near_tail_hbm), (tails16.at[1], far_tail_hbm), (own16, own_hbm)]
    for copy in arriving[2:]:
        copy.wait()
    leaving = fetch(pairs + [(rows.at[0], near_hbm), (rows.at[1], far_hbm)], out_sems)
    for copy in leaving:
        copy.wait()


def fetch(pairs, sems):
    copies = [pltpu.make_async_copy(src, dst, sems.at[k]) for k, (src, dst) in enumerate(pairs)]
    for copy in copies:
        copy.start()
    return copies


def encode(tiles, x_hbm, near_ref, far_ref, w_hbm, b_hbm, skip_hbm, pooled_hbm, near_hbm, far_hbm, pre_hbm,
           x_ref, w_ref, b_ref, stacked, skip_ref, pooled_ref, rows_ref, pre_ref, paired, in_sems, out_sems):
    cycles, height, cols, chans = x_ref.shape
    half = cols // 2
    pairs = [(b_hbm, b_ref), (x_hbm.at[0], x_ref.at[0])]
    pairs += [(w_hbm.at[:, tap], w_ref.at[tap]) for tap in range(3)]
    arriving = fetch(pairs, in_sems.at[pl.ds(0, 5)])
    strip = strip_of(tiles)
    odd = lax.rem(strip, 2)
    ends = (strip == 0) | (strip == tiles // FACES - 1)
    arriving[0].wait()
    arriving[1].wait()
    leaving = []
    for cycle in range(cycles):
        if cycle > 0:
            arriving[4 + cycle].wait()
        top, bottom = top_and_bottom(near_ref[cycle], far_ref[cycle], odd, ends)
        stack_taps(stacked, halo_rows(x_ref.at[cycle], top, bottom), height)
        for row in range(height):
            taps = []
            for tap in range(3):
                if cycle == 0 and row == 0:
                    arriving[2 + tap].wait()
                taps.append(dot(stacked[row], w_ref[tap].reshape(3 * chans, chans)))
            if cycle == 0 and row == 0:
                pairs = [(x_hbm.at[k], x_ref.at[k]) for k in range(1, cycles)]
                arriving += fetch(pairs, in_sems.at[pl.ds(5, cycles - 1)])
            total = shifted_sum(taps, cols) + b_ref[...]
            value = gelu(total).astype(BF16)
            skip_ref[cycle, row] = value
            pre_ref[cycle, 0, row : row + 1] = total[:1]
            pre_ref[cycle, 1, row : row + 1] = total[cols - 1 :]
            if row % 2 == 0:
                before = value.astype(F32)
            else:
                pair = 0.25 * (before + value.astype(F32))
                for lane in range(0, chans, 128):
                    paired[...] = pair[:, lane : lane + 128]
                    mean = paired[pl.ds(0, half, 2), :] + paired[pl.ds(1, half, 2), :]
                    pooled_ref[cycle, row // 2, :, lane : lane + 128] = mean.astype(BF16)
            if row % 4 == 3:
                rows = (cycle, pl.ds(row - 3, 4))
                leaving += fetch([(skip_ref.at[rows], skip_hbm.at[rows])], out_sems.at[cycle, pl.ds(row // 4, 1)])
        low = height // 2 - 1
        for k, at_top in ((0, odd == 1), (1, odd == 0)):
            rows_ref[k, cycle, :cols] = skip_ref[cycle, jnp.where(at_top, 0, height - 1)]
            rows_ref[k, cycle, cols : cols + half] = pooled_ref[cycle, jnp.where(at_top, 0, low)]
            rows_ref[k, cycle, cols + half :] = pooled_ref[cycle, jnp.where(at_top, 1, low - 1)]
        pairs = [(rows_ref.at[0, cycle], near_hbm.at[cycle]), (rows_ref.at[1, cycle], far_hbm.at[cycle])]
        pairs += [(pooled_ref.at[cycle], pooled_hbm.at[cycle]), (pre_ref.at[cycle], pre_hbm.at[cycle])]
        leaving += fetch(pairs, out_sems.at[cycle, pl.ds(height // 4, 4)])
    for copy in leaving:
        copy.wait()


def mend(layout, coarse, fine, recv_ref, w_hbm, skip_in, pooled_in, near_in, far_in, pre_hbm, tile_ref, code_ref,
         skip_hbm, pooled_hbm, near_hbm, far_hbm, own_hbm, near_tail_hbm, far_tail_hbm, table_hbm,
         w_ref, pre_ref, edges, pools, own, tails, own16, tails16, table_ref, in_sems, out_sems):
    tiles, height, low = layout.tiles, layout.height, coarse.height
    cycles, cols, chans = skip_in.shape[0], skip_in.shape[2], skip_in.shape[3]
    half = cols // 2
    pairs = [(w_hbm.at[:, 2 * side], w_ref.at[side]) for side in range(2)] + [(pre_hbm, pre_ref)]
    for side in range(2):
        pairs.append((skip_in.at[:, :, pl.ds((cols - 16) * side, 16)], edges.at[side]))
        pairs.append((pooled_in.at[:, :, pl.ds((half - 16) * side, 16)], pools.at[side]))
    arriving = fetch(pairs, in_sems)
    strip = strip_of(tiles)
    odd = lax.rem(strip, 2)
    row_iota = rows_iota(16) - 1
    targets = []
    for side in range(2):
        for cycle in range(cycles):
            other, face, side_bit, flip = seam_of(tile_ref, code_ref, tiles, cycle, side)
            place = layout.source(strip, flip, face, other * 2 + side_bit, row_iota)
            targets.append(jnp.where(row_iota <= height, place, -1))
    pads = pick(targets, recv_ref[...])
    noted = layout.near + layout.columns
    for member in range(2 * FACES):
        at = member * layout.payload + noted // 16 * 16
        block = recv_ref[at : at + 16, :128].astype(F32)
        table_ref[member : member + 1] = block[noted % 16 : noted % 16 + 1].astype(jnp.int32)
    part = pads.shape[0] // 2
    for copy in arriving[:3]:
        copy.wait()
    seams = [
        [dot(pads[side * part : (side + 1) * part], w_ref[side, tap]) for tap in range(3)] for side in range(2)
    ]
    iota16 = lax.broadcasted_iota(jnp.int32, (16, chans), 0)
    tails[...] = jnp.zeros_like(tails)
    for copy in arriving[3:]:
        copy.wait()
    at_top = (odd == 1, odd == 0)
    skip_at = [jnp.where(t, 0, height - 1) for t in at_top]
    pool_at = [(jnp.where(t, 0, low - 1), jnp.where(t, 1, low - 2)) for t in at_top]
    for cycle in range(cycles):
        for side in range(2):
            column = cycle * 2 + side
            at, inward = (0, 1) if side == 0 else (15, 14)
            total = gelu(pre_ref[cycle, side] + column_sum(seams[side], cycle, height))
            start = fine.own + column * height
            own[start : start + height] = total
            for row in range(height):
                block = edges[side, cycle, row].astype(F32)
                block = jnp.where(iota16 == at, total[row : row + 1], block).astype(BF16)
                edges[side, cycle, row] = block
                if row % 2 == 0:
                    before = block.astype(F32)
                else:
                    pair = before + block.astype(F32)
                    mean = 0.25 * (pair[at : at + 1] + pair[inward : inward + 1])
                    block = pools[side, cycle, row // 2].astype(F32)
                    block = jnp.where(iota16 == at, mean, block)
                    pools[side, cycle, row // 2] = block.astype(BF16)
                    for depth, place in enumerate((at, inward)):
                        start = coarse.own + (column * 2 + depth) * low + row // 2
                        own[start : start + 1] = block[place : place + 1]
            for k in range(2):
                start = fine.near - coarse.near + column
                value = edges[side, cycle, skip_at[k]].astype(F32)
                tails[k, start : start + 1] = value[at : at + 1]
                for away in range(2):
                    value = pools[side, cycle, pool_at[k][away]].astype(F32)
                    for depth, place in enumerate((at, inward)):
                        start = (column * 2 + depth) * 2 + away
                        tails[k, start : start + 1] = value[place : place + 1]
    own16[...] = own[...].astype(BF16)
    tails16[...] = tails[...].astype(BF16)
    pairs = [(tails16.at[0], near_tail_hbm), (own16, own_hbm), (tails16.at[1], far_tail_hbm), (table_ref, table_hbm)]
    for side in range(2):
        pairs.append((edges.at[side], skip_hbm.at[:, :, pl.ds((cols - 16) * side, 16)]))
        pairs.append((pools.at[side], pooled_hbm.at[:, :, pl.ds((half - 16) * side, 16)]))
        for k, ref in enumerate((near_hbm, far_hbm)):
            pairs.append((edges.at[side, :, skip_at[k]], ref.at[:, pl.ds((cols - 16) * side, 16)]))
            for away in range(2):
                first = cols + away * half + (half - 16) * side
                pairs.append((pools.at[side, :, pool_at[k][away]], ref.at[:, pl.ds(first, 16)]))
    leaving = fetch(pairs, out_sems)
    for copy in leaving:
        copy.wait()


def decode(tiles, skip_hbm, pooled_hbm, near_ref, far_ref, wm_hbm, bm_hbm, u_hbm, bu_hbm, wd_hbm, bd_hbm,
           out_hbm, edge_hbm, coarse_hbm, skip_ref, pooled_ref, wm_ref, bm_ref, u_ref, bu_ref, wd_ref,
           bd_ref, out_ref, edge_ref, coarse_ref, stacked, upper, joined, in_sems, out_sems):
    strips = tiles // FACES
    cycles, height, cols, chans = skip_ref.shape
    low, half = height // 2, cols // 2
    pairs = [(bm_hbm, bm_ref), (bu_hbm, bu_ref), (bd_hbm, bd_ref), (pooled_hbm, pooled_ref)]
    pairs += [(wm_hbm, wm_ref), (u_hbm, u_ref), (skip_hbm.at[0], skip_ref.at[0])]
    for tap in range(3):
        for part in range(2):
            source = wd_hbm.at[:, tap, pl.ds(part * chans, chans)]
            pairs.append((source, wd_ref.at[tap, pl.ds(3 * part, 3)]))
    pairs += [(skip_hbm.at[cycle], skip_ref.at[cycle]) for cycle in range(1, cycles)]
    arriving = fetch(pairs, in_sems)
    strip = strip_of(tiles)
    odd = lax.rem(strip, 2)
    first_strip, last_strip = strip == 0, strip == strips - 1
    ends = first_strip | last_strip
    place = lax.broadcasted_iota(jnp.int32, (cols, chans), 0)
    inner = (place > 1) & (place < cols - 2)
    coarse_ref[...] = jnp.zeros_like(coarse_ref)
    chunk = 1
    leaving = []
    for copy in arriving[:4]:
        copy.wait()
    for cycle in range(cycles):
        top, bottom = top_and_bottom(near_ref[cycle], far_ref[cycle], odd, ends)

        def pooled_row(row):
            if row < -1:
                return top[cols + half :]
            if row < 0:
                return top[cols : cols + half]
            if row < low:
                return pooled_ref[cycle, row]
            if row == low:
                return bottom[cols : cols + half]
            return bottom[cols + half :]

        stack_taps(upper, lambda row: pooled_row(row - 1), low + 2)
        lhs = upper[...].reshape((low + 2) * half, 3 * chans)
        if cycle == 0:
            arriving[4].wait()
        total = shifted_sum(column_taps(lhs, wm_ref), half) + bm_ref[...]
        for row in range(low + 2):
            coarse_ref[cycle, 0, row + 1 : row + 2] = total[row * half : row * half + 1]
            coarse_ref[cycle, 1, row + 1 : row + 2] = total[(row + 1) * half - 1 : (row + 1) * half]
        coarse = gelu(total).astype(BF16)
        if cycle == 0:
            arriving[5].wait()
        for a in range(2):
            part = coarse[half:] if a == 0 else coarse[:-half]
            for b in range(2):
                value = dot(part, u_ref[a, b]) + bu_ref[...]
                for k in range(low + 1):
                    at = 2 * k + 1 - a
                    for lane in range(0, chans, 128):
                        part_of = value[k * half : (k + 1) * half, lane : lane + 128]
                        joined[at, lane // 128, pl.ds(b, half, 2), :] = part_of
        arriving[6 if cycle == 0 else 12 + cycle].wait()

        def joined_row(row):
            value = jnp.concatenate([joined[row + 1, k] for k in range(chans // 128)], axis=1)
            keep = inner
            if row < 0:
                keep = keep & jnp.logical_not(first_strip)
            if row >= height:
                keep = keep & jnp.logical_not(last_strip)
            return jnp.where(keep, value, 0.0).astype(BF16)

        stack_taps(stacked.at[:, :, pl.ds(0, 3 * chans)], joined_row, height)
        skip_row = halo_rows(skip_ref.at[cycle], top[:cols], bottom[:cols])
        stack_taps(stacked.at[:, :, pl.ds(3 * chans, 3 * chans)], skip_row, height)
        for first in range(0, height, chunk):
            lhs = stacked[first : first + chunk].reshape(chunk * cols, 6 * chans)
            taps = []
            for tap in range(3):
                if cycle == 0 and first == 0:
                    arriving[7 + 2 * tap].wait()
                    arriving[8 + 2 * tap].wait()
                taps.append(dot(lhs, wd_ref[tap].reshape(6 * chans, chans)))
            total = (shifted_sum(taps, cols) + bd_ref[...]).reshape(chunk, cols, chans)
            out_ref[cycle, first : first + chunk] = total.astype(BF16)
            edge_ref[cycle, 0, first : first + chunk] = total[:, :16]
            edge_ref[cycle, 1, first : first + chunk] = total[:, cols - 16 :]
            rows = (cycle, pl.ds(first, chunk))
            leaving += fetch([(out_ref.at[rows], out_hbm.at[rows])], out_sems.at[cycle, pl.ds(first // chunk, 1)])
    leaving += fetch([(edge_ref, edge_hbm), (coarse_ref, coarse_hbm)], out_sems.at[cycles, pl.ds(0, 2)])
    for copy in leaving:
        copy.wait()


def seal(coarse_at, fine_at, tab_ref, tile_ref, code_ref, recv_ref, coarse_hbm, edge_hbm, wm_hbm, bm_hbm, u_hbm,
         bu_hbm, wd_hbm, out_in, out_hbm, coarse_ref, edge_ref, wm_ref, bm_ref, u_ref, bu_ref, wu_ref, ws_ref, out_ref,
         in_sems, out_sems):
    tiles, strips, height = coarse_at.tiles, coarse_at.strips, fine_at.height
    cycles, _, _, _, chans = edge_ref.shape
    cols = out_hbm.shape[2]
    low = height // 2
    pairs = [(bm_hbm, bm_ref), (bu_hbm, bu_ref), (coarse_hbm, coarse_ref), (wm_hbm, wm_ref), (u_hbm, u_ref)]
    pairs += [(wd_hbm.at[:, :, pl.ds(0, chans)], wu_ref), (edge_hbm, edge_ref)]
    pairs += [(wd_hbm.at[:, 2 * side, pl.ds(chans, chans)], ws_ref.at[side]) for side in range(2)]
    arriving = fetch(pairs, in_sems)
    strip = strip_of(tiles)
    rows8 = rows_iota(8) - 2
    rows16 = rows_iota(16) - 1
    aligned, taps, skips, sides, flips, strips_at = [], [[], [], []], [], [], [], []
    for side in range(2):
        for cycle in range(cycles):
            other, face, side_bit, flip = seam_of(tile_ref, code_ref, tiles, cycle, side)
            column = other * 2 + side_bit
            aligned.append(coarse_at.source(strip, flip, face, column * 2, rows8))
            place = fine_at.source(strip, flip, face, column, rows16)
            skips.append(jnp.where(rows16 <= height, place, -1))
            there = jnp.where(flip == 1, strips - 1 - strip, strip)
            number = tab_ref[face * 2, column]
            beyond = lax.div(number, 4)
            code = lax.rem(number, 4)
            other2, face2 = lax.div(beyond, FACES), lax.rem(beyond, FACES)
            column2 = other2 * 2 + lax.rem(code, 2)
            pad = coarse_at.source(there, lax.div(code, 2), face2, column2 * 2, rows8)
            edge = coarse_at.source(there, 0, face, column * 2, rows8)
            inner = coarse_at.source(there, 0, face, column * 2 + 1, rows8)
            taps[0].append(jnp.where(side_bit == 0, pad, inner))
            taps[1].append(edge)
            taps[2].append(jnp.where(side_bit == 0, inner, pad))
            sides.append(side_bit)
            flips.append(flip)
            strips_at.append(there)
    got = pick(aligned + taps[0] + taps[1] + taps[2] + skips, recv_ref[...])
    n = 8 * 2 * cycles
    at8 = lax.broadcasted_iota(jnp.int32, (8, chans), 0) - 2

    def on_face(s):
        return jnp.where(((at8 < 0) & (s == 0)) | ((at8 >= low) & (s == strips - 1)), 0.0, 1.0)

    for copy in arriving[:4]:
        copy.wait()
    own = got[:n]
    there = got[n : 4 * n]
    rows = []
    for row in range(3):
        here = [dot(own[side * n // 2 : (side + 1) * n // 2], wm_ref[row, 2 * side]) for side in range(2)]
        away = sum(dot(there[tap * n : (tap + 1) * n], wm_ref[row, tap]) for tap in range(3))
        rows.append(jnp.concatenate(here + [away], axis=0))
    total = pltpu.roll(rows[0], 1, 0) + rows[1] + pltpu.roll(rows[2], 2 * n - 1, 0)
    mine = [
        total[(side * cycles + cycle) * 8 : (side * cycles + cycle + 1) * 8] + coarse_ref[cycle, side]
        for side in range(2)
        for cycle in range(cycles)
    ]
    total = jnp.concatenate(mine + [total[n:] + bm_ref[...]], axis=0)
    keep = jnp.concatenate([on_face(s) for s in [strip] * (2 * cycles) + strips_at], axis=0)
    column = (gelu(total) * keep).astype(BF16)
    arriving[4].wait()
    phases = [
        [((dot(column, u_ref[a, b]) + bu_ref[...]) * keep).astype(BF16) for b in range(2)] for a in range(2)
    ]
    right = jnp.concatenate([jnp.where(at8 > -99, b, 0) for b in sides], axis=0) == 1
    place = lax.shift_right_arithmetic(rows16 - (rows16 & 1), 1) + 2
    fine_own = [jnp.where(rows16 <= height, (rows16 & 1) * n + k * 8 + place, -1) for k in range(2 * cycles)]
    fine_there = []
    for k in range(2 * cycles):
        fine = jnp.where(flips[k] == 1, height - 1 - rows16, rows16)
        a = fine & 1
        place = a * n + k * 8 + lax.shift_right_arithmetic(fine - a, 1) + 2
        fine_there.append(jnp.where(rows16 <= height, place, -1))
    beyond = [jnp.where(right, phases[a][1][n:], phases[a][0][n:]) for a in range(2)]
    outer = pick(fine_there, jnp.concatenate(beyond, axis=0))
    inside = [pick(fine_own, jnp.concatenate([phases[a][b][:n] for a in range(2)], axis=0)) for b in range(2)]
    skip_pad = got[4 * n :]
    m = 16 * cycles
    lines = [[outer[:m], inside[0][:m], inside[1][:m]], [outer[m:], inside[1][m:], inside[0][m:]]]
    for copy in arriving[5:]:
        copy.wait()
    sums = [[[], [], []], [[], [], []]]
    for row in range(3):
        found = [[0.0, 0.0, 0.0], [0.0, 0.0, 0.0]]
        for tap in range(3):
            uses = []
            for side in range(2):
                offset = tap if side == 0 else 2 - tap
                uses += [(side, line, line - offset) for line in range(3) if line >= offset]
            value = dot(jnp.concatenate([lines[side][line] for side, line, _ in uses], axis=0), wu_ref[row, tap])
            for k, (side, _, into) in enumerate(uses):
                found[side][into] = found[side][into] + value[k * m : (k + 1) * m]
        for side in range(2):
            found[side][0] = found[side][0] + dot(skip_pad[side * m : (side + 1) * m], ws_ref[side, row])
            for into in range(3):
                sums[side][into].append(found[side][into])
    iota16 = lax.broadcasted_iota(jnp.int32, (16, chans), 0)
    for side in range(2):
        for cycle in range(cycles):
            extra = [column_sum(sums[side][into], cycle, height) for into in range(3)]
            for row in range(height):
                value = edge_ref[cycle, side, row]
                for into in range(3):
                    at = into if side == 0 else 15 - into
                    value = value + jnp.where(iota16 == at, extra[into][row : row + 1], 0.0)
                out_ref[side, cycle, row] = value.astype(BF16)
    leaving = fetch(
        [(out_ref.at[side], out_hbm.at[:, :, pl.ds((cols - 16) * side, 16)]) for side in range(2)], out_sems
    )
    for copy in leaving:
        copy.wait()


def on_device(tiles, fields, seam_tile, seam_code, encoder_weight, encoder_bias, middle_weight,
              middle_bias, upconv_weight, upconv_bias, decoder_weight, decoder_offset_bias):
    cycles, height, cols, chans = fields.shape
    low, half = height // 2, cols // 2
    strips = tiles // FACES
    joint = strips == 4

    def strip(t):
        return (t + strips // 2) % strips

    near_pairs, far_pairs = [], []
    for t in range(tiles):
        pairs = near_pairs if strip(t) % 2 == 0 else far_pairs
        after = (t + 1) % tiles
        pairs += [(t, after), (after, t)]

    def tile_at(face, s):
        return (face * strips + s - strips // 2) % tiles

    groups = [
        [tile_at(face, s) for face in range(FACES) for s in (k, strips - 1 - k)]
        for k in range(strips // 2)
    ]
    members = 2 * FACES

    def share(x):
        return lax.all_to_all(x, "tile", 0, 0, tiled=True, axis_index_groups=groups)

    columns = 2 * cycles
    tail1 = (columns + 1 + 15) // 16 * 16
    spec = Layout(tiles, height, 1, columns, 0, columns * height, tail1)
    own2 = 2 * columns * low + columns * height
    tail2 = (4 * columns + columns + 15) // 16 * 16
    coarse_at = Layout(tiles, low, 2, 2 * columns, 0, own2, tail2)
    fine_at = Layout(tiles, height, 1, columns, 2 * columns * low, own2 + 4 * columns, tail2)
    halos = 1 if joint else 2
    spec.payload = columns * height + halos * tail1
    payload = own2 + halos * tail2
    coarse_at.payload = fine_at.payload = payload

    def to_near(x):
        return lax.ppermute(x, "tile", near_pairs)

    def to_far(x):
        return lax.ppermute(x, "tile", far_pairs)

    def pack(own, near_tail, far_tail):
        parts = [own, to_near(near_tail)] + ([] if joint else [to_far(far_tail)])
        parts = [jnp.broadcast_to(part[None], (members,) + part.shape) for part in parts]
        return share(jnp.concatenate(parts, axis=1))

    seams = (jnp.transpose(seam_tile, (1, 2, 0)), jnp.transpose(seam_code, (1, 2, 0)))
    eb, mb, ub, db = (b.reshape(1, chans) for b in (encoder_bias, middle_bias, upconv_bias, decoder_offset_bias))

    hbm = pl.BlockSpec(memory_space=pltpu.HBM)
    vmem = pl.BlockSpec(memory_space=pltpu.VMEM)
    smem = pl.BlockSpec(memory_space=pltpu.SMEM)
    dma = pltpu.SemaphoreType.DMA
    tall = (cycles, height, cols, chans)
    row_shape = (cycles, cols, chans)
    wide = (cycles, 2 * cols, chans)
    square = (chans, chans)
    wshape = (3, 3) + square
    pooled_shape = (cycles, low, half, chans)
    edge_shape = (2, cycles, height, 16, chans)

    def call(body, name, outs, in_specs, out_specs, scratch, *args, **options):
        return pl.pallas_call(
            body,
            out_shape=[jax.ShapeDtypeStruct(shape, dtype) for shape, dtype in outs],
            in_specs=in_specs,
            out_specs=out_specs,
            scratch_shapes=[pltpu.VMEM(*x) if isinstance(x, tuple) else x for x in scratch],
            compiler_params=pltpu.CompilerParams(vmem_limit_bytes=56 * MIB),
            name=name,
            **options,
        )(*args)

    far_cost = pl.CostEstimate(flops=10**12, bytes_accessed=10**9, transcendentals=0)
    vector = (1, chans)
    own, near_tail, far_tail, near, far = call(
        functools.partial(lift, spec), "lift",
        [((columns * height, chans), BF16)] + [((tail1, chans), BF16)] * 2 + [(row_shape, BF16)] * 2,
        [hbm, smem, smem], [hbm] * 5,
        [(edge_shape, BF16), ((2,) + row_shape, BF16), ((columns * height, chans), F32), ((2, tail1, chans), F32),
         ((columns * height, chans), BF16), ((2, tail1, chans), BF16), dma((4,)), dma((5,))],
        fields, *seams,
    )
    recv = pack(own, near_tail, far_tail)
    near, far = to_near(near), to_far(far)
    pre_shape = (cycles, 2, height, chans)
    skip, pooled, near, far, pre_col = call(
        functools.partial(encode, tiles), "encode",
        [(tall, BF16), (pooled_shape, BF16), (wide, BF16), (wide, BF16), (pre_shape, F32)],
        [hbm, vmem, vmem, hbm, hbm], [hbm] * 5,
        [(tall, BF16), (wshape, BF16), (vector, F32), ((height, cols, 3 * chans), BF16), (tall, BF16),
         (pooled_shape, BF16), ((2,) + wide, BF16), (pre_shape, F32), ((cols, 128), F32),
         dma((4 + cycles,)), dma((cycles, height // 4 + 4))],
        fields, near, far, encoder_weight, eb,
        cost_estimate=far_cost,
    )
    pool_edges = (2, cycles, low, 16, chans)
    skip, pooled, near, far, own, near_tail, far_tail, table = call(
        functools.partial(mend, spec, coarse_at, fine_at), "mend",
        [(tall, BF16), (pooled_shape, BF16), (wide, BF16), (wide, BF16), ((own2, chans), BF16)]
        + [((tail2, chans), BF16)] * 2 + [((members, 128), jnp.int32)],
        [vmem] + [hbm] * 6 + [smem, smem], [hbm] * 8,
        [((2, 3) + square, BF16), (pre_shape, F32), (edge_shape, BF16), (pool_edges, BF16), ((own2, chans), F32),
         ((2, tail2, chans), F32), ((own2, chans), BF16), ((2, tail2, chans), BF16), ((members, 128), jnp.int32),
         dma((7,)), dma((20,))],
        recv.reshape(-1, chans), encoder_weight, skip, pooled, near, far, pre_col, *seams,
        input_output_aliases={2: 0, 3: 1, 4: 2, 5: 3},
    )
    recv2 = pack(own, near_tail, far_tail)
    near2, far2 = to_near(near), to_far(far)
    edges = (cycles, 2, height, 16, chans)
    coarse_edges = (cycles, 2, 8, chans)
    out, edge, coarse = call(
        functools.partial(decode, tiles), "decode",
        [(tall, BF16), (edges, F32), (coarse_edges, F32)],
        [hbm, hbm, vmem, vmem] + [hbm] * 6, [hbm, hbm, hbm],
        [(tall, BF16), (pooled_shape, BF16), (wshape, BF16), (vector, F32), ((2, 2) + square, BF16),
         (vector, F32), ((3, 6) + square, BF16), (vector, F32), (tall, BF16), (edges, F32), (coarse_edges, F32),
         ((height, cols, 6 * chans), BF16), ((low + 2, half, 3 * chans), BF16),
         ((height + 2, chans // 128, cols, 128), F32), dma((12 + cycles,)), dma((cycles + 1, height))],
        skip, pooled, near2, far2, middle_weight, mb, upconv_weight, ub, decoder_weight, db,
        cost_estimate=far_cost,
    )
    (out,) = call(
        functools.partial(seal, coarse_at, fine_at), "seal",
        [(tall, BF16)],
        [smem, smem, smem, vmem] + [hbm] * 8, [hbm],
        [(coarse_edges, F32), (edges, F32), (wshape, BF16), (vector, F32), ((2, 2) + square, BF16), (vector, F32),
         (wshape, BF16), ((2, 3) + square, BF16), (edge_shape, BF16), dma((9,)), dma((2,))],
        table, *seams, recv2.reshape(-1, chans), coarse, edge, middle_weight, mb, upconv_weight, ub, decoder_weight, out,
        input_output_aliases={11: 0},
    )
    return out


def solution(mesh):
    return jax.shard_map(
        functools.partial(on_device, mesh.shape["tile"]),
        mesh=mesh,
        in_specs=(P("grp", "tile", None, None), P(None, "tile", None), P(None, "tile", None)) + (P(),) * 8,
        out_specs=P("grp", "tile", None, None),
        check_vma=False,
    )
```

```python
import functools

import jax
import jax.numpy as jnp
from jax import lax
from jax.experimental import pallas as pl
from jax.experimental.pallas import tpu as pltpu
from jax.sharding import PartitionSpec as P

F32 = jnp.float32
BF16 = jnp.bfloat16
FACES = 4
MIB = 1 << 20


def dot(a, b):
    return jnp.dot(a, b, preferred_element_type=F32)


def gelu(x):
    return 0.5 * x * (1.0 + jnp.tanh(0.7978845608 * (x + 0.044715 * x * x * x)))


def rows_iota(n):
    return lax.broadcasted_iota(jnp.int32, (n, 1), 0)


class Layout:
    def __init__(self, tiles, height, depth, columns, own, near, tail):
        self.tiles = tiles
        self.strips = tiles // FACES
        self.joint = self.strips == 4
        self.height = height
        self.depth = depth
        self.columns = columns
        self.own = own
        self.near = near
        self.far = near + tail
        self.payload = 0

    def source(self, strip, flip, face, column, row):
        height, last = self.height, self.strips - 1
        strip = jnp.where(flip == 1, last - strip, strip)
        row = jnp.where(flip == 1, height - 1 - row, row)
        upper = jnp.where(strip >= self.strips // 2, 1, 0)
        odd = lax.rem(strip, 2)
        above = row < 0
        below = row >= height
        away = jnp.where(above, -row, row - (height - 1)) - 1
        near = (above & (odd == 1)) | (below & (odd == 0))
        missing = (above & (strip == 0)) | (below & (strip == last))
        member = (face * 2 + upper) * self.payload
        inside = member + self.own + column * height + row
        beside = member + self.near + column * self.depth + away
        if self.joint:
            across = (face * 2 + 1 - upper) * self.payload + self.own + column * height
            far = across + jnp.where(above, height - 1 - away, away)
        else:
            far = member + self.far + column * self.depth + away
        place = jnp.where(above | below, jnp.where(near, beside, far), inside)
        return jnp.where(missing, -1, place)


def strip_of(tiles):
    strips = tiles // FACES
    return lax.rem(lax.axis_index("tile") + strips // 2, strips)


def seam_of(tile_ref, code_ref, tiles, cycle, side):
    strips = tiles // FACES
    partner = tile_ref[0, side, cycle]
    code = code_ref[0, side, cycle]
    other = lax.div(partner, tiles)
    place = partner - other * tiles + strips // 2
    face = lax.rem(lax.div(place, strips), FACES)
    return other, face, lax.rem(code, 2), lax.div(code, 2)


def pick(targets, table):
    wanted = jnp.concatenate(targets, axis=0)
    shape = (wanted.shape[0], table.shape[0])
    lanes = lax.broadcasted_iota(jnp.int32, shape, 1)
    chooser = jnp.where(lanes == wanted, 1.0, 0.0).astype(BF16)
    return dot(chooser, table).astype(BF16)


def shifted_sum(taps, cols):
    left, middle, right = taps
    n = middle.shape[0]
    place = lax.broadcasted_iota(jnp.int32, middle.shape, 0) & (cols - 1)
    left = jnp.where(place == 0, 0.0, pltpu.roll(left, 1, 0))
    right = jnp.where(place == cols - 1, 0.0, pltpu.roll(right, n - 1, 0))
    return middle + left + right


def stack_taps(stacked, row_of, rows):
    depth = stacked.shape[-1] // 3
    for row in range(-1, rows + 1):
        value = row_of(row)
        for tap in range(3):
            at = row + 1 - tap
            if 0 <= at < rows:
                stacked[at, :, tap * depth : (tap + 1) * depth] = value


def column_taps(lhs, weight_ref):
    depth = weight_ref.shape[2]
    return [
        dot(lhs, weight_ref[:, tap].reshape(3 * depth, weight_ref.shape[3]))
        for tap in range(3)
    ]


def halo_rows(rows_ref, top, bottom):
    def row_of(row):
        if row < 0:
            return top
        if row >= rows_ref.shape[0]:
            return bottom
        return rows_ref[row]

    return row_of


def top_and_bottom(near, far, odd, ends):
    far = jnp.where(ends, jnp.zeros_like(far), far)
    return jnp.where(odd == 1, near, far), jnp.where(odd == 1, far, near)


def column_sum(parts, cycle, height):
    at = cycle * 16
    return sum(parts[tap][at + tap : at + tap + height] for tap in range(3))


def lift(layout, x_hbm, tile_ref, code_ref, own_hbm, near_tail_hbm, far_tail_hbm, near_hbm, far_hbm,
         edges, rows, own, tails, own16, tails16, in_sems, out_sems):
    height = layout.height
    cycles, cols = x_hbm.shape[0], x_hbm.shape[2]
    upper = lax.rem(strip_of(layout.tiles), 2) * (height - 1)
    nearest = (height - 1 - upper, upper)
    pairs = [(x_hbm.at[:, :, pl.ds(first, 16)], edges.at[side]) for side, first in enumerate((0, cols - 16))]
    arriving = fetch(pairs + [(x_hbm.at[:, nearest[k]], rows.at[k]) for k in range(2)], in_sems)
    lanes = lax.broadcasted_iota(jnp.int32, (1, own.shape[1]), 1)
    noted = jnp.zeros((1, own.shape[1]), F32)
    for cycle in range(cycles):
        for side in range(2):
            other, face, side_bit, flip = seam_of(tile_ref, code_ref, layout.tiles, cycle, side)
            number = (other * FACES + face) * 4 + flip * 2 + side_bit
            noted = jnp.where(lanes == cycle * 2 + side, number.astype(F32), noted)
    tails[...] = jnp.zeros_like(tails)
    for k in range(2):
        tails[k, layout.columns : layout.columns + 1] = noted
    for side in range(2):
        arriving[side].wait()
        at = 15 * side
        for cycle in range(cycles):
            column = cycle * 2 + side
            for row in range(height):
                value = edges[side, cycle, row].astype(F32)[at : at + 1]
                own[column * height + row : column * height + row + 1] = value
            for k in range(2):
                value = edges[side, cycle, nearest[k]].astype(F32)[at : at + 1]
                tails[k, column : column + 1] = value
    own16[...] = own[...].astype(BF16)
    tails16[...] = tails[...].astype(BF16)
    pairs = [(tails16.at[0], near_tail_hbm), (tails16.at[1], far_tail_hbm)]
    pairs += [(own16, own_hbm.at[k, pl.ds(0, own16.shape[0])]) for k in range(2 * FACES)]
    for copy in arriving[2:]:
        copy.wait()
    leaving = fetch(pairs + [(rows.at[0], near_hbm), (rows.at[1], far_hbm)], out_sems)
    for copy in leaving:
        copy.wait()


def fetch(pairs, sems):
    copies = [pltpu.make_async_copy(src, dst, sems.at[k]) for k, (src, dst) in enumerate(pairs)]
    for copy in copies:
        copy.start()
    return copies


def encode(tiles, x_hbm, near_ref, far_ref, w_hbm, b_hbm, skip_hbm, pooled_hbm, near_hbm, far_hbm, pre_hbm,
           x_ref, w_ref, b_ref, stacked, skip_ref, pooled_ref, rows_ref, pre_ref, paired, in_sems, out_sems):
    cycles, height, cols, chans = x_ref.shape
    half = cols // 2
    pairs = [(b_hbm, b_ref), (x_hbm.at[0], x_ref.at[0])]
    pairs += [(w_hbm.at[:, tap], w_ref.at[tap]) for tap in range(3)]
    arriving = fetch(pairs, in_sems.at[pl.ds(0, 5)])
    strip = strip_of(tiles)
    odd = lax.rem(strip, 2)
    ends = (strip == 0) | (strip == tiles // FACES - 1)
    arriving[0].wait()
    arriving[1].wait()
    leaving = []
    for cycle in range(cycles):
        if cycle > 0:
            arriving[4 + cycle].wait()
        top, bottom = top_and_bottom(near_ref[cycle], far_ref[cycle], odd, ends)
        stack_taps(stacked, halo_rows(x_ref.at[cycle], top, bottom), height)
        for row in range(height):
            taps = []
            for tap in range(3):
                if cycle == 0 and row == 0:
                    arriving[2 + tap].wait()
                taps.append(dot(stacked[row], w_ref[tap].reshape(3 * chans, chans)))
            if cycle == 0 and row == 0:
                pairs = [(x_hbm.at[k], x_ref.at[k]) for k in range(1, cycles)]
                arriving += fetch(pairs, in_sems.at[pl.ds(5, cycles - 1)])
            total = shifted_sum(taps, cols) + b_ref[...]
            value = gelu(total).astype(BF16)
            skip_ref[cycle, row] = value
            pre_ref[cycle, 0, row : row + 1] = total[:1]
            pre_ref[cycle, 1, row : row + 1] = total[cols - 1 :]
            if row % 2 == 0:
                before = value.astype(F32)
            else:
                pair = 0.25 * (before + value.astype(F32))
                for lane in range(0, chans, 128):
                    paired[...] = pair[:, lane : lane + 128]
                    mean = paired[pl.ds(0, half, 2), :] + paired[pl.ds(1, half, 2), :]
                    pooled_ref[cycle, row // 2, :, lane : lane + 128] = mean.astype(BF16)
            if row % 4 == 3:
                rows = (cycle, pl.ds(row - 3, 4))
                leaving += fetch([(skip_ref.at[rows], skip_hbm.at[rows])], out_sems.at[cycle, pl.ds(row // 4, 1)])
        low = height // 2 - 1
        for k, at_top in ((0, odd == 1), (1, odd == 0)):
            rows_ref[k, cycle, :cols] = skip_ref[cycle, jnp.where(at_top, 0, height - 1)]
            rows_ref[k, cycle, cols : cols + half] = pooled_ref[cycle, jnp.where(at_top, 0, low)]
            rows_ref[k, cycle, cols + half :] = pooled_ref[cycle, jnp.where(at_top, 1, low - 1)]
        pairs = [(rows_ref.at[0, cycle], near_hbm.at[cycle]), (rows_ref.at[1, cycle], far_hbm.at[cycle])]
        pairs += [(pooled_ref.at[cycle], pooled_hbm.at[cycle]), (pre_ref.at[cycle], pre_hbm.at[cycle])]
        leaving += fetch(pairs, out_sems.at[cycle, pl.ds(height // 4, 4)])
    for copy in leaving:
        copy.wait()


def mend(layout, coarse, fine, recv_ref, w_hbm, skip_in, pooled_in, near_in, far_in, pre_hbm, tile_ref, code_ref,
         skip_hbm, pooled_hbm, near_hbm, far_hbm, own_hbm, near_tail_hbm, far_tail_hbm, table_hbm,
         w_ref, pre_ref, edges, pools, own, tails, own16, tails16, table_ref, in_sems, out_sems):
    tiles, height, low = layout.tiles, layout.height, coarse.height
    cycles, cols, chans = skip_in.shape[0], skip_in.shape[2], skip_in.shape[3]
    half = cols // 2
    pairs = [(w_hbm.at[:, 2 * side], w_ref.at[side]) for side in range(2)] + [(pre_hbm, pre_ref)]
    for side in range(2):
        pairs.append((skip_in.at[:, :, pl.ds((cols - 16) * side, 16)], edges.at[side]))
        pairs.append((pooled_in.at[:, :, pl.ds((half - 16) * side, 16)], pools.at[side]))
    arriving = fetch(pairs, in_sems)
    strip = strip_of(tiles)
    odd = lax.rem(strip, 2)
    row_iota = rows_iota(16) - 1
    targets = []
    for side in range(2):
        for cycle in range(cycles):
            other, face, side_bit, flip = seam_of(tile_ref, code_ref, tiles, cycle, side)
            place = layout.source(strip, flip, face, other * 2 + side_bit, row_iota)
            targets.append(jnp.where(row_iota <= height, place, -1))
    pads = pick(targets, recv_ref[...])
    noted = layout.near + layout.columns
    for member in range(2 * FACES):
        at = member * layout.payload + noted // 16 * 16
        block = recv_ref[at : at + 16, :128].astype(F32)
        table_ref[member : member + 1] = block[noted % 16 : noted % 16 + 1].astype(jnp.int32)
    part = pads.shape[0] // 2
    for copy in arriving[:3]:
        copy.wait()
    seams = [
        [dot(pads[side * part : (side + 1) * part], w_ref[side, tap]) for tap in range(3)] for side in range(2)
    ]
    iota16 = lax.broadcasted_iota(jnp.int32, (16, chans), 0)
    tails[...] = jnp.zeros_like(tails)
    for copy in arriving[3:]:
        copy.wait()
    at_top = (odd == 1, odd == 0)
    skip_at = [jnp.where(t, 0, height - 1) for t in at_top]
    pool_at = [(jnp.where(t, 0, low - 1), jnp.where(t, 1, low - 2)) for t in at_top]
    for cycle in range(cycles):
        for side in range(2):
            column = cycle * 2 + side
            at, inward = (0, 1) if side == 0 else (15, 14)
            total = gelu(pre_ref[cycle, side] + column_sum(seams[side], cycle, height))
            start = fine.own + column * height
            own[start : start + height] = total
            for row in range(height):
                block = edges[side, cycle, row].astype(F32)
                block = jnp.where(iota16 == at, total[row : row + 1], block).astype(BF16)
                edges[side, cycle, row] = block
                if row % 2 == 0:
                    before = block.astype(F32)
                else:
                    pair = before + block.astype(F32)
                    mean = 0.25 * (pair[at : at + 1] + pair[inward : inward + 1])
                    block = pools[side, cycle, row // 2].astype(F32)
                    block = jnp.where(iota16 == at, mean, block)
                    pools[side, cycle, row // 2] = block.astype(BF16)
                    for depth, place in enumerate((at, inward)):
                        start = coarse.own + (column * 2 + depth) * low + row // 2
                        own[start : start + 1] = block[place : place + 1]
            for k in range(2):
                start = fine.near - coarse.near + column
                value = edges[side, cycle, skip_at[k]].astype(F32)
                tails[k, start : start + 1] = value[at : at + 1]
                for away in range(2):
                    value = pools[side, cycle, pool_at[k][away]].astype(F32)
                    for depth, place in enumerate((at, inward)):
                        start = (column * 2 + depth) * 2 + away
                        tails[k, start : start + 1] = value[place : place + 1]
    own16[...] = own[...].astype(BF16)
    tails16[...] = tails[...].astype(BF16)
    pairs = [(tails16.at[0], near_tail_hbm), (tails16.at[1], far_tail_hbm), (table_ref, table_hbm)]
    pairs += [(own16, own_hbm.at[k, pl.ds(0, own16.shape[0])]) for k in range(2 * FACES)]
    for side in range(2):
        pairs.append((edges.at[side], skip_hbm.at[:, :, pl.ds((cols - 16) * side, 16)]))
        pairs.append((pools.at[side], pooled_hbm.at[:, :, pl.ds((half - 16) * side, 16)]))
        for k, ref in enumerate((near_hbm, far_hbm)):
            pairs.append((edges.at[side, :, skip_at[k]], ref.at[:, pl.ds((cols - 16) * side, 16)]))
            for away in range(2):
                first = cols + away * half + (half - 16) * side
                pairs.append((pools.at[side, :, pool_at[k][away]], ref.at[:, pl.ds(first, 16)]))
    leaving = fetch(pairs, out_sems)
    for copy in leaving:
        copy.wait()


def decode(tiles, skip_hbm, pooled_hbm, near_hbm, far_hbm, wm_hbm, bm_hbm, u_hbm, bu_hbm, wd_hbm, bd_hbm,
           out_hbm, edge_hbm, coarse_hbm, skip_ref, pooled_ref, near_ref, far_ref, wm_ref, bm_ref, u_ref, bu_ref,
           wd_ref, bd_ref, out_ref, edge_ref, coarse_ref, stacked_a, stacked_b, upper_a, upper_b, joined_a, joined_b,
           in_sems, out_sems):
    strips = tiles // FACES
    cycles, height, cols, chans = skip_ref.shape
    low, half = height // 2, cols // 2
    pairs = [(near_hbm, near_ref), (far_hbm, far_ref), (pooled_hbm, pooled_ref), (bm_hbm, bm_ref)]
    pairs += [(wm_hbm.at[:, tap], wm_ref.at[tap]) for tap in range(3)]
    pairs += [(bu_hbm, bu_ref), (u_hbm, u_ref), (skip_hbm.at[0], skip_ref.at[0]), (bd_hbm, bd_ref)]
    for tap in range(3):
        for part in range(2):
            source = wd_hbm.at[:, tap, pl.ds(part * chans, chans)]
            pairs.append((source, wd_ref.at[tap, pl.ds(3 * part, 3)]))
    pairs += [(skip_hbm.at[cycle], skip_ref.at[cycle]) for cycle in range(1, cycles)]
    arriving = fetch(pairs, in_sems)
    strip = strip_of(tiles)
    odd = lax.rem(strip, 2)
    first_strip, last_strip = strip == 0, strip == strips - 1
    ends = first_strip | last_strip
    place = lax.broadcasted_iota(jnp.int32, (cols, chans), 0)
    inner = (place > 1) & (place < cols - 2)
    coarse_ref[...] = jnp.zeros_like(coarse_ref)
    leaving = []
    for copy in arriving[:4]:
        copy.wait()

    def prepare(cycle):
        top, bottom = top_and_bottom(near_ref[cycle], far_ref[cycle], odd, ends)
        stacked, upper, joined = (stacked_a, upper_a, joined_a) if cycle % 2 == 0 else (stacked_b, upper_b, joined_b)

        def pooled_row(row):
            if row < -1:
                return top[cols + half :]
            if row < 0:
                return top[cols : cols + half]
            if row < low:
                return pooled_ref[cycle, row]
            if row == low:
                return bottom[cols : cols + half]
            return bottom[cols + half :]

        stack_taps(upper, lambda row: pooled_row(row - 1), low + 2)
        yield
        lhs = upper[...].reshape((low + 2) * half, 3 * chans)
        taps = []
        for tap in range(3):
            if cycle == 0:
                arriving[4 + tap].wait()
            taps.append(dot(lhs, wm_ref[tap].reshape(3 * chans, chans)))
        total = shifted_sum(taps, half) + bm_ref[...]
        yield
        coarse = []
        for row in range(low + 2):
            at = row * half
            coarse_ref[cycle, 0, row + 1 : row + 2] = total[at : at + 1]
            coarse_ref[cycle, 1, row + 1 : row + 2] = total[at + half - 1 : at + half]
            coarse.append(gelu(total[at : at + half]).astype(BF16))
        if cycle == 0:
            arriving[7].wait()
            arriving[8].wait()
        yield
        for a in range(2):
            part = jnp.concatenate(coarse[1:] if a == 0 else coarse[:-1], axis=0)
            for b in range(2):
                value = dot(part, u_ref[a, b]) + bu_ref[...]
                for k in range(low + 1):
                    at = 2 * k + 1 - a
                    for lane in range(0, chans, 128):
                        part_of = value[k * half : (k + 1) * half, lane : lane + 128]
                        joined[at, lane // 128, pl.ds(b, half, 2), :] = part_of
                yield
        arriving[9 if cycle == 0 else 16 + cycle].wait()
        skip_row = halo_rows(skip_ref.at[cycle], top[:cols], bottom[:cols])
        stack_taps(stacked.at[:, :, pl.ds(3 * chans, 3 * chans)], skip_row, height)
        for row in range(-1, height + 1):
            value = jnp.concatenate([joined[row + 1, k] for k in range(chans // 128)], axis=1)
            keep = inner
            if row < 0:
                keep = keep & jnp.logical_not(first_strip)
            if row >= height:
                keep = keep & jnp.logical_not(last_strip)
            value = jnp.where(keep, value, 0.0).astype(BF16)
            for tap in range(3):
                at = row + 1 - tap
                if 0 <= at < height:
                    stacked[at, :, tap * chans : (tap + 1) * chans] = value
            if row % 5 == 3:
                yield

    def convolve(cycle):
        stacked = stacked_a if cycle % 2 == 0 else stacked_b
        for row in range(height):
            taps = []
            for tap in range(3):
                if cycle == 0 and row == 0:
                    for k in range(10 if tap == 0 else 11 + 2 * tap, 13 + 2 * tap):
                        arriving[k].wait()
                taps.append(dot(stacked[row], wd_ref[tap].reshape(6 * chans, chans)))
            total = shifted_sum(taps, cols) + bd_ref[...]
            out_ref[cycle, row] = total.astype(BF16)
            edge_ref[cycle, 0, row] = total[:16]
            edge_ref[cycle, 1, row] = total[cols - 16 :]
            copies = []
            if row % 4 == 3:
                rows = (cycle, pl.ds(row - 3, 4))
                copies = [(out_ref.at[rows], out_hbm.at[rows])]
            if row == height - 1:
                copies.append((edge_ref.at[cycle], edge_hbm.at[cycle]))
            yield fetch(copies, out_sems.at[cycle, pl.ds(row // 4, len(copies))]) if copies else []

    for _ in prepare(0):
        pass
    for cycle in range(cycles):
        ahead = prepare(cycle + 1) if cycle + 1 < cycles else iter(())
        for copies in convolve(cycle):
            leaving += copies
            next(ahead, None)
            next(ahead, None)
        for _ in ahead:
            pass
    leaving += fetch([(coarse_ref, coarse_hbm)], out_sems.at[cycles, pl.ds(0, 1)])
    for copy in leaving:
        copy.wait()


def seal(coarse_at, fine_at, tab_ref, tile_ref, code_ref, recv_hbm, coarse_hbm, edge_hbm, wm_hbm, bm_hbm, u_hbm,
         bu_hbm, wd_hbm, out_in, out_hbm, recv_ref, coarse_ref, edge_ref, wm_ref, bm_ref, u_ref, bu_ref, wu_ref, ws_ref, out_ref,
         in_sems, out_sems):
    tiles, strips, height = coarse_at.tiles, coarse_at.strips, fine_at.height
    cycles, _, _, _, chans = edge_ref.shape
    cols = out_hbm.shape[2]
    low = height // 2
    pairs = [(recv_hbm, recv_ref), (bm_hbm, bm_ref), (bu_hbm, bu_ref), (coarse_hbm, coarse_ref), (wm_hbm, wm_ref), (u_hbm, u_ref)]
    pairs += [(wd_hbm.at[:, :, pl.ds(0, chans)], wu_ref), (edge_hbm, edge_ref)]
    pairs += [(wd_hbm.at[:, 2 * side, pl.ds(chans, chans)], ws_ref.at[side]) for side in range(2)]
    arriving = fetch(pairs, in_sems)
    strip = strip_of(tiles)
    rows8 = rows_iota(8) - 2
    rows16 = rows_iota(16) - 1
    aligned, taps, skips, sides, flips, strips_at = [], [[], [], []], [], [], [], []
    for side in range(2):
        for cycle in range(cycles):
            other, face, side_bit, flip = seam_of(tile_ref, code_ref, tiles, cycle, side)
            column = other * 2 + side_bit
            aligned.append(coarse_at.source(strip, flip, face, column * 2, rows8))
            place = fine_at.source(strip, flip, face, column, rows16)
            skips.append(jnp.where(rows16 <= height, place, -1))
            there = jnp.where(flip == 1, strips - 1 - strip, strip)
            number = tab_ref[face * 2, column]
            beyond = lax.div(number, 4)
            code = lax.rem(number, 4)
            other2, face2 = lax.div(beyond, FACES), lax.rem(beyond, FACES)
            column2 = other2 * 2 + lax.rem(code, 2)
            pad = coarse_at.source(there, lax.div(code, 2), face2, column2 * 2, rows8)
            edge = coarse_at.source(there, 0, face, column * 2, rows8)
            inner = coarse_at.source(there, 0, face, column * 2 + 1, rows8)
            taps[0].append(jnp.where(side_bit == 0, pad, inner))
            taps[1].append(edge)
            taps[2].append(jnp.where(side_bit == 0, inner, pad))
            sides.append(side_bit)
            flips.append(flip)
            strips_at.append(there)
    arriving[0].wait()
    got = pick(aligned + taps[0] + taps[1] + taps[2] + skips, recv_ref[...])
    n = 8 * 2 * cycles
    at8 = lax.broadcasted_iota(jnp.int32, (8, chans), 0) - 2

    def on_face(s):
        return jnp.where(((at8 < 0) & (s == 0)) | ((at8 >= low) & (s == strips - 1)), 0.0, 1.0)

    for copy in arriving[1:5]:
        copy.wait()
    own = got[:n]
    there = got[n : 4 * n]
    rows = []
    for row in range(3):
        here = [dot(own[side * n // 2 : (side + 1) * n // 2], wm_ref[row, 2 * side]) for side in range(2)]
        away = sum(dot(there[tap * n : (tap + 1) * n], wm_ref[row, tap]) for tap in range(3))
        rows.append(jnp.concatenate(here + [away], axis=0))
    total = pltpu.roll(rows[0], 1, 0) + rows[1] + pltpu.roll(rows[2], 2 * n - 1, 0)
    mine = [
        total[(side * cycles + cycle) * 8 : (side * cycles + cycle + 1) * 8] + coarse_ref[cycle, side]
        for side in range(2)
        for cycle in range(cycles)
    ]
    total = jnp.concatenate(mine + [total[n:] + bm_ref[...]], axis=0)
    keep = jnp.concatenate([on_face(s) for s in [strip] * (2 * cycles) + strips_at], axis=0)
    column = (gelu(total) * keep).astype(BF16)
    arriving[5].wait()
    phases = [
        [((dot(column, u_ref[a, b]) + bu_ref[...]) * keep).astype(BF16) for b in range(2)] for a in range(2)
    ]
    right = jnp.concatenate([jnp.where(at8 > -99, b, 0) for b in sides], axis=0) == 1
    place = lax.shift_right_arithmetic(rows16 - (rows16 & 1), 1) + 2
    fine_own = [jnp.where(rows16 <= height, (rows16 & 1) * n + k * 8 + place, -1) for k in range(2 * cycles)]
    fine_there = []
    for k in range(2 * cycles):
        fine = jnp.where(flips[k] == 1, height - 1 - rows16, rows16)
        a = fine & 1
        place = a * n + k * 8 + lax.shift_right_arithmetic(fine - a, 1) + 2
        fine_there.append(jnp.where(rows16 <= height, place, -1))
    beyond = [jnp.where(right, phases[a][1][n:], phases[a][0][n:]) for a in range(2)]
    outer = pick(fine_there, jnp.concatenate(beyond, axis=0))
    inside = [pick(fine_own, jnp.concatenate([phases[a][b][:n] for a in range(2)], axis=0)) for b in range(2)]
    skip_pad = got[4 * n :]
    m = 16 * cycles
    lines = [[outer[:m], inside[0][:m], inside[1][:m]], [outer[m:], inside[1][m:], inside[0][m:]]]
    for copy in arriving[6:]:
        copy.wait()
    sums = [[[], [], []], [[], [], []]]
    for row in range(3):
        found = [[0.0, 0.0, 0.0], [0.0, 0.0, 0.0]]
        for tap in range(3):
            uses = []
            for side in range(2):
                offset = tap if side == 0 else 2 - tap
                uses += [(side, line, line - offset) for line in range(3) if line >= offset]
            value = dot(jnp.concatenate([lines[side][line] for side, line, _ in uses], axis=0), wu_ref[row, tap])
            for k, (side, _, into) in enumerate(uses):
                found[side][into] = found[side][into] + value[k * m : (k + 1) * m]
        for side in range(2):
            found[side][0] = found[side][0] + dot(skip_pad[side * m : (side + 1) * m], ws_ref[side, row])
            for into in range(3):
                sums[side][into].append(found[side][into])
    iota16 = lax.broadcasted_iota(jnp.int32, (16, chans), 0)
    for side in range(2):
        for cycle in range(cycles):
            extra = [column_sum(sums[side][into], cycle, height) for into in range(3)]
            for row in range(height):
                value = edge_ref[cycle, side, row]
                for into in range(3):
                    at = into if side == 0 else 15 - into
                    value = value + jnp.where(iota16 == at, extra[into][row : row + 1], 0.0)
                out_ref[side, cycle, row] = value.astype(BF16)
    leaving = fetch(
        [(out_ref.at[side], out_hbm.at[:, :, pl.ds((cols - 16) * side, 16)]) for side in range(2)], out_sems
    )
    for copy in leaving:
        copy.wait()


def on_device(tiles, fields, seam_tile, seam_code, encoder_weight, encoder_bias, middle_weight,
              middle_bias, upconv_weight, upconv_bias, decoder_weight, decoder_offset_bias):
    cycles, height, cols, chans = fields.shape
    low, half = height // 2, cols // 2
    strips = tiles // FACES
    joint = strips == 4

    def strip(t):
        return (t + strips // 2) % strips

    near_pairs, far_pairs = [], []
    for t in range(tiles):
        pairs = near_pairs if strip(t) % 2 == 0 else far_pairs
        after = (t + 1) % tiles
        pairs += [(t, after), (after, t)]

    def tile_at(face, s):
        return (face * strips + s - strips // 2) % tiles

    groups = [
        [tile_at(face, s) for face in range(FACES) for s in (k, strips - 1 - k)]
        for k in range(strips // 2)
    ]
    members = 2 * FACES

    def share(x):
        return lax.all_to_all(x, "tile", 0, 0, tiled=True, axis_index_groups=groups)

    columns = 2 * cycles
    tail1 = (columns + 1 + 15) // 16 * 16
    spec = Layout(tiles, height, 1, columns, 0, columns * height, tail1)
    own2 = 2 * columns * low + columns * height
    tail2 = (4 * columns + columns + 15) // 16 * 16
    coarse_at = Layout(tiles, low, 2, 2 * columns, 0, own2, tail2)
    fine_at = Layout(tiles, height, 1, columns, 2 * columns * low, own2 + 4 * columns, tail2)
    halos = 1 if joint else 2
    spec.payload = columns * height + halos * tail1
    payload = own2 + halos * tail2
    coarse_at.payload = fine_at.payload = payload

    def to_near(x):
        return lax.ppermute(x, "tile", near_pairs)

    def to_far(x):
        return lax.ppermute(x, "tile", far_pairs)

    def pack(own, near_tail, far_tail):
        tails = [to_near(near_tail)] + ([] if joint else [to_far(far_tail)])
        rows = own.shape[1] - sum(tail.shape[0] for tail in tails)
        for tail in tails:
            tail = jnp.broadcast_to(tail[None], (members,) + tail.shape)
            own = lax.dynamic_update_slice(own, tail, (0, rows, 0))
            rows += tail.shape[1]
        return share(own)

    seams = (jnp.transpose(seam_tile, (1, 2, 0)), jnp.transpose(seam_code, (1, 2, 0)))
    eb, mb, ub, db = (b.reshape(1, chans) for b in (encoder_bias, middle_bias, upconv_bias, decoder_offset_bias))

    hbm = pl.BlockSpec(memory_space=pltpu.HBM)
    vmem = pl.BlockSpec(memory_space=pltpu.VMEM)
    smem = pl.BlockSpec(memory_space=pltpu.SMEM)
    dma = pltpu.SemaphoreType.DMA
    tall = (cycles, height, cols, chans)
    row_shape = (cycles, cols, chans)
    wide = (cycles, 2 * cols, chans)
    square = (chans, chans)
    wshape = (3, 3) + square
    pooled_shape = (cycles, low, half, chans)
    edge_shape = (2, cycles, height, 16, chans)

    def call(body, name, outs, in_specs, out_specs, scratch, *args, **options):
        return pl.pallas_call(
            body,
            out_shape=[jax.ShapeDtypeStruct(shape, dtype) for shape, dtype in outs],
            in_specs=in_specs,
            out_specs=out_specs,
            scratch_shapes=[pltpu.VMEM(*x) if isinstance(x, tuple) else x for x in scratch],
            compiler_params=pltpu.CompilerParams(vmem_limit_bytes=56 * MIB),
            name=name,
            **options,
        )(*args)

    far_cost = pl.CostEstimate(flops=10**12, bytes_accessed=10**9, transcendentals=0)
    vector = (1, chans)
    own, near_tail, far_tail, near, far = call(
        functools.partial(lift, spec), "lift",
        [((members, spec.payload, chans), BF16)] + [((tail1, chans), BF16)] * 2 + [(row_shape, BF16)] * 2,
        [hbm, smem, smem], [hbm] * 5,
        [(edge_shape, BF16), ((2,) + row_shape, BF16), ((columns * height, chans), F32), ((2, tail1, chans), F32),
         ((columns * height, chans), BF16), ((2, tail1, chans), BF16), dma((4,)), dma((4 + members,))],
        fields, *seams,
    )
    recv = pack(own, near_tail, far_tail)
    near, far = to_near(near), to_far(far)
    pre_shape = (cycles, 2, height, chans)
    skip, pooled, near, far, pre_col = call(
        functools.partial(encode, tiles), "encode",
        [(tall, BF16), (pooled_shape, BF16), (wide, BF16), (wide, BF16), (pre_shape, F32)],
        [hbm, vmem, vmem, hbm, hbm], [hbm] * 5,
        [(tall, BF16), (wshape, BF16), (vector, F32), ((height, cols, 3 * chans), BF16), (tall, BF16),
         (pooled_shape, BF16), ((2,) + wide, BF16), (pre_shape, F32), ((cols, 128), F32),
         dma((4 + cycles,)), dma((cycles, height // 4 + 4))],
        fields, near, far, encoder_weight, eb,
        cost_estimate=far_cost,
    )
    pool_edges = (2, cycles, low, 16, chans)
    skip, pooled, near, far, own, near_tail, far_tail, table = call(
        functools.partial(mend, spec, coarse_at, fine_at), "mend",
        [(tall, BF16), (pooled_shape, BF16), (wide, BF16), (wide, BF16), ((members, payload, chans), BF16)]
        + [((tail2, chans), BF16)] * 2 + [((members, 128), jnp.int32)],
        [vmem] + [hbm] * 6 + [smem, smem], [hbm] * 8,
        [((2, 3) + square, BF16), (pre_shape, F32), (edge_shape, BF16), (pool_edges, BF16), ((own2, chans), F32),
         ((2, tail2, chans), F32), ((own2, chans), BF16), ((2, tail2, chans), BF16), ((members, 128), jnp.int32),
         dma((7,)), dma((19 + members,))],
        recv.reshape(-1, chans), encoder_weight, skip, pooled, near, far, pre_col, *seams,
        input_output_aliases={2: 0, 3: 1, 4: 2, 5: 3},
    )
    recv2 = pack(own, near_tail, far_tail)
    near2, far2 = to_near(near), to_far(far)
    edges = (cycles, 2, height, 16, chans)
    coarse_edges = (cycles, 2, 8, chans)
    out, edge, coarse = call(
        functools.partial(decode, tiles), "decode",
        [(tall, BF16), (edges, F32), (coarse_edges, F32)],
        [hbm] * 10, [hbm, hbm, hbm],
        [(tall, BF16), (pooled_shape, BF16), (wide, BF16), (wide, BF16), (wshape, BF16), (vector, F32),
         ((2, 2) + square, BF16), (vector, F32), ((3, 6) + square, BF16), (vector, F32), (tall, BF16), (edges, F32),
         (coarse_edges, F32)]
        + [((height, cols, 6 * chans), BF16)] * 2 + [((low + 2, half, 3 * chans), BF16)] * 2
        + [((height + 2, chans // 128, cols, 128), F32)] * 2
        + [dma((16 + cycles,)), dma((cycles + 1, height // 4 + 1))],
        skip, pooled, near2, far2, middle_weight, mb, upconv_weight, ub, decoder_weight, db,
        cost_estimate=far_cost,
    )
    (out,) = call(
        functools.partial(seal, coarse_at, fine_at), "seal",
        [(tall, BF16)],
        [smem, smem, smem] + [hbm] * 9, [hbm],
        [((members * payload, chans), BF16), (coarse_edges, F32), (edges, F32), (wshape, BF16), (vector, F32), ((2, 2) + square, BF16), (vector, F32),
         (wshape, BF16), ((2, 3) + square, BF16), (edge_shape, BF16), dma((10,)), dma((2,))],
        table, *seams, recv2.reshape(-1, chans), coarse, edge, middle_weight, mb, upconv_weight, ub, decoder_weight, out,
        input_output_aliases={11: 0},
    )
    return out


def solution(mesh):
    return jax.shard_map(
        functools.partial(on_device, mesh.shape["tile"]),
        mesh=mesh,
        in_specs=(P("grp", "tile", None, None), P(None, "tile", None), P(None, "tile", None)) + (P(),) * 8,
        out_specs=P("grp", "tile", None, None),
        check_vma=False,
    )
```

```python
import functools

import jax
import jax.numpy as jnp
from jax import lax
from jax.experimental import pallas as pl
from jax.experimental.pallas import tpu as pltpu
from jax.sharding import PartitionSpec as P

F32 = jnp.float32
BF16 = jnp.bfloat16
FACES = 4
MIB = 1 << 20


def dot(a, b):
    return jnp.dot(a, b, preferred_element_type=F32)


def gelu(x):
    return 0.5 * x * (1.0 + jnp.tanh(0.7978845608 * (x + 0.044715 * x * x * x)))


def rows_iota(n):
    return lax.broadcasted_iota(jnp.int32, (n, 1), 0)


class Layout:
    def __init__(self, tiles, height, depth, columns, own, near, tail):
        self.tiles = tiles
        self.strips = tiles // FACES
        self.joint = self.strips == 4
        self.height = height
        self.depth = depth
        self.columns = columns
        self.own = own
        self.near = near
        self.far = near + tail
        self.payload = 0

    def source(self, strip, flip, face, column, row):
        height, last = self.height, self.strips - 1
        strip = jnp.where(flip == 1, last - strip, strip)
        row = jnp.where(flip == 1, height - 1 - row, row)
        upper = jnp.where(strip >= self.strips // 2, 1, 0)
        odd = lax.rem(strip, 2)
        above = row < 0
        below = row >= height
        away = jnp.where(above, -row, row - (height - 1)) - 1
        near = (above & (odd == 1)) | (below & (odd == 0))
        missing = (above & (strip == 0)) | (below & (strip == last))
        member = (face * 2 + upper) * self.payload
        inside = member + self.own + column * height + row
        beside = member + self.near + column * self.depth + away
        if self.joint:
            across = (face * 2 + 1 - upper) * self.payload + self.own + column * height
            far = across + jnp.where(above, height - 1 - away, away)
        else:
            far = member + self.far + column * self.depth + away
        place = jnp.where(above | below, jnp.where(near, beside, far), inside)
        return jnp.where(missing, -1, place)


def strip_of(tiles):
    strips = tiles // FACES
    return lax.rem(lax.axis_index("tile") + strips // 2, strips)


def seam_of(tile_ref, code_ref, tiles, cycle, side):
    strips = tiles // FACES
    partner = tile_ref[0, side, cycle]
    code = code_ref[0, side, cycle]
    other = lax.div(partner, tiles)
    place = partner - other * tiles + strips // 2
    face = lax.rem(lax.div(place, strips), FACES)
    return other, face, lax.rem(code, 2), lax.div(code, 2)


def pick(targets, table):
    wanted = jnp.concatenate(targets, axis=0)
    shape = (wanted.shape[0], table.shape[0])
    lanes = lax.broadcasted_iota(jnp.int32, shape, 1)
    chooser = jnp.where(lanes == wanted, 1.0, 0.0).astype(BF16)
    return dot(chooser, table).astype(BF16)


def shifted_sum(taps, cols):
    left, middle, right = taps
    n = middle.shape[0]
    place = lax.broadcasted_iota(jnp.int32, middle.shape, 0) & (cols - 1)
    left = jnp.where(place == 0, 0.0, pltpu.roll(left, 1, 0))
    right = jnp.where(place == cols - 1, 0.0, pltpu.roll(right, n - 1, 0))
    return middle + left + right


def stack_taps(stacked, row_of, rows):
    depth = stacked.shape[-1] // 3
    for row in range(-1, rows + 1):
        value = row_of(row)
        for tap in range(3):
            at = row + 1 - tap
            if 0 <= at < rows:
                stacked[at, :, tap * depth : (tap + 1) * depth] = value


def column_taps(lhs, weight_ref):
    depth = weight_ref.shape[2]
    return [
        dot(lhs, weight_ref[:, tap].reshape(3 * depth, weight_ref.shape[3]))
        for tap in range(3)
    ]


def halo_rows(rows_ref, top, bottom):
    def row_of(row):
        if row < 0:
            return top
        if row >= rows_ref.shape[0]:
            return bottom
        return rows_ref[row]

    return row_of


def top_and_bottom(near, far, odd, ends):
    far = jnp.where(ends, jnp.zeros_like(far), far)
    return jnp.where(odd == 1, near, far), jnp.where(odd == 1, far, near)


def column_sum(parts, cycle, height):
    at = cycle * 16
    return sum(parts[tap][at + tap : at + tap + height] for tap in range(3))


def lift(layout, x_hbm, tile_hbm, code_hbm, own_hbm, near_tail_hbm, far_tail_hbm, near_hbm, far_hbm,
         edges, rows, own, tails, own16, tails16, tile_ref, code_ref, in_sems, out_sems):
    height = layout.height
    cycles, cols = x_hbm.shape[0], x_hbm.shape[2]
    upper = lax.rem(strip_of(layout.tiles), 2) * (height - 1)
    nearest = (height - 1 - upper, upper)
    pairs = [(x_hbm.at[:, :, pl.ds(first, 16)], edges.at[side]) for side, first in enumerate((0, cols - 16))]
    pairs += [(x_hbm.at[:, nearest[k]], rows.at[k]) for k in range(2)]
    arriving = fetch(pairs + [(tile_hbm, tile_ref), (code_hbm, code_ref)], in_sems)
    tails[...] = jnp.zeros_like(tails)
    for side in range(2):
        arriving[side].wait()
        at = 15 * side
        for cycle in range(cycles):
            column = cycle * 2 + side
            for row in range(height):
                value = edges[side, cycle, row].astype(F32)[at : at + 1]
                own[column * height + row : column * height + row + 1] = value
            for k in range(2):
                value = edges[side, cycle, nearest[k]].astype(F32)[at : at + 1]
                tails[k, column : column + 1] = value
    for copy in arriving[4:]:
        copy.wait()
    lanes = lax.broadcasted_iota(jnp.int32, (1, own.shape[1]), 1)
    noted = jnp.zeros((1, own.shape[1]), F32)
    for cycle in range(cycles):
        for side in range(2):
            other, face, side_bit, flip = seam_of(tile_ref, code_ref, layout.tiles, cycle, side)
            number = (other * FACES + face) * 4 + flip * 2 + side_bit
            noted = jnp.where(lanes == cycle * 2 + side, number.astype(F32), noted)
    for k in range(2):
        tails[k, layout.columns : layout.columns + 1] = noted
    own16[...] = own[...].astype(BF16)
    tails16[...] = tails[...].astype(BF16)
    pairs = [(tails16.at[0], near_tail_hbm), (tails16.at[1], far_tail_hbm)]
    pairs += [(own16, own_hbm.at[k, pl.ds(0, own16.shape[0])]) for k in range(2 * FACES)]
    for copy in arriving[2:4]:
        copy.wait()
    leaving = fetch(pairs + [(rows.at[0], near_hbm), (rows.at[1], far_hbm)], out_sems)
    for copy in leaving:
        copy.wait()


def fetch(pairs, sems):
    copies = [pltpu.make_async_copy(src, dst, sems.at[k]) for k, (src, dst) in enumerate(pairs)]
    for copy in copies:
        copy.start()
    return copies


def encode(tiles, x_hbm, near_in, far_in, w_hbm, b_hbm, skip_hbm, pooled_hbm, near_hbm, far_hbm, pre_hbm,
           x_ref, near_ref, far_ref, w_ref, b_ref, stacked, skip_ref, pooled_ref, rows_ref, pre_ref, paired, in_sems, out_sems):
    cycles, height, cols, chans = x_ref.shape
    half = cols // 2
    pairs = [(x_hbm.at[0], x_ref.at[0]), (near_in, near_ref), (far_in, far_ref), (b_hbm, b_ref)]
    pairs += [(w_hbm.at[:, tap], w_ref.at[tap]) for tap in range(3)]
    arriving = fetch(pairs, in_sems.at[pl.ds(0, 7)])
    strip = strip_of(tiles)
    odd = lax.rem(strip, 2)
    ends = (strip == 0) | (strip == tiles // FACES - 1)
    for copy in arriving[:4]:
        copy.wait()
    leaving = []
    for cycle in range(cycles):
        if cycle > 0:
            arriving[6 + cycle].wait()
        top, bottom = top_and_bottom(near_ref[cycle], far_ref[cycle], odd, ends)
        stack_taps(stacked, halo_rows(x_ref.at[cycle], top, bottom), height)
        for row in range(height):
            taps = []
            for tap in range(3):
                if cycle == 0 and row == 0:
                    arriving[4 + tap].wait()
                taps.append(dot(stacked[row], w_ref[tap].reshape(3 * chans, chans)))
            if cycle == 0 and row == 0:
                pairs = [(x_hbm.at[k], x_ref.at[k]) for k in range(1, cycles)]
                arriving += fetch(pairs, in_sems.at[pl.ds(7, cycles - 1)])
            total = shifted_sum(taps, cols) + b_ref[...]
            value = gelu(total).astype(BF16)
            skip_ref[cycle, row] = value
            pre_ref[cycle, 0, row : row + 1] = total[:1]
            pre_ref[cycle, 1, row : row + 1] = total[cols - 1 :]
            if row % 2 == 0:
                before = value.astype(F32)
            else:
                pair = 0.25 * (before + value.astype(F32))
                for lane in range(0, chans, 128):
                    paired[...] = pair[:, lane : lane + 128]
                    mean = paired[pl.ds(0, half, 2), :] + paired[pl.ds(1, half, 2), :]
                    pooled_ref[cycle, row // 2, :, lane : lane + 128] = mean.astype(BF16)
            if row % 4 == 3:
                rows = (cycle, pl.ds(row - 3, 4))
                leaving += fetch([(skip_ref.at[rows], skip_hbm.at[rows])], out_sems.at[cycle, pl.ds(row // 4, 1)])
        low = height // 2 - 1
        for k, at_top in ((0, odd == 1), (1, odd == 0)):
            rows_ref[k, cycle, :cols] = skip_ref[cycle, jnp.where(at_top, 0, height - 1)]
            rows_ref[k, cycle, cols : cols + half] = pooled_ref[cycle, jnp.where(at_top, 0, low)]
            rows_ref[k, cycle, cols + half :] = pooled_ref[cycle, jnp.where(at_top, 1, low - 1)]
        pairs = [(rows_ref.at[0, cycle], near_hbm.at[cycle]), (rows_ref.at[1, cycle], far_hbm.at[cycle])]
        pairs += [(pooled_ref.at[cycle], pooled_hbm.at[cycle]), (pre_ref.at[cycle], pre_hbm.at[cycle])]
        leaving += fetch(pairs, out_sems.at[cycle, pl.ds(height // 4, 4)])
    for copy in leaving:
        copy.wait()


def mend(layout, coarse, fine, recv_ref, w_hbm, skip_in, pooled_in, near_in, far_in, pre_hbm, tile_hbm, code_hbm,
         skip_hbm, pooled_hbm, near_hbm, far_hbm, own_hbm, near_tail_hbm, far_tail_hbm, table_hbm,
         w_ref, pre_ref, edges, pools, own, tails, own16, tails16, table_ref, tile_ref, code_ref, in_sems, out_sems):
    tiles, height, low = layout.tiles, layout.height, coarse.height
    cycles, cols, chans = skip_in.shape[0], skip_in.shape[2], skip_in.shape[3]
    half = cols // 2
    pairs = [(tile_hbm, tile_ref), (code_hbm, code_ref)]
    pairs += [(w_hbm.at[:, 2 * side], w_ref.at[side]) for side in range(2)] + [(pre_hbm, pre_ref)]
    for side in range(2):
        pairs.append((skip_in.at[:, :, pl.ds((cols - 16) * side, 16)], edges.at[side]))
        pairs.append((pooled_in.at[:, :, pl.ds((half - 16) * side, 16)], pools.at[side]))
    arriving = fetch(pairs, in_sems)
    strip = strip_of(tiles)
    odd = lax.rem(strip, 2)
    row_iota = rows_iota(16) - 1
    targets = []
    for copy in arriving[:2]:
        copy.wait()
    for side in range(2):
        for cycle in range(cycles):
            other, face, side_bit, flip = seam_of(tile_ref, code_ref, tiles, cycle, side)
            place = layout.source(strip, flip, face, other * 2 + side_bit, row_iota)
            targets.append(jnp.where(row_iota <= height, place, -1))
    pads = pick(targets, recv_ref[...])
    noted = layout.near + layout.columns
    for member in range(2 * FACES):
        at = member * layout.payload + noted // 16 * 16
        block = recv_ref[at : at + 16, :128].astype(F32)
        table_ref[member : member + 1] = block[noted % 16 : noted % 16 + 1].astype(jnp.int32)
    part = pads.shape[0] // 2
    for copy in arriving[2:5]:
        copy.wait()
    seams = [
        [dot(pads[side * part : (side + 1) * part], w_ref[side, tap]) for tap in range(3)] for side in range(2)
    ]
    iota16 = lax.broadcasted_iota(jnp.int32, (16, chans), 0)
    tails[...] = jnp.zeros_like(tails)
    for copy in arriving[5:]:
        copy.wait()
    at_top = (odd == 1, odd == 0)
    skip_at = [jnp.where(t, 0, height - 1) for t in at_top]
    pool_at = [(jnp.where(t, 0, low - 1), jnp.where(t, 1, low - 2)) for t in at_top]
    for cycle in range(cycles):
        for side in range(2):
            column = cycle * 2 + side
            at, inward = (0, 1) if side == 0 else (15, 14)
            total = gelu(pre_ref[cycle, side] + column_sum(seams[side], cycle, height))
            start = fine.own + column * height
            own[start : start + height] = total
            for row in range(height):
                block = edges[side, cycle, row].astype(F32)
                block = jnp.where(iota16 == at, total[row : row + 1], block).astype(BF16)
                edges[side, cycle, row] = block
                if row % 2 == 0:
                    before = block.astype(F32)
                else:
                    pair = before + block.astype(F32)
                    mean = 0.25 * (pair[at : at + 1] + pair[inward : inward + 1])
                    block = pools[side, cycle, row // 2].astype(F32)
                    block = jnp.where(iota16 == at, mean, block)
                    pools[side, cycle, row // 2] = block.astype(BF16)
                    for depth, place in enumerate((at, inward)):
                        start = coarse.own + (column * 2 + depth) * low + row // 2
                        own[start : start + 1] = block[place : place + 1]
            for k in range(2):
                start = fine.near - coarse.near + column
                value = edges[side, cycle, skip_at[k]].astype(F32)
                tails[k, start : start + 1] = value[at : at + 1]
                for away in range(2):
                    value = pools[side, cycle, pool_at[k][away]].astype(F32)
                    for depth, place in enumerate((at, inward)):
                        start = (column * 2 + depth) * 2 + away
                        tails[k, start : start + 1] = value[place : place + 1]
    own16[...] = own[...].astype(BF16)
    tails16[...] = tails[...].astype(BF16)
    pairs = [(tails16.at[0], near_tail_hbm), (tails16.at[1], far_tail_hbm), (table_ref, table_hbm)]
    pairs += [(own16, own_hbm.at[k, pl.ds(0, own16.shape[0])]) for k in range(2 * FACES)]
    for side in range(2):
        pairs.append((edges.at[side], skip_hbm.at[:, :, pl.ds((cols - 16) * side, 16)]))
        pairs.append((pools.at[side], pooled_hbm.at[:, :, pl.ds((half - 16) * side, 16)]))
        for k, ref in enumerate((near_hbm, far_hbm)):
            pairs.append((edges.at[side, :, skip_at[k]], ref.at[:, pl.ds((cols - 16) * side, 16)]))
            for away in range(2):
                first = cols + away * half + (half - 16) * side
                pairs.append((pools.at[side, :, pool_at[k][away]], ref.at[:, pl.ds(first, 16)]))
    leaving = fetch(pairs, out_sems)
    for copy in leaving:
        copy.wait()


def decode(tiles, skip_hbm, pooled_hbm, near_hbm, far_hbm, wm_hbm, bm_hbm, u_hbm, bu_hbm, wd_hbm, bd_hbm,
           out_hbm, edge_hbm, coarse_hbm, skip_ref, pooled_ref, near_ref, far_ref, wm_ref, bm_ref, u_ref, bu_ref,
           wd_ref, bd_ref, out_ref, edge_ref, coarse_ref, stacked_a, stacked_b, upper_a, upper_b, joined_a, joined_b,
           in_sems, out_sems):
    strips = tiles // FACES
    cycles, height, cols, chans = skip_ref.shape
    low, half = height // 2, cols // 2
    halos = ((near_hbm, near_ref), (far_hbm, far_ref), (pooled_hbm, pooled_ref))
    pairs = [(src.at[0], dst.at[0]) for src, dst in halos] + [(bm_hbm, bm_ref)]
    pairs += [(wm_hbm.at[:, tap], wm_ref.at[tap]) for tap in range(3)]
    pairs += [(bu_hbm, bu_ref), (u_hbm, u_ref), (skip_hbm.at[0], skip_ref.at[0]), (bd_hbm, bd_ref)]
    for tap in range(3):
        for part in range(2):
            source = wd_hbm.at[:, tap, pl.ds(part * chans, chans)]
            pairs.append((source, wd_ref.at[tap, pl.ds(3 * part, 3)]))
    pairs += [(skip_hbm.at[cycle], skip_ref.at[cycle]) for cycle in range(1, cycles)]
    rest = pl.ds(1, cycles - 1)
    pairs += [(src.at[rest], dst.at[rest]) for src, dst in halos]
    arriving = fetch(pairs, in_sems)
    strip = strip_of(tiles)
    odd = lax.rem(strip, 2)
    first_strip, last_strip = strip == 0, strip == strips - 1
    ends = first_strip | last_strip
    place = lax.broadcasted_iota(jnp.int32, (cols, chans), 0)
    inner = (place > 1) & (place < cols - 2)
    coarse_ref[...] = jnp.zeros_like(coarse_ref)
    leaving = []
    for copy in arriving[:4]:
        copy.wait()

    def prepare(cycle):
        if cycle == 1:
            for copy in arriving[16 + cycles :]:
                copy.wait()
        top, bottom = top_and_bottom(near_ref[cycle], far_ref[cycle], odd, ends)
        stacked, upper, joined = (stacked_a, upper_a, joined_a) if cycle % 2 == 0 else (stacked_b, upper_b, joined_b)

        def pooled_row(row):
            if row < -1:
                return top[cols + half :]
            if row < 0:
                return top[cols : cols + half]
            if row < low:
                return pooled_ref[cycle, row]
            if row == low:
                return bottom[cols : cols + half]
            return bottom[cols + half :]

        stack_taps(upper, lambda row: pooled_row(row - 1), low + 2)
        yield
        lhs = upper[...].reshape((low + 2) * half, 3 * chans)
        taps = []
        for tap in range(3):
            if cycle == 0:
                arriving[4 + tap].wait()
            taps.append(dot(lhs, wm_ref[tap].reshape(3 * chans, chans)))
        total = shifted_sum(taps, half) + bm_ref[...]
        yield
        coarse = []
        for row in range(low + 2):
            at = row * half
            coarse_ref[cycle, 0, row + 1 : row + 2] = total[at : at + 1]
            coarse_ref[cycle, 1, row + 1 : row + 2] = total[at + half - 1 : at + half]
            coarse.append(gelu(total[at : at + half]).astype(BF16))
        if cycle == 0:
            arriving[7].wait()
            arriving[8].wait()
        yield
        for a in range(2):
            part = jnp.concatenate(coarse[1:] if a == 0 else coarse[:-1], axis=0)
            for b in range(2):
                value = dot(part, u_ref[a, b]) + bu_ref[...]
                for k in range(low + 1):
                    at = 2 * k + 1 - a
                    for lane in range(0, chans, 128):
                        part_of = value[k * half : (k + 1) * half, lane : lane + 128]
                        joined[at, lane // 128, pl.ds(b, half, 2), :] = part_of
                yield
        arriving[9 if cycle == 0 else 16 + cycle].wait()
        skip_row = halo_rows(skip_ref.at[cycle], top[:cols], bottom[:cols])
        stack_taps(stacked.at[:, :, pl.ds(3 * chans, 3 * chans)], skip_row, height)
        for row in range(-1, height + 1):
            value = jnp.concatenate([joined[row + 1, k] for k in range(chans // 128)], axis=1)
            keep = inner
            if row < 0:
                keep = keep & jnp.logical_not(first_strip)
            if row >= height:
                keep = keep & jnp.logical_not(last_strip)
            value = jnp.where(keep, value, 0.0).astype(BF16)
            for tap in range(3):
                at = row + 1 - tap
                if 0 <= at < height:
                    stacked[at, :, tap * chans : (tap + 1) * chans] = value
            if row % 5 == 3:
                yield

    def convolve(cycle):
        stacked = stacked_a if cycle % 2 == 0 else stacked_b
        for row in range(height):
            taps = []
            for tap in range(3):
                if cycle == 0 and row == 0:
                    for k in range(10 if tap == 0 else 11 + 2 * tap, 13 + 2 * tap):
                        arriving[k].wait()
                taps.append(dot(stacked[row], wd_ref[tap].reshape(6 * chans, chans)))
            total = shifted_sum(taps, cols) + bd_ref[...]
            out_ref[cycle, row] = total.astype(BF16)
            edge_ref[cycle, 0, row] = total[:16]
            edge_ref[cycle, 1, row] = total[cols - 16 :]
            copies = []
            if row % 4 == 3:
                rows = (cycle, pl.ds(row - 3, 4))
                copies = [(out_ref.at[rows], out_hbm.at[rows])]
            if row == height - 1:
                copies.append((edge_ref.at[cycle], edge_hbm.at[cycle]))
            yield fetch(copies, out_sems.at[cycle, pl.ds(row // 4, len(copies))]) if copies else []

    for _ in prepare(0):
        pass
    for cycle in range(cycles):
        ahead = prepare(cycle + 1) if cycle + 1 < cycles else iter(())
        for copies in convolve(cycle):
            leaving += copies
            next(ahead, None)
            next(ahead, None)
        for _ in ahead:
            pass
    leaving += fetch([(coarse_ref, coarse_hbm)], out_sems.at[cycles, pl.ds(0, 1)])
    for copy in leaving:
        copy.wait()


def seal(coarse_at, fine_at, tab_hbm, tile_hbm, code_hbm, recv_hbm, coarse_hbm, edge_hbm, wm_hbm, bm_hbm, u_hbm,
         bu_hbm, wd_hbm, out_in, out_hbm, recv_ref, coarse_ref, edge_ref, wm_ref, bm_ref, u_ref, bu_ref, wu_ref, ws_ref, out_ref,
         tab_ref, tile_ref, code_ref, in_sems, out_sems):
    tiles, strips, height = coarse_at.tiles, coarse_at.strips, fine_at.height
    cycles, _, _, _, chans = edge_ref.shape
    cols = out_hbm.shape[2]
    low = height // 2
    pairs = [(recv_hbm, recv_ref), (bm_hbm, bm_ref), (bu_hbm, bu_ref), (coarse_hbm, coarse_ref), (wm_hbm, wm_ref), (u_hbm, u_ref)]
    pairs += [(wd_hbm.at[:, :, pl.ds(0, chans)], wu_ref), (edge_hbm, edge_ref)]
    pairs += [(wd_hbm.at[:, 2 * side, pl.ds(chans, chans)], ws_ref.at[side]) for side in range(2)]
    seams = fetch([(tab_hbm, tab_ref), (tile_hbm, tile_ref), (code_hbm, code_ref)], in_sems.at[pl.ds(10, 3)])
    arriving = fetch(pairs, in_sems.at[pl.ds(0, 10)])
    for copy in seams:
        copy.wait()
    strip = strip_of(tiles)
    rows8 = rows_iota(8) - 2
    rows16 = rows_iota(16) - 1
    aligned, taps, skips, sides, flips, strips_at = [], [[], [], []], [], [], [], []
    for side in range(2):
        for cycle in range(cycles):
            other, face, side_bit, flip = seam_of(tile_ref, code_ref, tiles, cycle, side)
            column = other * 2 + side_bit
            aligned.append(coarse_at.source(strip, flip, face, column * 2, rows8))
            place = fine_at.source(strip, flip, face, column, rows16)
            skips.append(jnp.where(rows16 <= height, place, -1))
            there = jnp.where(flip == 1, strips - 1 - strip, strip)
            number = tab_ref[face * 2, column]
            beyond = lax.div(number, 4)
            code = lax.rem(number, 4)
            other2, face2 = lax.div(beyond, FACES), lax.rem(beyond, FACES)
            column2 = other2 * 2 + lax.rem(code, 2)
            pad = coarse_at.source(there, lax.div(code, 2), face2, column2 * 2, rows8)
            edge = coarse_at.source(there, 0, face, column * 2, rows8)
            inner = coarse_at.source(there, 0, face, column * 2 + 1, rows8)
            taps[0].append(jnp.where(side_bit == 0, pad, inner))
            taps[1].append(edge)
            taps[2].append(jnp.where(side_bit == 0, inner, pad))
            sides.append(side_bit)
            flips.append(flip)
            strips_at.append(there)
    arriving[0].wait()
    got = pick(aligned + taps[0] + taps[1] + taps[2] + skips, recv_ref[...])
    n = 8 * 2 * cycles
    at8 = lax.broadcasted_iota(jnp.int32, (8, chans), 0) - 2

    def on_face(s):
        return jnp.where(((at8 < 0) & (s == 0)) | ((at8 >= low) & (s == strips - 1)), 0.0, 1.0)

    for copy in arriving[1:5]:
        copy.wait()
    own = got[:n]
    there = got[n : 4 * n]
    rows = []
    for row in range(3):
        here = [dot(own[side * n // 2 : (side + 1) * n // 2], wm_ref[row, 2 * side]) for side in range(2)]
        away = sum(dot(there[tap * n : (tap + 1) * n], wm_ref[row, tap]) for tap in range(3))
        rows.append(jnp.concatenate(here + [away], axis=0))
    total = pltpu.roll(rows[0], 1, 0) + rows[1] + pltpu.roll(rows[2], 2 * n - 1, 0)
    mine = [
        total[(side * cycles + cycle) * 8 : (side * cycles + cycle + 1) * 8] + coarse_ref[cycle, side]
        for side in range(2)
        for cycle in range(cycles)
    ]
    total = jnp.concatenate(mine + [total[n:] + bm_ref[...]], axis=0)
    keep = jnp.concatenate([on_face(s) for s in [strip] * (2 * cycles) + strips_at], axis=0)
    column = (gelu(total) * keep).astype(BF16)
    arriving[5].wait()
    phases = [
        [((dot(column, u_ref[a, b]) + bu_ref[...]) * keep).astype(BF16) for b in range(2)] for a in range(2)
    ]
    right = jnp.concatenate([jnp.where(at8 > -99, b, 0) for b in sides], axis=0) == 1
    place = lax.shift_right_arithmetic(rows16 - (rows16 & 1), 1) + 2
    fine_own = [jnp.where(rows16 <= height, (rows16 & 1) * n + k * 8 + place, -1) for k in range(2 * cycles)]
    fine_there = []
    for k in range(2 * cycles):
        fine = jnp.where(flips[k] == 1, height - 1 - rows16, rows16)
        a = fine & 1
        place = a * n + k * 8 + lax.shift_right_arithmetic(fine - a, 1) + 2
        fine_there.append(jnp.where(rows16 <= height, place, -1))
    beyond = [jnp.where(right, phases[a][1][n:], phases[a][0][n:]) for a in range(2)]
    outer = pick(fine_there, jnp.concatenate(beyond, axis=0))
    inside = [pick(fine_own, jnp.concatenate([phases[a][b][:n] for a in range(2)], axis=0)) for b in range(2)]
    skip_pad = got[4 * n :]
    m = 16 * cycles
    lines = [[outer[:m], inside[0][:m], inside[1][:m]], [outer[m:], inside[1][m:], inside[0][m:]]]
    for copy in arriving[6:]:
        copy.wait()
    sums = [[[], [], []], [[], [], []]]
    for row in range(3):
        found = [[0.0, 0.0, 0.0], [0.0, 0.0, 0.0]]
        for tap in range(3):
            uses = []
            for side in range(2):
                offset = tap if side == 0 else 2 - tap
                uses += [(side, line, line - offset) for line in range(3) if line >= offset]
            value = dot(jnp.concatenate([lines[side][line] for side, line, _ in uses], axis=0), wu_ref[row, tap])
            for k, (side, _, into) in enumerate(uses):
                found[side][into] = found[side][into] + value[k * m : (k + 1) * m]
        for side in range(2):
            found[side][0] = found[side][0] + dot(skip_pad[side * m : (side + 1) * m], ws_ref[side, row])
            for into in range(3):
                sums[side][into].append(found[side][into])
    iota16 = lax.broadcasted_iota(jnp.int32, (16, chans), 0)
    for side in range(2):
        for cycle in range(cycles):
            extra = [column_sum(sums[side][into], cycle, height) for into in range(3)]
            for row in range(height):
                value = edge_ref[cycle, side, row]
                for into in range(3):
                    at = into if side == 0 else 15 - into
                    value = value + jnp.where(iota16 == at, extra[into][row : row + 1], 0.0)
                out_ref[side, cycle, row] = value.astype(BF16)
    leaving = fetch(
        [(out_ref.at[side], out_hbm.at[:, :, pl.ds((cols - 16) * side, 16)]) for side in range(2)], out_sems
    )
    for copy in leaving:
        copy.wait()


def on_device(tiles, fields, seam_tile, seam_code, encoder_weight, encoder_bias, middle_weight,
              middle_bias, upconv_weight, upconv_bias, decoder_weight, decoder_offset_bias):
    cycles, height, cols, chans = fields.shape
    low, half = height // 2, cols // 2
    strips = tiles // FACES
    joint = strips == 4

    def strip(t):
        return (t + strips // 2) % strips

    near_pairs, far_pairs = [], []
    for t in range(tiles):
        pairs = near_pairs if strip(t) % 2 == 0 else far_pairs
        after = (t + 1) % tiles
        pairs += [(t, after), (after, t)]

    def tile_at(face, s):
        return (face * strips + s - strips // 2) % tiles

    groups = [
        [tile_at(face, s) for face in range(FACES) for s in (k, strips - 1 - k)]
        for k in range(strips // 2)
    ]
    members = 2 * FACES

    def share(x):
        return lax.all_to_all(x, "tile", 0, 0, tiled=True, axis_index_groups=groups)

    columns = 2 * cycles
    tail1 = (columns + 1 + 15) // 16 * 16
    spec = Layout(tiles, height, 1, columns, 0, columns * height, tail1)
    own2 = 2 * columns * low + columns * height
    tail2 = (4 * columns + columns + 15) // 16 * 16
    coarse_at = Layout(tiles, low, 2, 2 * columns, 0, own2, tail2)
    fine_at = Layout(tiles, height, 1, columns, 2 * columns * low, own2 + 4 * columns, tail2)
    halos = 1 if joint else 2
    spec.payload = columns * height + halos * tail1
    payload = own2 + halos * tail2
    coarse_at.payload = fine_at.payload = payload

    def to_near(x):
        return lax.ppermute(x, "tile", near_pairs)

    def to_far(x):
        return lax.ppermute(x, "tile", far_pairs)

    def pack(own, near_tail, far_tail, near):
        tails = [to_near(near_tail)] + ([] if joint else [to_far(far_tail)])
        rows = own.shape[1] - sum(tail.shape[0] for tail in tails)
        for tail in tails:
            tail = jnp.broadcast_to(tail[None], (members,) + tail.shape)
            own = lax.dynamic_update_slice(own, tail, (0, rows, 0))
            rows += tail.shape[1]
        return share(own), to_near(near)

    seams = (jnp.transpose(seam_tile, (1, 2, 0)), jnp.transpose(seam_code, (1, 2, 0)))
    eb, mb, ub, db = (b.reshape(1, chans) for b in (encoder_bias, middle_bias, upconv_bias, decoder_offset_bias))

    hbm = pl.BlockSpec(memory_space=pltpu.HBM)
    vmem = pl.BlockSpec(memory_space=pltpu.VMEM)
    seam_scratch = [pltpu.SMEM((1, 2, cycles), jnp.int32)] * 2
    dma = pltpu.SemaphoreType.DMA
    tall = (cycles, height, cols, chans)
    row_shape = (cycles, cols, chans)
    wide = (cycles, 2 * cols, chans)
    square = (chans, chans)
    wshape = (3, 3) + square
    pooled_shape = (cycles, low, half, chans)
    edge_shape = (2, cycles, height, 16, chans)

    def call(body, name, outs, in_specs, out_specs, scratch, *args, **options):
        return pl.pallas_call(
            body,
            out_shape=[jax.ShapeDtypeStruct(shape, dtype) for shape, dtype in outs],
            in_specs=in_specs,
            out_specs=out_specs,
            scratch_shapes=[pltpu.VMEM(*x) if isinstance(x, tuple) else x for x in scratch],
            compiler_params=pltpu.CompilerParams(vmem_limit_bytes=56 * MIB),
            name=name,
            **options,
        )(*args)

    far_cost = pl.CostEstimate(flops=10**12, bytes_accessed=10**9, transcendentals=0)
    vector = (1, chans)
    own, near_tail, far_tail, near, far = call(
        functools.partial(lift, spec), "lift",
        [((members, spec.payload, chans), BF16)] + [((tail1, chans), BF16)] * 2 + [(row_shape, BF16)] * 2,
        [hbm] * 3, [hbm] * 5,
        [(edge_shape, BF16), ((2,) + row_shape, BF16), ((columns * height, chans), F32), ((2, tail1, chans), F32),
         ((columns * height, chans), BF16), ((2, tail1, chans), BF16), *seam_scratch, dma((6,)), dma((4 + members,))],
        fields, *seams,
    )
    recv, near = pack(own, near_tail, far_tail, near)
    far = to_far(far)
    pre_shape = (cycles, 2, height, chans)
    skip, pooled, near, far, pre_col = call(
        functools.partial(encode, tiles), "encode",
        [(tall, BF16), (pooled_shape, BF16), (wide, BF16), (wide, BF16), (pre_shape, F32)],
        [hbm] * 5, [hbm] * 5,
        [(tall, BF16), (row_shape, BF16), (row_shape, BF16), (wshape, BF16), (vector, F32), ((height, cols, 3 * chans), BF16), (tall, BF16),
         (pooled_shape, BF16), ((2,) + wide, BF16), (pre_shape, F32), ((cols, 128), F32),
         dma((6 + cycles,)), dma((cycles, height // 4 + 4))],
        fields, near, far, encoder_weight, eb,
        cost_estimate=far_cost,
    )
    pool_edges = (2, cycles, low, 16, chans)
    skip, pooled, near, far, own, near_tail, far_tail, table = call(
        functools.partial(mend, spec, coarse_at, fine_at), "mend",
        [(tall, BF16), (pooled_shape, BF16), (wide, BF16), (wide, BF16), ((members, payload, chans), BF16)]
        + [((tail2, chans), BF16)] * 2 + [((members, 128), jnp.int32)],
        [vmem] + [hbm] * 8, [hbm] * 8,
        [((2, 3) + square, BF16), (pre_shape, F32), (edge_shape, BF16), (pool_edges, BF16), ((own2, chans), F32),
         ((2, tail2, chans), F32), ((own2, chans), BF16), ((2, tail2, chans), BF16), ((members, 128), jnp.int32),
         *seam_scratch, dma((9,)), dma((19 + members,))],
        recv.reshape(-1, chans), encoder_weight, skip, pooled, near, far, pre_col, *seams,
        input_output_aliases={2: 0, 3: 1, 4: 2, 5: 3},
    )
    recv2, near2 = pack(own, near_tail, far_tail, near)
    far2 = to_far(far)
    edges = (cycles, 2, height, 16, chans)
    coarse_edges = (cycles, 2, 8, chans)
    out, edge, coarse = call(
        functools.partial(decode, tiles), "decode",
        [(tall, BF16), (edges, F32), (coarse_edges, F32)],
        [hbm] * 10, [hbm, hbm, hbm],
        [(tall, BF16), (pooled_shape, BF16), (wide, BF16), (wide, BF16), (wshape, BF16), (vector, F32),
         ((2, 2) + square, BF16), (vector, F32), ((3, 6) + square, BF16), (vector, F32), (tall, BF16), (edges, F32),
         (coarse_edges, F32)]
        + [((height, cols, 6 * chans), BF16)] * 2 + [((low + 2, half, 3 * chans), BF16)] * 2
        + [((height + 2, chans // 128, cols, 128), F32)] * 2
        + [dma((19 + cycles,)), dma((cycles + 1, height // 4 + 1))],
        skip, pooled, near2, far2, middle_weight, mb, upconv_weight, ub, decoder_weight, db,
        cost_estimate=far_cost,
    )
    (out,) = call(
        functools.partial(seal, coarse_at, fine_at), "seal",
        [(tall, BF16)],
        [hbm] * 12, [hbm],
        [((members * payload, chans), BF16), (coarse_edges, F32), (edges, F32), (wshape, BF16), (vector, F32), ((2, 2) + square, BF16), (vector, F32),
         (wshape, BF16), ((2, 3) + square, BF16), (edge_shape, BF16),
         pltpu.SMEM((members, 128), jnp.int32), *seam_scratch, dma((13,)), dma((2,))],
        table, *seams, recv2.reshape(-1, chans), coarse, edge, middle_weight, mb, upconv_weight, ub, decoder_weight, out,
        input_output_aliases={11: 0},
    )
    return out


def solution(mesh):
    return jax.shard_map(
        functools.partial(on_device, mesh.shape["tile"]),
        mesh=mesh,
        in_specs=(P("grp", "tile", None, None), P(None, "tile", None), P(None, "tile", None)) + (P(),) * 8,
        out_specs=P("grp", "tile", None, None),
        check_vma=False,
    )
```

```python
import functools

import jax
import jax.numpy as jnp
from jax import lax
from jax.experimental import pallas as pl
from jax.experimental.pallas import tpu as pltpu
from jax.sharding import PartitionSpec as P

F32 = jnp.float32
BF16 = jnp.bfloat16
FACES = 4
MIB = 1 << 20


def dot(a, b):
    return jnp.dot(a, b, preferred_element_type=F32)


def gelu(x):
    return 0.5 * x * (1.0 + jnp.tanh(0.7978845608 * (x + 0.044715 * x * x * x)))


def rows_iota(n):
    return lax.broadcasted_iota(jnp.int32, (n, 1), 0)


class Layout:
    def __init__(self, tiles, height, depth, columns, own, near, tail):
        self.tiles = tiles
        self.strips = tiles // FACES
        self.joint = self.strips == 4
        self.height = height
        self.depth = depth
        self.columns = columns
        self.own = own
        self.near = near
        self.far = near + tail
        self.payload = 0

    def source(self, strip, flip, face, column, row):
        height, last = self.height, self.strips - 1
        strip = jnp.where(flip == 1, last - strip, strip)
        row = jnp.where(flip == 1, height - 1 - row, row)
        upper = jnp.where(strip >= self.strips // 2, 1, 0)
        odd = lax.rem(strip, 2)
        above = row < 0
        below = row >= height
        away = jnp.where(above, -row, row - (height - 1)) - 1
        near = (above & (odd == 1)) | (below & (odd == 0))
        missing = (above & (strip == 0)) | (below & (strip == last))
        member = (face * 2 + upper) * self.payload
        inside = member + self.own + column * height + row
        beside = member + self.near + column * self.depth + away
        if self.joint:
            across = (face * 2 + 1 - upper) * self.payload + self.own + column * height
            far = across + jnp.where(above, height - 1 - away, away)
        else:
            far = member + self.far + column * self.depth + away
        place = jnp.where(above | below, jnp.where(near, beside, far), inside)
        return jnp.where(missing, -1, place)


def strip_of(tiles):
    strips = tiles // FACES
    return lax.rem(lax.axis_index("tile") + strips // 2, strips)


def seam_of(tile_ref, code_ref, tiles, cycle, side):
    strips = tiles // FACES
    partner = tile_ref[0, side, cycle]
    code = code_ref[0, side, cycle]
    other = lax.div(partner, tiles)
    place = partner - other * tiles + strips // 2
    face = lax.rem(lax.div(place, strips), FACES)
    return other, face, lax.rem(code, 2), lax.div(code, 2)


def pick(targets, table):
    wanted = jnp.concatenate(targets, axis=0)
    shape = (wanted.shape[0], table.shape[0])
    lanes = lax.broadcasted_iota(jnp.int32, shape, 1)
    chooser = jnp.where(lanes == wanted, 1.0, 0.0).astype(BF16)
    return dot(chooser, table).astype(BF16)


def shifted_sum(taps, cols):
    left, middle, right = taps
    n = middle.shape[0]
    place = lax.broadcasted_iota(jnp.int32, middle.shape, 0) & (cols - 1)
    left = jnp.where(place == 0, 0.0, pltpu.roll(left, 1, 0))
    right = jnp.where(place == cols - 1, 0.0, pltpu.roll(right, n - 1, 0))
    return middle + left + right


def stack_taps(stacked, row_of, rows):
    depth = stacked.shape[-1] // 3
    for row in range(-1, rows + 1):
        value = row_of(row)
        for tap in range(3):
            at = row + 1 - tap
            if 0 <= at < rows:
                stacked[at, :, tap * depth : (tap + 1) * depth] = value


def column_taps(lhs, weight_ref):
    depth = weight_ref.shape[2]
    return [
        dot(lhs, weight_ref[:, tap].reshape(3 * depth, weight_ref.shape[3]))
        for tap in range(3)
    ]


def halo_rows(rows_ref, top, bottom):
    def row_of(row):
        if row < 0:
            return top
        if row >= rows_ref.shape[0]:
            return bottom
        return rows_ref[row]

    return row_of


def top_and_bottom(near, far, odd, ends):
    far = jnp.where(ends, jnp.zeros_like(far), far)
    return jnp.where(odd == 1, near, far), jnp.where(odd == 1, far, near)


def column_sum(parts, cycle, height):
    at = cycle * 16
    return sum(parts[tap][at + tap : at + tap + height] for tap in range(3))


def lift(layout, x_hbm, tile_hbm, code_hbm, own_hbm, near_tail_hbm, far_tail_hbm, near_hbm, far_hbm,
         edges, rows, own, tails, own16, tails16, tile_ref, code_ref, in_sems, out_sems):
    height = layout.height
    cycles, cols = x_hbm.shape[0], x_hbm.shape[2]
    upper = lax.rem(strip_of(layout.tiles), 2) * (height - 1)
    nearest = (height - 1 - upper, upper)
    pairs = [(x_hbm.at[:, :, pl.ds(first, 16)], edges.at[side]) for side, first in enumerate((0, cols - 16))]
    pairs += [(x_hbm.at[:, nearest[k]], rows.at[k]) for k in range(2)]
    arriving = fetch(pairs + [(tile_hbm, tile_ref), (code_hbm, code_ref)], in_sems)
    tails[...] = jnp.zeros_like(tails)
    for side in range(2):
        arriving[side].wait()
        at = 15 * side
        for cycle in range(cycles):
            column = cycle * 2 + side
            for row in range(height):
                value = edges[side, cycle, row].astype(F32)[at : at + 1]
                own[column * height + row : column * height + row + 1] = value
            for k in range(2):
                value = edges[side, cycle, nearest[k]].astype(F32)[at : at + 1]
                tails[k, column : column + 1] = value
    for copy in arriving[4:]:
        copy.wait()
    lanes = lax.broadcasted_iota(jnp.int32, (1, own.shape[1]), 1)
    noted = jnp.zeros((1, own.shape[1]), F32)
    for cycle in range(cycles):
        for side in range(2):
            other, face, side_bit, flip = seam_of(tile_ref, code_ref, layout.tiles, cycle, side)
            number = (other * FACES + face) * 4 + flip * 2 + side_bit
            noted = jnp.where(lanes == cycle * 2 + side, number.astype(F32), noted)
    for k in range(2):
        tails[k, layout.columns : layout.columns + 1] = noted
    own16[...] = own[...].astype(BF16)
    tails16[...] = tails[...].astype(BF16)
    pairs = [(tails16.at[0], near_tail_hbm), (tails16.at[1], far_tail_hbm)]
    pairs += [(own16, own_hbm.at[k, pl.ds(0, own16.shape[0])]) for k in range(2 * FACES)]
    for copy in arriving[2:4]:
        copy.wait()
    leaving = fetch(pairs + [(rows.at[0], near_hbm), (rows.at[1], far_hbm)], out_sems)
    for copy in leaving:
        copy.wait()


def fetch(pairs, sems):
    copies = [pltpu.make_async_copy(src, dst, sems.at[k]) for k, (src, dst) in enumerate(pairs)]
    for copy in copies:
        copy.start()
    return copies


def encode(tiles, x_hbm, near_in, far_in, w_hbm, b_hbm, skip_hbm, pooled_hbm, near_hbm, far_hbm, pre_hbm,
           x_ref, near_ref, far_ref, w_ref, b_ref, stacked, skip_ref, pooled_ref, rows_ref, pre_ref, paired, in_sems, out_sems):
    cycles, height, cols, chans = x_ref.shape
    half = cols // 2
    pairs = [(x_hbm.at[0], x_ref.at[0]), (near_in, near_ref), (far_in, far_ref), (b_hbm, b_ref)]
    pairs += [(w_hbm.at[:, tap], w_ref.at[tap]) for tap in range(3)]
    arriving = fetch(pairs, in_sems.at[pl.ds(0, 7)])
    strip = strip_of(tiles)
    odd = lax.rem(strip, 2)
    ends = (strip == 0) | (strip == tiles // FACES - 1)
    for copy in arriving[:4]:
        copy.wait()
    leaving = []
    for cycle in range(cycles):
        if cycle > 0:
            arriving[6 + cycle].wait()
        top, bottom = top_and_bottom(near_ref[cycle], far_ref[cycle], odd, ends)
        stack_taps(stacked, halo_rows(x_ref.at[cycle], top, bottom), height)
        for row in range(height):
            taps = []
            for tap in range(3):
                if cycle == 0 and row == 0:
                    arriving[4 + tap].wait()
                taps.append(dot(stacked[row], w_ref[tap].reshape(3 * chans, chans)))
            if cycle == 0 and row == 0:
                pairs = [(x_hbm.at[k], x_ref.at[k]) for k in range(1, cycles)]
                arriving += fetch(pairs, in_sems.at[pl.ds(7, cycles - 1)])
            total = shifted_sum(taps, cols) + b_ref[...]
            value = gelu(total).astype(BF16)
            skip_ref[cycle, row] = value
            pre_ref[cycle, 0, row : row + 1] = total[:1]
            pre_ref[cycle, 1, row : row + 1] = total[cols - 1 :]
            if row % 2 == 0:
                before = value.astype(F32)
            else:
                pair = 0.25 * (before + value.astype(F32))
                for lane in range(0, chans, 128):
                    paired[...] = pair[:, lane : lane + 128]
                    mean = paired[pl.ds(0, half, 2), :] + paired[pl.ds(1, half, 2), :]
                    pooled_ref[cycle, row // 2, :, lane : lane + 128] = mean.astype(BF16)
            if row % 4 == 3:
                rows = (cycle, pl.ds(row - 3, 4))
                leaving += fetch([(skip_ref.at[rows], skip_hbm.at[rows])], out_sems.at[cycle, pl.ds(row // 4, 1)])
        low = height // 2 - 1
        for k, at_top in ((0, odd == 1), (1, odd == 0)):
            rows_ref[k, cycle, :cols] = skip_ref[cycle, jnp.where(at_top, 0, height - 1)]
            rows_ref[k, cycle, cols : cols + half] = pooled_ref[cycle, jnp.where(at_top, 0, low)]
            rows_ref[k, cycle, cols + half :] = pooled_ref[cycle, jnp.where(at_top, 1, low - 1)]
        pairs = [(rows_ref.at[0, cycle], near_hbm.at[cycle]), (rows_ref.at[1, cycle], far_hbm.at[cycle])]
        pairs += [(pooled_ref.at[cycle], pooled_hbm.at[cycle]), (pre_ref.at[cycle], pre_hbm.at[cycle])]
        leaving += fetch(pairs, out_sems.at[cycle, pl.ds(height // 4, 4)])
    for copy in leaving:
        copy.wait()


def mend(layout, coarse, fine, recv_hbm, w_hbm, skip_in, pooled_in, near_in, far_in, pre_hbm, tile_hbm, code_hbm,
         skip_hbm, pooled_hbm, near_hbm, far_hbm, own_hbm, near_tail_hbm, far_tail_hbm, table_hbm,
         recv_ref, w_ref, pre_ref, edges, pools, own, tails, own16, tails16, table_ref, tile_ref, code_ref, in_sems, out_sems):
    tiles, height, low = layout.tiles, layout.height, coarse.height
    cycles, cols, chans = skip_in.shape[0], skip_in.shape[2], skip_in.shape[3]
    half = cols // 2
    pairs = [(tile_hbm, tile_ref), (code_hbm, code_ref), (recv_hbm, recv_ref)]
    pairs += [(w_hbm.at[:, 2 * side], w_ref.at[side]) for side in range(2)] + [(pre_hbm, pre_ref)]
    for side in range(2):
        pairs.append((skip_in.at[:, :, pl.ds((cols - 16) * side, 16)], edges.at[side]))
        pairs.append((pooled_in.at[:, :, pl.ds((half - 16) * side, 16)], pools.at[side]))
    arriving = fetch(pairs, in_sems)
    strip = strip_of(tiles)
    odd = lax.rem(strip, 2)
    row_iota = rows_iota(16) - 1
    targets = []
    for copy in arriving[:2]:
        copy.wait()
    for side in range(2):
        for cycle in range(cycles):
            other, face, side_bit, flip = seam_of(tile_ref, code_ref, tiles, cycle, side)
            place = layout.source(strip, flip, face, other * 2 + side_bit, row_iota)
            targets.append(jnp.where(row_iota <= height, place, -1))
    arriving[2].wait()
    pads = pick(targets, recv_ref[...])
    noted = layout.near + layout.columns
    for member in range(2 * FACES):
        at = member * layout.payload + noted // 16 * 16
        block = recv_ref[at : at + 16, :128].astype(F32)
        table_ref[member : member + 1] = block[noted % 16 : noted % 16 + 1].astype(jnp.int32)
    part = pads.shape[0] // 2
    for copy in arriving[3:6]:
        copy.wait()
    seams = [
        [dot(pads[side * part : (side + 1) * part], w_ref[side, tap]) for tap in range(3)] for side in range(2)
    ]
    iota16 = lax.broadcasted_iota(jnp.int32, (16, chans), 0)
    tails[...] = jnp.zeros_like(tails)
    for copy in arriving[6:]:
        copy.wait()
    at_top = (odd == 1, odd == 0)
    skip_at = [jnp.where(t, 0, height - 1) for t in at_top]
    pool_at = [(jnp.where(t, 0, low - 1), jnp.where(t, 1, low - 2)) for t in at_top]
    for cycle in range(cycles):
        for side in range(2):
            column = cycle * 2 + side
            at, inward = (0, 1) if side == 0 else (15, 14)
            total = gelu(pre_ref[cycle, side] + column_sum(seams[side], cycle, height))
            start = fine.own + column * height
            own[start : start + height] = total
            for row in range(height):
                block = edges[side, cycle, row].astype(F32)
                block = jnp.where(iota16 == at, total[row : row + 1], block).astype(BF16)
                edges[side, cycle, row] = block
                if row % 2 == 0:
                    before = block.astype(F32)
                else:
                    pair = before + block.astype(F32)
                    mean = 0.25 * (pair[at : at + 1] + pair[inward : inward + 1])
                    block = pools[side, cycle, row // 2].astype(F32)
                    block = jnp.where(iota16 == at, mean, block)
                    pools[side, cycle, row // 2] = block.astype(BF16)
                    for depth, place in enumerate((at, inward)):
                        start = coarse.own + (column * 2 + depth) * low + row // 2
                        own[start : start + 1] = block[place : place + 1]
            for k in range(2):
                start = fine.near - coarse.near + column
                value = edges[side, cycle, skip_at[k]].astype(F32)
                tails[k, start : start + 1] = value[at : at + 1]
                for away in range(2):
                    value = pools[side, cycle, pool_at[k][away]].astype(F32)
                    for depth, place in enumerate((at, inward)):
                        start = (column * 2 + depth) * 2 + away
                        tails[k, start : start + 1] = value[place : place + 1]
    own16[...] = own[...].astype(BF16)
    tails16[...] = tails[...].astype(BF16)
    pairs = [(tails16.at[0], near_tail_hbm), (tails16.at[1], far_tail_hbm), (table_ref, table_hbm)]
    pairs += [(own16, own_hbm.at[k, pl.ds(0, own16.shape[0])]) for k in range(2 * FACES)]
    for side in range(2):
        pairs.append((edges.at[side], skip_hbm.at[:, :, pl.ds((cols - 16) * side, 16)]))
        pairs.append((pools.at[side], pooled_hbm.at[:, :, pl.ds((half - 16) * side, 16)]))
        for k, ref in enumerate((near_hbm, far_hbm)):
            pairs.append((edges.at[side, :, skip_at[k]], ref.at[:, pl.ds((cols - 16) * side, 16)]))
            for away in range(2):
                first = cols + away * half + (half - 16) * side
                pairs.append((pools.at[side, :, pool_at[k][away]], ref.at[:, pl.ds(first, 16)]))
    leaving = fetch(pairs, out_sems)
    for copy in leaving:
        copy.wait()


def decode(tiles, skip_hbm, pooled_hbm, near_hbm, far_hbm, wm_hbm, bm_hbm, u_hbm, bu_hbm, wd_hbm, bd_hbm,
           out_hbm, edge_hbm, coarse_hbm, skip_ref, pooled_ref, near_ref, far_ref, wm_ref, bm_ref, u_ref, bu_ref,
           wd_ref, bd_ref, out_ref, edge_ref, coarse_ref, stacked_a, stacked_b, upper_a, upper_b, joined_a, joined_b,
           in_sems, out_sems):
    strips = tiles // FACES
    cycles, height, cols, chans = skip_ref.shape
    low, half = height // 2, cols // 2
    halos = ((near_hbm, near_ref), (far_hbm, far_ref), (pooled_hbm, pooled_ref))
    pairs = [(src.at[0], dst.at[0]) for src, dst in halos] + [(bm_hbm, bm_ref)]
    pairs += [(wm_hbm.at[:, tap], wm_ref.at[tap]) for tap in range(3)]
    pairs += [(bu_hbm, bu_ref), (u_hbm, u_ref), (skip_hbm.at[0], skip_ref.at[0]), (bd_hbm, bd_ref)]
    for tap in range(3):
        for part in range(2):
            source = wd_hbm.at[:, tap, pl.ds(part * chans, chans)]
            pairs.append((source, wd_ref.at[tap, pl.ds(3 * part, 3)]))
    pairs += [(skip_hbm.at[cycle], skip_ref.at[cycle]) for cycle in range(1, cycles)]
    rest = pl.ds(1, cycles - 1)
    pairs += [(src.at[rest], dst.at[rest]) for src, dst in halos]
    arriving = fetch(pairs, in_sems)
    strip = strip_of(tiles)
    odd = lax.rem(strip, 2)
    first_strip, last_strip = strip == 0, strip == strips - 1
    ends = first_strip | last_strip
    place = lax.broadcasted_iota(jnp.int32, (cols, chans), 0)
    inner = (place > 1) & (place < cols - 2)
    coarse_ref[...] = jnp.zeros_like(coarse_ref)
    leaving = []
    for copy in arriving[:4]:
        copy.wait()

    def prepare(cycle):
        if cycle == 1:
            for copy in arriving[16 + cycles :]:
                copy.wait()
        top, bottom = top_and_bottom(near_ref[cycle], far_ref[cycle], odd, ends)
        stacked, upper, joined = (stacked_a, upper_a, joined_a) if cycle % 2 == 0 else (stacked_b, upper_b, joined_b)

        def pooled_row(row):
            if row < -1:
                return top[cols + half :]
            if row < 0:
                return top[cols : cols + half]
            if row < low:
                return pooled_ref[cycle, row]
            if row == low:
                return bottom[cols : cols + half]
            return bottom[cols + half :]

        stack_taps(upper, lambda row: pooled_row(row - 1), low + 2)
        yield
        lhs = upper[...].reshape((low + 2) * half, 3 * chans)
        taps = []
        for tap in range(3):
            if cycle == 0:
                arriving[4 + tap].wait()
            taps.append(dot(lhs, wm_ref[tap].reshape(3 * chans, chans)))
        total = shifted_sum(taps, half) + bm_ref[...]
        yield
        coarse = []
        for row in range(low + 2):
            at = row * half
            coarse_ref[cycle, 0, row + 1 : row + 2] = total[at : at + 1]
            coarse_ref[cycle, 1, row + 1 : row + 2] = total[at + half - 1 : at + half]
            coarse.append(gelu(total[at : at + half]).astype(BF16))
        if cycle == 0:
            arriving[7].wait()
            arriving[8].wait()
        yield
        for a in range(2):
            part = jnp.concatenate(coarse[1:] if a == 0 else coarse[:-1], axis=0)
            for b in range(2):
                value = dot(part, u_ref[a, b]) + bu_ref[...]
                for k in range(low + 1):
                    at = 2 * k + 1 - a
                    for lane in range(0, chans, 128):
                        part_of = value[k * half : (k + 1) * half, lane : lane + 128]
                        joined[at, lane // 128, pl.ds(b, half, 2), :] = part_of
                yield
        arriving[9 if cycle == 0 else 16 + cycle].wait()
        skip_row = halo_rows(skip_ref.at[cycle], top[:cols], bottom[:cols])
        stack_taps(stacked.at[:, :, pl.ds(3 * chans, 3 * chans)], skip_row, height)
        for row in range(-1, height + 1):
            value = jnp.concatenate([joined[row + 1, k] for k in range(chans // 128)], axis=1)
            keep = inner
            if row < 0:
                keep = keep & jnp.logical_not(first_strip)
            if row >= height:
                keep = keep & jnp.logical_not(last_strip)
            value = jnp.where(keep, value, 0.0).astype(BF16)
            for tap in range(3):
                at = row + 1 - tap
                if 0 <= at < height:
                    stacked[at, :, tap * chans : (tap + 1) * chans] = value
            if row % 5 == 3:
                yield

    def convolve(cycle):
        stacked = stacked_a if cycle % 2 == 0 else stacked_b
        for row in range(height):
            taps = []
            for tap in range(3):
                if cycle == 0 and row == 0:
                    for k in range(10 if tap == 0 else 11 + 2 * tap, 13 + 2 * tap):
                        arriving[k].wait()
                taps.append(dot(stacked[row], wd_ref[tap].reshape(6 * chans, chans)))
            total = shifted_sum(taps, cols) + bd_ref[...]
            out_ref[cycle, row] = total.astype(BF16)
            edge_ref[cycle, 0, row] = total[:16]
            edge_ref[cycle, 1, row] = total[cols - 16 :]
            copies = []
            if row % 4 == 3:
                rows = (cycle, pl.ds(row - 3, 4))
                copies = [(out_ref.at[rows], out_hbm.at[rows])]
            if row == height - 1:
                copies.append((edge_ref.at[cycle], edge_hbm.at[cycle]))
            yield fetch(copies, out_sems.at[cycle, pl.ds(row // 4, len(copies))]) if copies else []

    for _ in prepare(0):
        pass
    for cycle in range(cycles):
        ahead = prepare(cycle + 1) if cycle + 1 < cycles else iter(())
        for copies in convolve(cycle):
            leaving += copies
            next(ahead, None)
            next(ahead, None)
        for _ in ahead:
            pass
    leaving += fetch([(coarse_ref, coarse_hbm)], out_sems.at[cycles, pl.ds(0, 1)])
    for copy in leaving:
        copy.wait()


def seal(coarse_at, fine_at, tab_hbm, tile_hbm, code_hbm, recv_hbm, coarse_hbm, edge_hbm, wm_hbm, bm_hbm, u_hbm,
         bu_hbm, wd_hbm, out_in, out_hbm, recv_ref, coarse_ref, edge_ref, wm_ref, bm_ref, u_ref, bu_ref, wu_ref, ws_ref, out_ref,
         tab_ref, tile_ref, code_ref, in_sems, out_sems):
    tiles, strips, height = coarse_at.tiles, coarse_at.strips, fine_at.height
    cycles, _, _, _, chans = edge_ref.shape
    cols = out_hbm.shape[2]
    low = height // 2
    pairs = [(recv_hbm, recv_ref), (bm_hbm, bm_ref), (bu_hbm, bu_ref), (coarse_hbm, coarse_ref), (wm_hbm, wm_ref), (u_hbm, u_ref)]
    pairs += [(wd_hbm.at[:, :, pl.ds(0, chans)], wu_ref), (edge_hbm, edge_ref)]
    pairs += [(wd_hbm.at[:, 2 * side, pl.ds(chans, chans)], ws_ref.at[side]) for side in range(2)]
    seams = fetch([(tab_hbm, tab_ref), (tile_hbm, tile_ref), (code_hbm, code_ref)], in_sems.at[pl.ds(10, 3)])
    arriving = fetch(pairs, in_sems.at[pl.ds(0, 10)])
    for copy in seams:
        copy.wait()
    strip = strip_of(tiles)
    rows8 = rows_iota(8) - 2
    rows16 = rows_iota(16) - 1
    aligned, taps, skips, sides, flips, strips_at = [], [[], [], []], [], [], [], []
    for side in range(2):
        for cycle in range(cycles):
            other, face, side_bit, flip = seam_of(tile_ref, code_ref, tiles, cycle, side)
            column = other * 2 + side_bit
            aligned.append(coarse_at.source(strip, flip, face, column * 2, rows8))
            place = fine_at.source(strip, flip, face, column, rows16)
            skips.append(jnp.where(rows16 <= height, place, -1))
            there = jnp.where(flip == 1, strips - 1 - strip, strip)
            number = tab_ref[face * 2, column]
            beyond = lax.div(number, 4)
            code = lax.rem(number, 4)
            other2, face2 = lax.div(beyond, FACES), lax.rem(beyond, FACES)
            column2 = other2 * 2 + lax.rem(code, 2)
            pad = coarse_at.source(there, lax.div(code, 2), face2, column2 * 2, rows8)
            edge = coarse_at.source(there, 0, face, column * 2, rows8)
            inner = coarse_at.source(there, 0, face, column * 2 + 1, rows8)
            taps[0].append(jnp.where(side_bit == 0, pad, inner))
            taps[1].append(edge)
            taps[2].append(jnp.where(side_bit == 0, inner, pad))
            sides.append(side_bit)
            flips.append(flip)
            strips_at.append(there)
    arriving[0].wait()
    got = pick(aligned + taps[0] + taps[1] + taps[2] + skips, recv_ref[...])
    n = 8 * 2 * cycles
    at8 = lax.broadcasted_iota(jnp.int32, (8, chans), 0) - 2

    def on_face(s):
        return jnp.where(((at8 < 0) & (s == 0)) | ((at8 >= low) & (s == strips - 1)), 0.0, 1.0)

    for copy in arriving[1:5]:
        copy.wait()
    own = got[:n]
    there = got[n : 4 * n]
    rows = []
    for row in range(3):
        here = [dot(own[side * n // 2 : (side + 1) * n // 2], wm_ref[row, 2 * side]) for side in range(2)]
        away = sum(dot(there[tap * n : (tap + 1) * n], wm_ref[row, tap]) for tap in range(3))
        rows.append(jnp.concatenate(here + [away], axis=0))
    total = pltpu.roll(rows[0], 1, 0) + rows[1] + pltpu.roll(rows[2], 2 * n - 1, 0)
    mine = [
        total[(side * cycles + cycle) * 8 : (side * cycles + cycle + 1) * 8] + coarse_ref[cycle, side]
        for side in range(2)
        for cycle in range(cycles)
    ]
    total = jnp.concatenate(mine + [total[n:] + bm_ref[...]], axis=0)
    keep = jnp.concatenate([on_face(s) for s in [strip] * (2 * cycles) + strips_at], axis=0)
    column = (gelu(total) * keep).astype(BF16)
    arriving[5].wait()
    phases = [
        [((dot(column, u_ref[a, b]) + bu_ref[...]) * keep).astype(BF16) for b in range(2)] for a in range(2)
    ]
    right = jnp.concatenate([jnp.where(at8 > -99, b, 0) for b in sides], axis=0) == 1
    place = lax.shift_right_arithmetic(rows16 - (rows16 & 1), 1) + 2
    fine_own = [jnp.where(rows16 <= height, (rows16 & 1) * n + k * 8 + place, -1) for k in range(2 * cycles)]
    fine_there = []
    for k in range(2 * cycles):
        fine = jnp.where(flips[k] == 1, height - 1 - rows16, rows16)
        a = fine & 1
        place = a * n + k * 8 + lax.shift_right_arithmetic(fine - a, 1) + 2
        fine_there.append(jnp.where(rows16 <= height, place, -1))
    beyond = [jnp.where(right, phases[a][1][n:], phases[a][0][n:]) for a in range(2)]
    outer = pick(fine_there, jnp.concatenate(beyond, axis=0))
    inside = [pick(fine_own, jnp.concatenate([phases[a][b][:n] for a in range(2)], axis=0)) for b in range(2)]
    skip_pad = got[4 * n :]
    m = 16 * cycles
    lines = [[outer[:m], inside[0][:m], inside[1][:m]], [outer[m:], inside[1][m:], inside[0][m:]]]
    for copy in arriving[6:]:
        copy.wait()
    sums = [[[], [], []], [[], [], []]]
    for row in range(3):
        found = [[0.0, 0.0, 0.0], [0.0, 0.0, 0.0]]
        for tap in range(3):
            uses = []
            for side in range(2):
                offset = tap if side == 0 else 2 - tap
                uses += [(side, line, line - offset) for line in range(3) if line >= offset]
            value = dot(jnp.concatenate([lines[side][line] for side, line, _ in uses], axis=0), wu_ref[row, tap])
            for k, (side, _, into) in enumerate(uses):
                found[side][into] = found[side][into] + value[k * m : (k + 1) * m]
        for side in range(2):
            found[side][0] = found[side][0] + dot(skip_pad[side * m : (side + 1) * m], ws_ref[side, row])
            for into in range(3):
                sums[side][into].append(found[side][into])
    iota16 = lax.broadcasted_iota(jnp.int32, (16, chans), 0)
    for side in range(2):
        for cycle in range(cycles):
            extra = [column_sum(sums[side][into], cycle, height) for into in range(3)]
            for row in range(height):
                value = edge_ref[cycle, side, row]
                for into in range(3):
                    at = into if side == 0 else 15 - into
                    value = value + jnp.where(iota16 == at, extra[into][row : row + 1], 0.0)
                out_ref[side, cycle, row] = value.astype(BF16)
    leaving = fetch(
        [(out_ref.at[side], out_hbm.at[:, :, pl.ds((cols - 16) * side, 16)]) for side in range(2)], out_sems
    )
    for copy in leaving:
        copy.wait()


def on_device(tiles, fields, seam_tile, seam_code, encoder_weight, encoder_bias, middle_weight,
              middle_bias, upconv_weight, upconv_bias, decoder_weight, decoder_offset_bias):
    cycles, height, cols, chans = fields.shape
    low, half = height // 2, cols // 2
    strips = tiles // FACES
    joint = strips == 4

    def strip(t):
        return (t + strips // 2) % strips

    near_pairs, far_pairs = [], []
    for t in range(tiles):
        pairs = near_pairs if strip(t) % 2 == 0 else far_pairs
        after = (t + 1) % tiles
        pairs += [(t, after), (after, t)]

    def tile_at(face, s):
        return (face * strips + s - strips // 2) % tiles

    groups = [
        [tile_at(face, s) for face in range(FACES) for s in (k, strips - 1 - k)]
        for k in range(strips // 2)
    ]
    members = 2 * FACES

    def share(x):
        return lax.all_to_all(x, "tile", 0, 0, tiled=True, axis_index_groups=groups)

    columns = 2 * cycles
    tail1 = (columns + 1 + 15) // 16 * 16
    spec = Layout(tiles, height, 1, columns, 0, columns * height, tail1)
    own2 = 2 * columns * low + columns * height
    tail2 = (4 * columns + columns + 15) // 16 * 16
    coarse_at = Layout(tiles, low, 2, 2 * columns, 0, own2, tail2)
    fine_at = Layout(tiles, height, 1, columns, 2 * columns * low, own2 + 4 * columns, tail2)
    halos = 1 if joint else 2
    spec.payload = columns * height + halos * tail1
    payload = own2 + halos * tail2
    coarse_at.payload = fine_at.payload = payload

    def to_near(x):
        return lax.ppermute(x, "tile", near_pairs)

    def to_far(x):
        return lax.ppermute(x, "tile", far_pairs)

    def pack(own, near_tail, far_tail, near):
        tails = [to_near(near_tail)] + ([] if joint else [to_far(far_tail)])
        rows = own.shape[1] - sum(tail.shape[0] for tail in tails)
        for tail in tails:
            tail = jnp.broadcast_to(tail[None], (members,) + tail.shape)
            own = lax.dynamic_update_slice(own, tail, (0, rows, 0))
            rows += tail.shape[1]
        return share(own), to_near(near)

    seams = (jnp.transpose(seam_tile, (1, 2, 0)), jnp.transpose(seam_code, (1, 2, 0)))
    eb, mb, ub, db = (b.reshape(1, chans) for b in (encoder_bias, middle_bias, upconv_bias, decoder_offset_bias))

    hbm = pl.BlockSpec(memory_space=pltpu.HBM)
    vmem = pl.BlockSpec(memory_space=pltpu.VMEM)
    seam_scratch = [pltpu.SMEM((1, 2, cycles), jnp.int32)] * 2
    dma = pltpu.SemaphoreType.DMA
    tall = (cycles, height, cols, chans)
    row_shape = (cycles, cols, chans)
    wide = (cycles, 2 * cols, chans)
    square = (chans, chans)
    wshape = (3, 3) + square
    pooled_shape = (cycles, low, half, chans)
    edge_shape = (2, cycles, height, 16, chans)

    def call(body, name, outs, in_specs, out_specs, scratch, *args, **options):
        return pl.pallas_call(
            body,
            out_shape=[jax.ShapeDtypeStruct(shape, dtype) for shape, dtype in outs],
            in_specs=in_specs,
            out_specs=out_specs,
            scratch_shapes=[pltpu.VMEM(*x) if isinstance(x, tuple) else x for x in scratch],
            compiler_params=pltpu.CompilerParams(vmem_limit_bytes=56 * MIB),
            name=name,
            **options,
        )(*args)

    far_cost = pl.CostEstimate(flops=10**12, bytes_accessed=10**9, transcendentals=0)
    vector = (1, chans)
    own, near_tail, far_tail, near, far = call(
        functools.partial(lift, spec), "lift",
        [((members, spec.payload, chans), BF16)] + [((tail1, chans), BF16)] * 2 + [(row_shape, BF16)] * 2,
        [hbm] * 3, [hbm] * 5,
        [(edge_shape, BF16), ((2,) + row_shape, BF16), ((columns * height, chans), F32), ((2, tail1, chans), F32),
         ((columns * height, chans), BF16), ((2, tail1, chans), BF16), *seam_scratch, dma((6,)), dma((4 + members,))],
        fields, *seams,
    )
    recv, near = pack(own, near_tail, far_tail, near)
    far = to_far(far)
    pre_shape = (cycles, 2, height, chans)
    skip, pooled, near, far, pre_col = call(
        functools.partial(encode, tiles), "encode",
        [(tall, BF16), (pooled_shape, BF16), (wide, BF16), (wide, BF16), (pre_shape, F32)],
        [hbm] * 5, [hbm] * 5,
        [(tall, BF16), (row_shape, BF16), (row_shape, BF16), (wshape, BF16), (vector, F32), ((height, cols, 3 * chans), BF16), (tall, BF16),
         (pooled_shape, BF16), ((2,) + wide, BF16), (pre_shape, F32), ((cols, 128), F32),
         dma((6 + cycles,)), dma((cycles, height // 4 + 4))],
        fields, near, far, encoder_weight, eb,
        cost_estimate=far_cost,
    )
    pool_edges = (2, cycles, low, 16, chans)
    skip, pooled, near, far, own, near_tail, far_tail, table = call(
        functools.partial(mend, spec, coarse_at, fine_at), "mend",
        [(tall, BF16), (pooled_shape, BF16), (wide, BF16), (wide, BF16), ((members, payload, chans), BF16)]
        + [((tail2, chans), BF16)] * 2 + [((members, 128), jnp.int32)],
        [hbm] * 9, [hbm] * 8,
        [((members * spec.payload, chans), BF16), ((2, 3) + square, BF16), (pre_shape, F32), (edge_shape, BF16), (pool_edges, BF16), ((own2, chans), F32),
         ((2, tail2, chans), F32), ((own2, chans), BF16), ((2, tail2, chans), BF16), ((members, 128), jnp.int32),
         *seam_scratch, dma((10,)), dma((19 + members,))],
        recv.reshape(-1, chans), encoder_weight, skip, pooled, near, far, pre_col, *seams,
        input_output_aliases={2: 0, 3: 1, 4: 2, 5: 3},
    )
    recv2, near2 = pack(own, near_tail, far_tail, near)
    far2 = to_far(far)
    edges = (cycles, 2, height, 16, chans)
    coarse_edges = (cycles, 2, 8, chans)
    out, edge, coarse = call(
        functools.partial(decode, tiles), "decode",
        [(tall, BF16), (edges, F32), (coarse_edges, F32)],
        [hbm] * 10, [hbm, hbm, hbm],
        [(tall, BF16), (pooled_shape, BF16), (wide, BF16), (wide, BF16), (wshape, BF16), (vector, F32),
         ((2, 2) + square, BF16), (vector, F32), ((3, 6) + square, BF16), (vector, F32), (tall, BF16), (edges, F32),
         (coarse_edges, F32)]
        + [((height, cols, 6 * chans), BF16)] * 2 + [((low + 2, half, 3 * chans), BF16)] * 2
        + [((height + 2, chans // 128, cols, 128), F32)] * 2
        + [dma((19 + cycles,)), dma((cycles + 1, height // 4 + 1))],
        skip, pooled, near2, far2, middle_weight, mb, upconv_weight, ub, decoder_weight, db,
        cost_estimate=far_cost,
    )
    (out,) = call(
        functools.partial(seal, coarse_at, fine_at), "seal",
        [(tall, BF16)],
        [hbm] * 12, [hbm],
        [((members * payload, chans), BF16), (coarse_edges, F32), (edges, F32), (wshape, BF16), (vector, F32), ((2, 2) + square, BF16), (vector, F32),
         (wshape, BF16), ((2, 3) + square, BF16), (edge_shape, BF16),
         pltpu.SMEM((members, 128), jnp.int32), *seam_scratch, dma((13,)), dma((2,))],
        table, *seams, recv2.reshape(-1, chans), coarse, edge, middle_weight, mb, upconv_weight, ub, decoder_weight, out,
        input_output_aliases={11: 0},
    )
    return out


def solution(mesh):
    return jax.shard_map(
        functools.partial(on_device, mesh.shape["tile"]),
        mesh=mesh,
        in_specs=(P("grp", "tile", None, None), P(None, "tile", None), P(None, "tile", None)) + (P(),) * 8,
        out_specs=P("grp", "tile", None, None),
        check_vma=False,
    )
```

```python
import functools

import jax
import jax.numpy as jnp
from jax import lax
from jax.experimental import pallas as pl
from jax.experimental.pallas import tpu as pltpu
from jax.sharding import PartitionSpec as P

F32 = jnp.float32
BF16 = jnp.bfloat16
FACES = 4
MIB = 1 << 20


def dot(a, b):
    return jnp.dot(a, b, preferred_element_type=F32)


def gelu(x):
    return 0.5 * x * (1.0 + jnp.tanh(0.7978845608 * (x + 0.044715 * x * x * x)))


def rows_iota(n):
    return lax.broadcasted_iota(jnp.int32, (n, 1), 0)


class Layout:
    def __init__(self, tiles, height, depth, columns, own, near, tail):
        self.tiles = tiles
        self.strips = tiles // FACES
        self.joint = self.strips == 4
        self.height = height
        self.depth = depth
        self.columns = columns
        self.own = own
        self.near = near
        self.far = near + tail
        self.payload = 0

    def source(self, strip, flip, face, column, row):
        height, last = self.height, self.strips - 1
        strip = jnp.where(flip == 1, last - strip, strip)
        row = jnp.where(flip == 1, height - 1 - row, row)
        upper = jnp.where(strip >= self.strips // 2, 1, 0)
        odd = lax.rem(strip, 2)
        above = row < 0
        below = row >= height
        away = jnp.where(above, -row, row - (height - 1)) - 1
        near = (above & (odd == 1)) | (below & (odd == 0))
        missing = (above & (strip == 0)) | (below & (strip == last))
        member = (face * 2 + upper) * self.payload
        inside = member + self.own + column * height + row
        beside = member + self.near + column * self.depth + away
        if self.joint:
            across = (face * 2 + 1 - upper) * self.payload + self.own + column * height
            far = across + jnp.where(above, height - 1 - away, away)
        else:
            far = member + self.far + column * self.depth + away
        place = jnp.where(above | below, jnp.where(near, beside, far), inside)
        return jnp.where(missing, -1, place)


def strip_of(tiles):
    strips = tiles // FACES
    return lax.rem(lax.axis_index("tile") + strips // 2, strips)


def seam_of(tile_ref, code_ref, tiles, cycle, side):
    strips = tiles // FACES
    partner = tile_ref[0, side, cycle]
    code = code_ref[0, side, cycle]
    other = lax.div(partner, tiles)
    place = partner - other * tiles + strips // 2
    face = lax.rem(lax.div(place, strips), FACES)
    return other, face, lax.rem(code, 2), lax.div(code, 2)


def pick(targets, table):
    wanted = jnp.concatenate(targets, axis=0)
    shape = (wanted.shape[0], table.shape[0])
    lanes = lax.broadcasted_iota(jnp.int32, shape, 1)
    chooser = jnp.where(lanes == wanted, 1.0, 0.0).astype(BF16)
    return dot(chooser, table).astype(BF16)


def shifted_sum(taps, cols):
    left, middle, right = taps
    n = middle.shape[0]
    place = lax.broadcasted_iota(jnp.int32, middle.shape, 0) & (cols - 1)
    left = jnp.where(place == 0, 0.0, pltpu.roll(left, 1, 0))
    right = jnp.where(place == cols - 1, 0.0, pltpu.roll(right, n - 1, 0))
    return middle + left + right


def stack_taps(stacked, row_of, rows):
    depth = stacked.shape[-1] // 3
    for row in range(-1, rows + 1):
        value = row_of(row)
        for tap in range(3):
            at = row + 1 - tap
            if 0 <= at < rows:
                stacked[at, :, tap * depth : (tap + 1) * depth] = value


def column_taps(lhs, weight_ref):
    depth = weight_ref.shape[2]
    return [
        dot(lhs, weight_ref[:, tap].reshape(3 * depth, weight_ref.shape[3]))
        for tap in range(3)
    ]


def halo_rows(rows_ref, top, bottom):
    def row_of(row):
        if row < 0:
            return top
        if row >= rows_ref.shape[0]:
            return bottom
        return rows_ref[row]

    return row_of


def top_and_bottom(near, far, odd, ends):
    far = jnp.where(ends, jnp.zeros_like(far), far)
    return jnp.where(odd == 1, near, far), jnp.where(odd == 1, far, near)


def column_sum(parts, cycle, height):
    at = cycle * 16
    return sum(parts[tap][at + tap : at + tap + height] for tap in range(3))


def lift(layout, x_hbm, tile_hbm, code_hbm, own_hbm, near_tail_hbm, far_tail_hbm, near_hbm, far_hbm,
         edges, rows, own, tails, own16, tails16, tile_ref, code_ref, in_sems, out_sems):
    height = layout.height
    cycles, cols = x_hbm.shape[0], x_hbm.shape[2]
    upper = lax.rem(strip_of(layout.tiles), 2) * (height - 1)
    nearest = (height - 1 - upper, upper)
    pairs = [(x_hbm.at[:, :, pl.ds(first, 16)], edges.at[side]) for side, first in enumerate((0, cols - 16))]
    pairs += [(x_hbm.at[:, nearest[k]], rows.at[k]) for k in range(2)]
    arriving = fetch(pairs + [(tile_hbm, tile_ref), (code_hbm, code_ref)], in_sems)
    tails[...] = jnp.zeros_like(tails)
    for side in range(2):
        arriving[side].wait()
        at = 15 * side
        for cycle in range(cycles):
            column = cycle * 2 + side
            for row in range(height):
                value = edges[side, cycle, row].astype(F32)[at : at + 1]
                own[column * height + row : column * height + row + 1] = value
            for k in range(2):
                value = edges[side, cycle, nearest[k]].astype(F32)[at : at + 1]
                tails[k, column : column + 1] = value
    for copy in arriving[4:]:
        copy.wait()
    lanes = lax.broadcasted_iota(jnp.int32, (1, own.shape[1]), 1)
    noted = jnp.zeros((1, own.shape[1]), F32)
    for cycle in range(cycles):
        for side in range(2):
            other, face, side_bit, flip = seam_of(tile_ref, code_ref, layout.tiles, cycle, side)
            number = (other * FACES + face) * 4 + flip * 2 + side_bit
            noted = jnp.where(lanes == cycle * 2 + side, number.astype(F32), noted)
    for k in range(2):
        tails[k, layout.columns : layout.columns + 1] = noted
    own16[...] = own[...].astype(BF16)
    tails16[...] = tails[...].astype(BF16)
    pairs = [(tails16.at[0], near_tail_hbm), (tails16.at[1], far_tail_hbm)]
    pairs += [(own16, own_hbm.at[k, pl.ds(0, own16.shape[0])]) for k in range(2 * FACES)]
    leaving = fetch(pairs, out_sems.at[pl.ds(0, len(pairs))])
    for copy in arriving[2:4]:
        copy.wait()
    leaving += fetch([(rows.at[0], near_hbm), (rows.at[1], far_hbm)], out_sems.at[pl.ds(len(pairs), 2)])
    for copy in leaving:
        copy.wait()


def fetch(pairs, sems):
    copies = [pltpu.make_async_copy(src, dst, sems.at[k]) for k, (src, dst) in enumerate(pairs)]
    for copy in copies:
        copy.start()
    return copies


def encode(tiles, x_hbm, near_in, far_in, w_hbm, b_hbm, skip_hbm, pooled_hbm, near_hbm, far_hbm, pre_hbm,
           x_ref, near_ref, far_ref, w_ref, b_ref, stacked, skip_ref, pooled_ref, rows_ref, pre_ref, paired, in_sems, out_sems):
    cycles, height, cols, chans = x_ref.shape
    half = cols // 2
    pairs = [(x_hbm.at[0], x_ref.at[0]), (near_in, near_ref), (far_in, far_ref), (b_hbm, b_ref)]
    pairs += [(w_hbm.at[:, tap], w_ref.at[tap]) for tap in range(3)]
    arriving = fetch(pairs, in_sems.at[pl.ds(0, 7)])
    strip = strip_of(tiles)
    odd = lax.rem(strip, 2)
    ends = (strip == 0) | (strip == tiles // FACES - 1)
    for copy in arriving[:4]:
        copy.wait()
    leaving = []
    for cycle in range(cycles):
        if cycle > 0:
            arriving[6 + cycle].wait()
        top, bottom = top_and_bottom(near_ref[cycle], far_ref[cycle], odd, ends)
        stack_taps(stacked, halo_rows(x_ref.at[cycle], top, bottom), height)
        for row in range(height):
            taps = []
            for tap in range(3):
                if cycle == 0 and row == 0:
                    arriving[4 + tap].wait()
                taps.append(dot(stacked[row], w_ref[tap].reshape(3 * chans, chans)))
            if cycle == 0 and row == 0:
                pairs = [(x_hbm.at[k], x_ref.at[k]) for k in range(1, cycles)]
                arriving += fetch(pairs, in_sems.at[pl.ds(7, cycles - 1)])
            total = shifted_sum(taps, cols) + b_ref[...]
            value = gelu(total).astype(BF16)
            skip_ref[cycle, row] = value
            pre_ref[cycle, 0, row : row + 1] = total[:1]
            pre_ref[cycle, 1, row : row + 1] = total[cols - 1 :]
            if row % 2 == 0:
                before = value.astype(F32)
            else:
                pair = 0.25 * (before + value.astype(F32))
                for lane in range(0, chans, 128):
                    paired[...] = pair[:, lane : lane + 128]
                    mean = paired[pl.ds(0, half, 2), :] + paired[pl.ds(1, half, 2), :]
                    pooled_ref[cycle, row // 2, :, lane : lane + 128] = mean.astype(BF16)
            if row % 4 == 3:
                rows = (cycle, pl.ds(row - 3, 4))
                leaving += fetch([(skip_ref.at[rows], skip_hbm.at[rows])], out_sems.at[cycle, pl.ds(row // 4, 1)])
        low = height // 2 - 1
        for k, at_top in ((0, odd == 1), (1, odd == 0)):
            rows_ref[k, cycle, :cols] = skip_ref[cycle, jnp.where(at_top, 0, height - 1)]
            rows_ref[k, cycle, cols : cols + half] = pooled_ref[cycle, jnp.where(at_top, 0, low)]
            rows_ref[k, cycle, cols + half :] = pooled_ref[cycle, jnp.where(at_top, 1, low - 1)]
        pairs = [(rows_ref.at[0, cycle], near_hbm.at[cycle]), (rows_ref.at[1, cycle], far_hbm.at[cycle])]
        pairs += [(pooled_ref.at[cycle], pooled_hbm.at[cycle]), (pre_ref.at[cycle], pre_hbm.at[cycle])]
        leaving += fetch(pairs, out_sems.at[cycle, pl.ds(height // 4, 4)])
    for copy in leaving:
        copy.wait()


def mend(layout, coarse, fine, recv_hbm, w_hbm, skip_in, pooled_in, near_in, far_in, pre_hbm, tile_hbm, code_hbm,
         skip_hbm, pooled_hbm, near_hbm, far_hbm, own_hbm, near_tail_hbm, far_tail_hbm, table_hbm,
         recv_ref, w_ref, pre_ref, edges, pools, own, tails, own16, tails16, table_ref, tile_ref, code_ref, in_sems, out_sems):
    tiles, height, low = layout.tiles, layout.height, coarse.height
    cycles, cols, chans = skip_in.shape[0], skip_in.shape[2], skip_in.shape[3]
    half = cols // 2
    pairs = [(tile_hbm, tile_ref), (code_hbm, code_ref), (recv_hbm, recv_ref)]
    pairs += [(w_hbm.at[:, 2 * side], w_ref.at[side]) for side in range(2)] + [(pre_hbm, pre_ref)]
    for side in range(2):
        pairs.append((skip_in.at[:, :, pl.ds((cols - 16) * side, 16)], edges.at[side]))
        pairs.append((pooled_in.at[:, :, pl.ds((half - 16) * side, 16)], pools.at[side]))
    arriving = fetch(pairs, in_sems)
    strip = strip_of(tiles)
    odd = lax.rem(strip, 2)
    row_iota = rows_iota(16) - 1
    targets = []
    for copy in arriving[:2]:
        copy.wait()
    for side in range(2):
        for cycle in range(cycles):
            other, face, side_bit, flip = seam_of(tile_ref, code_ref, tiles, cycle, side)
            place = layout.source(strip, flip, face, other * 2 + side_bit, row_iota)
            targets.append(jnp.where(row_iota <= height, place, -1))
    arriving[2].wait()
    pads = pick(targets, recv_ref[...])
    noted = layout.near + layout.columns
    for member in range(2 * FACES):
        at = member * layout.payload + noted // 16 * 16
        block = recv_ref[at : at + 16, :128].astype(F32)
        table_ref[member : member + 1] = block[noted % 16 : noted % 16 + 1].astype(jnp.int32)
    part = pads.shape[0] // 2
    for copy in arriving[3:6]:
        copy.wait()
    seams = [
        [dot(pads[side * part : (side + 1) * part], w_ref[side, tap]) for tap in range(3)] for side in range(2)
    ]
    iota16 = lax.broadcasted_iota(jnp.int32, (16, chans), 0)
    tails[...] = jnp.zeros_like(tails)
    for copy in arriving[6:]:
        copy.wait()
    at_top = (odd == 1, odd == 0)
    skip_at = [jnp.where(t, 0, height - 1) for t in at_top]
    pool_at = [(jnp.where(t, 0, low - 1), jnp.where(t, 1, low - 2)) for t in at_top]
    for cycle in range(cycles):
        for side in range(2):
            column = cycle * 2 + side
            at, inward = (0, 1) if side == 0 else (15, 14)
            total = gelu(pre_ref[cycle, side] + column_sum(seams[side], cycle, height))
            start = fine.own + column * height
            own[start : start + height] = total
            for row in range(height):
                block = edges[side, cycle, row].astype(F32)
                block = jnp.where(iota16 == at, total[row : row + 1], block).astype(BF16)
                edges[side, cycle, row] = block
                if row % 2 == 0:
                    before = block.astype(F32)
                else:
                    pair = before + block.astype(F32)
                    mean = 0.25 * (pair[at : at + 1] + pair[inward : inward + 1])
                    block = pools[side, cycle, row // 2].astype(F32)
                    block = jnp.where(iota16 == at, mean, block)
                    pools[side, cycle, row // 2] = block.astype(BF16)
                    for depth, place in enumerate((at, inward)):
                        start = coarse.own + (column * 2 + depth) * low + row // 2
                        own[start : start + 1] = block[place : place + 1]
            for k in range(2):
                start = fine.near - coarse.near + column
                value = edges[side, cycle, skip_at[k]].astype(F32)
                tails[k, start : start + 1] = value[at : at + 1]
                for away in range(2):
                    value = pools[side, cycle, pool_at[k][away]].astype(F32)
                    for depth, place in enumerate((at, inward)):
                        start = (column * 2 + depth) * 2 + away
                        tails[k, start : start + 1] = value[place : place + 1]
    own16[...] = own[...].astype(BF16)
    tails16[...] = tails[...].astype(BF16)
    pairs = [(tails16.at[0], near_tail_hbm), (tails16.at[1], far_tail_hbm), (table_ref, table_hbm)]
    pairs += [(own16, own_hbm.at[k, pl.ds(0, own16.shape[0])]) for k in range(2 * FACES)]
    for side in range(2):
        pairs.append((edges.at[side], skip_hbm.at[:, :, pl.ds((cols - 16) * side, 16)]))
        pairs.append((pools.at[side], pooled_hbm.at[:, :, pl.ds((half - 16) * side, 16)]))
        for k, ref in enumerate((near_hbm, far_hbm)):
            pairs.append((edges.at[side, :, skip_at[k]], ref.at[:, pl.ds((cols - 16) * side, 16)]))
            for away in range(2):
                first = cols + away * half + (half - 16) * side
                pairs.append((pools.at[side, :, pool_at[k][away]], ref.at[:, pl.ds(first, 16)]))
    leaving = fetch(pairs, out_sems)
    for copy in leaving:
        copy.wait()


def decode(tiles, skip_hbm, pooled_hbm, near_hbm, far_hbm, wm_hbm, bm_hbm, u_hbm, bu_hbm, wd_hbm, bd_hbm,
           out_hbm, edge_hbm, coarse_hbm, skip_ref, pooled_ref, near_ref, far_ref, wm_ref, bm_ref, u_ref, bu_ref,
           wd_ref, bd_ref, out_ref, edge_ref, coarse_ref, stacked_a, stacked_b, upper_a, upper_b, joined_a, joined_b,
           in_sems, out_sems):
    strips = tiles // FACES
    cycles, height, cols, chans = skip_ref.shape
    low, half = height // 2, cols // 2
    halos = ((near_hbm, near_ref), (far_hbm, far_ref), (pooled_hbm, pooled_ref))
    pairs = [(src.at[0], dst.at[0]) for src, dst in halos] + [(bm_hbm, bm_ref)]
    pairs += [(wm_hbm.at[:, tap], wm_ref.at[tap]) for tap in range(3)]
    pairs += [(bu_hbm, bu_ref), (u_hbm, u_ref), (skip_hbm.at[0], skip_ref.at[0]), (bd_hbm, bd_ref)]
    for tap in range(3):
        for part in range(2):
            source = wd_hbm.at[:, tap, pl.ds(part * chans, chans)]
            pairs.append((source, wd_ref.at[tap, pl.ds(3 * part, 3)]))
    pairs += [(skip_hbm.at[cycle], skip_ref.at[cycle]) for cycle in range(1, cycles)]
    rest = pl.ds(1, cycles - 1)
    pairs += [(src.at[rest], dst.at[rest]) for src, dst in halos]
    arriving = fetch(pairs, in_sems)
    strip = strip_of(tiles)
    odd = lax.rem(strip, 2)
    first_strip, last_strip = strip == 0, strip == strips - 1
    ends = first_strip | last_strip
    place = lax.broadcasted_iota(jnp.int32, (cols, chans), 0)
    inner = (place > 1) & (place < cols - 2)
    coarse_ref[...] = jnp.zeros_like(coarse_ref)
    leaving = []
    for copy in arriving[:4]:
        copy.wait()

    def prepare(cycle):
        if cycle == 1:
            for copy in arriving[16 + cycles :]:
                copy.wait()
        top, bottom = top_and_bottom(near_ref[cycle], far_ref[cycle], odd, ends)
        stacked, upper, joined = (stacked_a, upper_a, joined_a) if cycle % 2 == 0 else (stacked_b, upper_b, joined_b)

        def pooled_row(row):
            if row < -1:
                return top[cols + half :]
            if row < 0:
                return top[cols : cols + half]
            if row < low:
                return pooled_ref[cycle, row]
            if row == low:
                return bottom[cols : cols + half]
            return bottom[cols + half :]

        stack_taps(upper, lambda row: pooled_row(row - 1), low + 2)
        yield
        lhs = upper[...].reshape((low + 2) * half, 3 * chans)
        taps = []
        for tap in range(3):
            if cycle == 0:
                arriving[4 + tap].wait()
            taps.append(dot(lhs, wm_ref[tap].reshape(3 * chans, chans)))
        total = shifted_sum(taps, half) + bm_ref[...]
        yield
        coarse = []
        for row in range(low + 2):
            at = row * half
            coarse_ref[cycle, 0, row + 1 : row + 2] = total[at : at + 1]
            coarse_ref[cycle, 1, row + 1 : row + 2] = total[at + half - 1 : at + half]
            coarse.append(gelu(total[at : at + half]).astype(BF16))
        if cycle == 0:
            arriving[7].wait()
            arriving[8].wait()
        yield
        for a in range(2):
            part = jnp.concatenate(coarse[1:] if a == 0 else coarse[:-1], axis=0)
            for b in range(2):
                value = dot(part, u_ref[a, b]) + bu_ref[...]
                for k in range(low + 1):
                    at = 2 * k + 1 - a
                    for lane in range(0, chans, 128):
                        part_of = value[k * half : (k + 1) * half, lane : lane + 128]
                        joined[at, lane // 128, pl.ds(b, half, 2), :] = part_of
                yield
        arriving[9 if cycle == 0 else 16 + cycle].wait()
        skip_row = halo_rows(skip_ref.at[cycle], top[:cols], bottom[:cols])
        stack_taps(stacked.at[:, :, pl.ds(3 * chans, 3 * chans)], skip_row, height)
        for row in range(-1, height + 1):
            value = jnp.concatenate([joined[row + 1, k] for k in range(chans // 128)], axis=1)
            keep = inner
            if row < 0:
                keep = keep & jnp.logical_not(first_strip)
            if row >= height:
                keep = keep & jnp.logical_not(last_strip)
            value = jnp.where(keep, value, 0.0).astype(BF16)
            for tap in range(3):
                at = row + 1 - tap
                if 0 <= at < height:
                    stacked[at, :, tap * chans : (tap + 1) * chans] = value
            if row % 5 == 3:
                yield

    def convolve(cycle):
        stacked = stacked_a if cycle % 2 == 0 else stacked_b
        for row in range(height):
            taps = []
            for tap in range(3):
                if cycle == 0 and row == 0:
                    for k in range(10 if tap == 0 else 11 + 2 * tap, 13 + 2 * tap):
                        arriving[k].wait()
                taps.append(dot(stacked[row], wd_ref[tap].reshape(6 * chans, chans)))
            total = shifted_sum(taps, cols) + bd_ref[...]
            out_ref[cycle, row] = total.astype(BF16)
            edge_ref[cycle, 0, row] = total[:16]
            edge_ref[cycle, 1, row] = total[cols - 16 :]
            copies = []
            if row % 4 == 3:
                rows = (cycle, pl.ds(row - 3, 4))
                copies = [(out_ref.at[rows], out_hbm.at[rows])]
            if row == height - 1:
                copies.append((edge_ref.at[cycle], edge_hbm.at[cycle]))
            yield fetch(copies, out_sems.at[cycle, pl.ds(row // 4, len(copies))]) if copies else []

    for _ in prepare(0):
        pass
    for cycle in range(cycles):
        ahead = prepare(cycle + 1) if cycle + 1 < cycles else iter(())
        for copies in convolve(cycle):
            leaving += copies
            next(ahead, None)
            next(ahead, None)
        for _ in ahead:
            pass
    leaving += fetch([(coarse_ref, coarse_hbm)], out_sems.at[cycles, pl.ds(0, 1)])
    for copy in leaving:
        copy.wait()


def seal(coarse_at, fine_at, tab_hbm, tile_hbm, code_hbm, recv_hbm, coarse_hbm, edge_hbm, wm_hbm, bm_hbm, u_hbm,
         bu_hbm, wd_hbm, out_in, out_hbm, recv_ref, coarse_ref, edge_ref, wm_ref, bm_ref, u_ref, bu_ref, wu_ref, ws_ref, out_ref,
         tab_ref, tile_ref, code_ref, in_sems, out_sems):
    tiles, strips, height = coarse_at.tiles, coarse_at.strips, fine_at.height
    cycles, _, _, _, chans = edge_ref.shape
    cols = out_hbm.shape[2]
    low = height // 2
    pairs = [(recv_hbm, recv_ref), (bm_hbm, bm_ref), (bu_hbm, bu_ref), (coarse_hbm, coarse_ref), (wm_hbm, wm_ref), (u_hbm, u_ref)]
    pairs += [(wd_hbm.at[:, :, pl.ds(0, chans)], wu_ref)]
    pairs += [(wd_hbm.at[:, 2 * side, pl.ds(chans, chans)], ws_ref.at[side]) for side in range(2)]
    pairs += [(edge_hbm, edge_ref)]
    seams = fetch([(tab_hbm, tab_ref), (tile_hbm, tile_ref), (code_hbm, code_ref)], in_sems.at[pl.ds(10, 3)])
    arriving = fetch(pairs, in_sems.at[pl.ds(0, 10)])
    for copy in seams:
        copy.wait()
    strip = strip_of(tiles)
    rows8 = rows_iota(8) - 2
    rows16 = rows_iota(16) - 1
    aligned, taps, skips, sides, flips, strips_at = [], [[], [], []], [], [], [], []
    for side in range(2):
        for cycle in range(cycles):
            other, face, side_bit, flip = seam_of(tile_ref, code_ref, tiles, cycle, side)
            column = other * 2 + side_bit
            aligned.append(coarse_at.source(strip, flip, face, column * 2, rows8))
            place = fine_at.source(strip, flip, face, column, rows16)
            skips.append(jnp.where(rows16 <= height, place, -1))
            there = jnp.where(flip == 1, strips - 1 - strip, strip)
            number = tab_ref[face * 2, column]
            beyond = lax.div(number, 4)
            code = lax.rem(number, 4)
            other2, face2 = lax.div(beyond, FACES), lax.rem(beyond, FACES)
            column2 = other2 * 2 + lax.rem(code, 2)
            pad = coarse_at.source(there, lax.div(code, 2), face2, column2 * 2, rows8)
            edge = coarse_at.source(there, 0, face, column * 2, rows8)
            inner = coarse_at.source(there, 0, face, column * 2 + 1, rows8)
            taps[0].append(jnp.where(side_bit == 0, pad, inner))
            taps[1].append(edge)
            taps[2].append(jnp.where(side_bit == 0, inner, pad))
            sides.append(side_bit)
            flips.append(flip)
            strips_at.append(there)
    arriving[0].wait()
    got = pick(aligned + taps[0] + taps[1] + taps[2] + skips, recv_ref[...])
    n = 8 * 2 * cycles
    at8 = lax.broadcasted_iota(jnp.int32, (8, chans), 0) - 2

    def on_face(s):
        return jnp.where(((at8 < 0) & (s == 0)) | ((at8 >= low) & (s == strips - 1)), 0.0, 1.0)

    for copy in arriving[1:5]:
        copy.wait()
    own = got[:n]
    there = got[n : 4 * n]
    rows = []
    for row in range(3):
        here = [dot(own[side * n // 2 : (side + 1) * n // 2], wm_ref[row, 2 * side]) for side in range(2)]
        away = sum(dot(there[tap * n : (tap + 1) * n], wm_ref[row, tap]) for tap in range(3))
        rows.append(jnp.concatenate(here + [away], axis=0))
    total = pltpu.roll(rows[0], 1, 0) + rows[1] + pltpu.roll(rows[2], 2 * n - 1, 0)
    mine = [
        total[(side * cycles + cycle) * 8 : (side * cycles + cycle + 1) * 8] + coarse_ref[cycle, side]
        for side in range(2)
        for cycle in range(cycles)
    ]
    total = jnp.concatenate(mine + [total[n:] + bm_ref[...]], axis=0)
    keep = jnp.concatenate([on_face(s) for s in [strip] * (2 * cycles) + strips_at], axis=0)
    column = (gelu(total) * keep).astype(BF16)
    arriving[5].wait()
    phases = [
        [((dot(column, u_ref[a, b]) + bu_ref[...]) * keep).astype(BF16) for b in range(2)] for a in range(2)
    ]
    right = jnp.concatenate([jnp.where(at8 > -99, b, 0) for b in sides], axis=0) == 1
    place = lax.shift_right_arithmetic(rows16 - (rows16 & 1), 1) + 2
    fine_own = [jnp.where(rows16 <= height, (rows16 & 1) * n + k * 8 + place, -1) for k in range(2 * cycles)]
    fine_there = []
    for k in range(2 * cycles):
        fine = jnp.where(flips[k] == 1, height - 1 - rows16, rows16)
        a = fine & 1
        place = a * n + k * 8 + lax.shift_right_arithmetic(fine - a, 1) + 2
        fine_there.append(jnp.where(rows16 <= height, place, -1))
    beyond = [jnp.where(right, phases[a][1][n:], phases[a][0][n:]) for a in range(2)]
    outer = pick(fine_there, jnp.concatenate(beyond, axis=0))
    inside = [pick(fine_own, jnp.concatenate([phases[a][b][:n] for a in range(2)], axis=0)) for b in range(2)]
    skip_pad = got[4 * n :]
    m = 16 * cycles
    lines = [[outer[:m], inside[0][:m], inside[1][:m]], [outer[m:], inside[1][m:], inside[0][m:]]]
    for copy in arriving[6:9]:
        copy.wait()
    sums = [[[], [], []], [[], [], []]]
    for row in range(3):
        found = [[0.0, 0.0, 0.0], [0.0, 0.0, 0.0]]
        for tap in range(3):
            uses = []
            for side in range(2):
                offset = tap if side == 0 else 2 - tap
                uses += [(side, line, line - offset) for line in range(3) if line >= offset]
            value = dot(jnp.concatenate([lines[side][line] for side, line, _ in uses], axis=0), wu_ref[row, tap])
            for k, (side, _, into) in enumerate(uses):
                found[side][into] = found[side][into] + value[k * m : (k + 1) * m]
        for side in range(2):
            found[side][0] = found[side][0] + dot(skip_pad[side * m : (side + 1) * m], ws_ref[side, row])
            for into in range(3):
                sums[side][into].append(found[side][into])
    iota16 = lax.broadcasted_iota(jnp.int32, (16, chans), 0)
    arriving[9].wait()
    for side in range(2):
        for cycle in range(cycles):
            extra = [column_sum(sums[side][into], cycle, height) for into in range(3)]
            for row in range(height):
                value = edge_ref[cycle, side, row]
                for into in range(3):
                    at = into if side == 0 else 15 - into
                    value = value + jnp.where(iota16 == at, extra[into][row : row + 1], 0.0)
                out_ref[side, cycle, row] = value.astype(BF16)
    leaving = fetch(
        [(out_ref.at[side], out_hbm.at[:, :, pl.ds((cols - 16) * side, 16)]) for side in range(2)], out_sems
    )
    for copy in leaving:
        copy.wait()


def on_device(tiles, fields, seam_tile, seam_code, encoder_weight, encoder_bias, middle_weight,
              middle_bias, upconv_weight, upconv_bias, decoder_weight, decoder_offset_bias):
    cycles, height, cols, chans = fields.shape
    low, half = height // 2, cols // 2
    strips = tiles // FACES
    joint = strips == 4

    def strip(t):
        return (t + strips // 2) % strips

    near_pairs, far_pairs = [], []
    for t in range(tiles):
        pairs = near_pairs if strip(t) % 2 == 0 else far_pairs
        after = (t + 1) % tiles
        pairs += [(t, after), (after, t)]

    def tile_at(face, s):
        return (face * strips + s - strips // 2) % tiles

    groups = [
        [tile_at(face, s) for face in range(FACES) for s in (k, strips - 1 - k)]
        for k in range(strips // 2)
    ]
    members = 2 * FACES

    def share(x):
        return lax.all_to_all(x, "tile", 0, 0, tiled=True, axis_index_groups=groups)

    columns = 2 * cycles
    tail1 = (columns + 1 + 15) // 16 * 16
    spec = Layout(tiles, height, 1, columns, 0, columns * height, tail1)
    own2 = 2 * columns * low + columns * height
    tail2 = (4 * columns + columns + 15) // 16 * 16
    coarse_at = Layout(tiles, low, 2, 2 * columns, 0, own2, tail2)
    fine_at = Layout(tiles, height, 1, columns, 2 * columns * low, own2 + 4 * columns, tail2)
    halos = 1 if joint else 2
    spec.payload = columns * height + halos * tail1
    payload = own2 + halos * tail2
    coarse_at.payload = fine_at.payload = payload

    def to_near(x):
        return lax.ppermute(x, "tile", near_pairs)

    def to_far(x):
        return lax.ppermute(x, "tile", far_pairs)

    def pack(own, near_tail, far_tail, near):
        tails = [to_near(near_tail)] + ([] if joint else [to_far(far_tail)])
        rows = own.shape[1] - sum(tail.shape[0] for tail in tails)
        for tail in tails:
            tail = jnp.broadcast_to(tail[None], (members,) + tail.shape)
            own = lax.dynamic_update_slice(own, tail, (0, rows, 0))
            rows += tail.shape[1]
        return share(own), to_near(near)

    seams = (jnp.transpose(seam_tile, (1, 2, 0)), jnp.transpose(seam_code, (1, 2, 0)))
    eb, mb, ub, db = (b.reshape(1, chans) for b in (encoder_bias, middle_bias, upconv_bias, decoder_offset_bias))

    hbm = pl.BlockSpec(memory_space=pltpu.HBM)
    vmem = pl.BlockSpec(memory_space=pltpu.VMEM)
    seam_scratch = [pltpu.SMEM((1, 2, cycles), jnp.int32)] * 2
    dma = pltpu.SemaphoreType.DMA
    tall = (cycles, height, cols, chans)
    row_shape = (cycles, cols, chans)
    wide = (cycles, 2 * cols, chans)
    square = (chans, chans)
    wshape = (3, 3) + square
    pooled_shape = (cycles, low, half, chans)
    edge_shape = (2, cycles, height, 16, chans)

    def call(body, name, outs, in_specs, out_specs, scratch, *args, **options):
        return pl.pallas_call(
            body,
            out_shape=[jax.ShapeDtypeStruct(shape, dtype) for shape, dtype in outs],
            in_specs=in_specs,
            out_specs=out_specs,
            scratch_shapes=[pltpu.VMEM(*x) if isinstance(x, tuple) else x for x in scratch],
            compiler_params=pltpu.CompilerParams(vmem_limit_bytes=56 * MIB),
            name=name,
            **options,
        )(*args)

    far_cost = pl.CostEstimate(flops=10**12, bytes_accessed=10**9, transcendentals=0)
    vector = (1, chans)
    own, near_tail, far_tail, near, far = call(
        functools.partial(lift, spec), "lift",
        [((members, spec.payload, chans), BF16)] + [((tail1, chans), BF16)] * 2 + [(row_shape, BF16)] * 2,
        [hbm] * 3, [hbm] * 5,
        [(edge_shape, BF16), ((2,) + row_shape, BF16), ((columns * height, chans), F32), ((2, tail1, chans), F32),
         ((columns * height, chans), BF16), ((2, tail1, chans), BF16), *seam_scratch, dma((6,)), dma((4 + members,))],
        fields, *seams,
    )
    recv, near = pack(own, near_tail, far_tail, near)
    far = to_far(far)
    pre_shape = (cycles, 2, height, chans)
    skip, pooled, near, far, pre_col = call(
        functools.partial(encode, tiles), "encode",
        [(tall, BF16), (pooled_shape, BF16), (wide, BF16), (wide, BF16), (pre_shape, F32)],
        [hbm] * 5, [hbm] * 5,
        [(tall, BF16), (row_shape, BF16), (row_shape, BF16), (wshape, BF16), (vector, F32), ((height, cols, 3 * chans), BF16), (tall, BF16),
         (pooled_shape, BF16), ((2,) + wide, BF16), (pre_shape, F32), ((cols, 128), F32),
         dma((6 + cycles,)), dma((cycles, height // 4 + 4))],
        fields, near, far, encoder_weight, eb,
        cost_estimate=far_cost,
    )
    pool_edges = (2, cycles, low, 16, chans)
    skip, pooled, near, far, own, near_tail, far_tail, table = call(
        functools.partial(mend, spec, coarse_at, fine_at), "mend",
        [(tall, BF16), (pooled_shape, BF16), (wide, BF16), (wide, BF16), ((members, payload, chans), BF16)]
        + [((tail2, chans), BF16)] * 2 + [((members, 128), jnp.int32)],
        [hbm] * 9, [hbm] * 8,
        [((members * spec.payload, chans), BF16), ((2, 3) + square, BF16), (pre_shape, F32), (edge_shape, BF16), (pool_edges, BF16), ((own2, chans), F32),
         ((2, tail2, chans), F32), ((own2, chans), BF16), ((2, tail2, chans), BF16), ((members, 128), jnp.int32),
         *seam_scratch, dma((10,)), dma((19 + members,))],
        recv.reshape(-1, chans), encoder_weight, skip, pooled, near, far, pre_col, *seams,
        input_output_aliases={2: 0, 3: 1, 4: 2, 5: 3},
    )
    recv2, near2 = pack(own, near_tail, far_tail, near)
    far2 = to_far(far)
    edges = (cycles, 2, height, 16, chans)
    coarse_edges = (cycles, 2, 8, chans)
    out, edge, coarse = call(
        functools.partial(decode, tiles), "decode",
        [(tall, BF16), (edges, F32), (coarse_edges, F32)],
        [hbm] * 10, [hbm, hbm, hbm],
        [(tall, BF16), (pooled_shape, BF16), (wide, BF16), (wide, BF16), (wshape, BF16), (vector, F32),
         ((2, 2) + square, BF16), (vector, F32), ((3, 6) + square, BF16), (vector, F32), (tall, BF16), (edges, F32),
         (coarse_edges, F32)]
        + [((height, cols, 6 * chans), BF16)] * 2 + [((low + 2, half, 3 * chans), BF16)] * 2
        + [((height + 2, chans // 128, cols, 128), F32)] * 2
        + [dma((19 + cycles,)), dma((cycles + 1, height // 4 + 1))],
        skip, pooled, near2, far2, middle_weight, mb, upconv_weight, ub, decoder_weight, db,
        cost_estimate=far_cost,
    )
    (out,) = call(
        functools.partial(seal, coarse_at, fine_at), "seal",
        [(tall, BF16)],
        [hbm] * 12, [hbm],
        [((members * payload, chans), BF16), (coarse_edges, F32), (edges, F32), (wshape, BF16), (vector, F32), ((2, 2) + square, BF16), (vector, F32),
         (wshape, BF16), ((2, 3) + square, BF16), (edge_shape, BF16),
         pltpu.SMEM((members, 128), jnp.int32), *seam_scratch, dma((13,)), dma((2,))],
        table, *seams, recv2.reshape(-1, chans), coarse, edge, middle_weight, mb, upconv_weight, ub, decoder_weight, out,
        input_output_aliases={11: 0},
    )
    return out


def solution(mesh):
    return jax.shard_map(
        functools.partial(on_device, mesh.shape["tile"]),
        mesh=mesh,
        in_specs=(P("grp", "tile", None, None), P(None, "tile", None), P(None, "tile", None)) + (P(),) * 8,
        out_specs=P("grp", "tile", None, None),
        check_vma=False,
    )
```
